32 devices in a mesh: shard: 4 (over z), ctx: 4 (over y, core), tp: 2 (over x).
Axes of the slice: x: 2, y: 2, z: 4, core: 2. Of those that a mesh axis runs over, the one named last changes fastest.
Arguments:
- activations: bfloat16 [12, 1024, 2048], P('shard', 'ctx'), may hold values from -6 to 6
- segments: int32 [12, 1024], P('shard'), may hold values from 0 to 3, as said below
- query_weight: bfloat16 [2048, 2048], P('shard', 'tp'), may hold values from -0.125 to 0.125
- key_weight: bfloat16 [2048, 256], P('shard', 'tp'), may hold values from -0.125 to 0.125
- value_weight: bfloat16 [2048, 256], P('shard', 'tp'), may hold values from -0.125 to 0.125
- output_weight: bfloat16 [2048, 2048], P('tp', 'shard'), may hold values from -2 to 2
- gate_weight: bfloat16 [2048, 5632], P('shard', 'tp'), may hold values from -0.125 to 0.125
- up_weight: bfloat16 [2048, 5632], P('shard', 'tp'), may hold values from -0.125 to 0.125
- down_weight: bfloat16 [5632, 2048], P('tp', 'shard'), may hold values from -0.078125 to 0.078125
- attn_gain: bfloat16 [2048], P('shard'), may hold values from 0.099609375 to 1.8984375
- ffn_gain: bfloat16 [2048], P('shard'), may hold values from 0.099609375 to 1.8984375
- cotangent: bfloat16 [12, 1024, 2048], P('shard', 'ctx'), may hold values from -6 to 6
Outputs:
- block_out: bfloat16 [12, 1024, 2048], P('shard', 'ctx')
- input_grad: float32 [12, 1024, 2048], P('shard', 'ctx')
- query_grad: float32 [2048, 2048], P('shard', 'tp')
- key_grad: float32 [2048, 256], P('shard', 'tp')
- value_grad: float32 [2048, 256], P('shard', 'tp')
- output_grad: float32 [2048, 2048], P('tp', 'shard')
- gate_grad: float32 [2048, 5632], P('shard', 'tp')
- up_grad: float32 [2048, 5632], P('shard', 'tp')
- down_grad: float32 [5632, 2048], P('tp', 'shard')
- attn_gain_grad: float32 [2048], P('shard')
- ffn_gain_grad: float32 [2048], P('shard')
The draws below stay inside these ranges and needn't reach their ends.
Inputs may be any that keep to these rules, and one draw needn't show every extreme that they name: Along each sequence the numbers start at 0 and rise by one at each new document (the last segment may be padding). In each aligned group of 3 sequences exactly one is all 0; each other sequence has exactly 4 segments.
All inputs are finite; a program needn't handle non-finite values.
Results may differ from the reference program's by a relative error of at most 0.013.
Values may be sent and summed in bfloat16 or wider, within the bound.
No kernel may reach another device: no remote copies, remote signals or barrier semaphores. Data moves between devices by JAX's collectives and lax.ppermute only.
A program may use at most 384 MiB of HBM per device.

```python
from functools import partial
import jax
import jax.numpy as jnp
from jax import lax

D = 2048
FF = 5632
HEADS = 32
KV_HEADS = 4
HEAD = 64
SEQ_DEV = 3
LEN = 1024
DOCS = 4
SEQS = 12


def draw_segments(key, part):
    key = jax.random.fold_in(key, 7)
    pick_key, cut_key = jax.random.split(key)
    chosen = jax.random.randint(pick_key, (SEQS // SEQ_DEV,), 0, SEQ_DEV)
    seq_ids = jnp.arange(SEQS)
    single = seq_ids % SEQ_DEV == chosen[seq_ids // SEQ_DEV]
    cut_keys = jax.random.split(cut_key, SEQS)
    cuts = jax.vmap(lambda one_key: jax.random.permutation(one_key, LEN - 1)[:DOCS - 1] + 1)(cut_keys)
    places = jnp.arange(LEN)
    numbers = jnp.sum((places[None, :, None] >= cuts[:, None, :]).astype(jnp.int32), -1)
    return jnp.where(single[:, None], 0, numbers).astype(jnp.int32)


def shard_levels(key, extent, cuts, least, high):
    level, own = 1.0, jax.random.fold_in(key, 6)
    for axis_at, shards_of in cuts:
        heights = jnp.exp(jax.random.uniform(jax.random.fold_in(own, axis_at), (shards_of,), jnp.float32, least / len(cuts), high / len(cuts)))
        level = level * jnp.repeat(heights, extent[axis_at] // shards_of).reshape([-1 if axis == axis_at else 1 for axis in range(len(extent))])
    return level


def normal_values(key, extent, scale, most, pieces=(), kind=jnp.bfloat16):
    result = jax.random.normal(key, extent, jnp.float32) * scale
    if len(pieces) > 0:
        result = shard_levels(key, extent, pieces, -0.22, 0.18) * result
    return jnp.clip(result, min=-most, max=most).astype(kind)


def setup_inputs(seed: int = 0) -> dict:
    streams_of = jax.random.split(jax.random.key(seed), 13)
    return {
        "activations": normal_values(streams_of[0], (SEQS, LEN, D), 1.0, 6.0, ((0, 4), (1, 4))),
        "segments": draw_segments(jax.random.fold_in(streams_of[12], 71), 0),
        "query_weight": normal_values(streams_of[2], (D, HEADS * HEAD), D ** -0.5, 0.125, ((0, 4), (1, 2))),
        "key_weight": normal_values(streams_of[3], (D, KV_HEADS * HEAD), D ** -0.5, 0.125, ((0, 4), (1, 2))),
        "value_weight": normal_values(streams_of[4], (D, KV_HEADS * HEAD), D ** -0.5, 0.125, ((0, 4), (1, 2))),
        "output_weight": normal_values(streams_of[5], (HEADS * HEAD, D), (max(1, HEADS * HEAD // 256)) ** -0.5, 2.0, ((0, 2), (1, 4))),
        "gate_weight": normal_values(streams_of[6], (D, FF), D ** -0.5, 0.125, ((0, 4), (1, 2))),
        "up_weight": normal_values(streams_of[7], (D, FF), D ** -0.5, 0.125, ((0, 4), (1, 2))),
        "down_weight": normal_values(streams_of[8], (FF, D), FF ** -0.5, 0.078125, ((0, 2), (1, 4))),
        "attn_gain": jnp.clip(1.0 + 0.18 * jax.random.normal(streams_of[9], (D,), jnp.float32), 0.099609375, 1.8984375).astype(jnp.bfloat16),
        "ffn_gain": jnp.clip(1.0 + 0.18 * jax.random.normal(streams_of[10], (D,), jnp.float32), 0.099609375, 1.8984375).astype(jnp.bfloat16),
        "cotangent": normal_values(streams_of[11], (SEQS, LEN, D), 1.0, 6.0, ((0, 4), (1, 4))),
    }


epsilon = 1e-05
rope_base = 10000.0
masked_value = -1e+30
highest = lax.Precision.HIGHEST

@jax.custom_vjp
def low(v):
    return lax.optimization_barrier(v.astype(jnp.bfloat16)).astype(jnp.float32)

@jax.custom_vjp
def low_back(v):
    return v

def low_keep(v):
    return (low(v), None)

def low_pass(kept, grad):
    return (grad,)

def back_keep(v):
    return (v, None)

def back_low(kept, grad):
    return (low(grad),)
low.defvjp(low_keep, low_pass)
low_back.defvjp(back_keep, back_low)

def doc_positions(segment_row):
    indices = jnp.arange(segment_row.shape[0], dtype=jnp.int32)
    previous = jnp.concatenate([segment_row[:1], segment_row[:-1]])
    starts_at = jnp.where(segment_row != previous, indices, 0).astype(jnp.int32)
    return indices - lax.cummax(starts_at, axis=0)

def rope_tables(positions):
    half_dim = HEAD // 2
    frequency = jnp.power(rope_base, -jnp.arange(half_dim, dtype=jnp.float32) / half_dim)
    angles = positions.astype(jnp.float32)[..., None] * frequency
    return (jnp.cos(angles)[..., None, :], jnp.sin(angles)[..., None, :])

def rotate(values, cosine, sine_table):
    half_dim = HEAD // 2
    first_half = values[..., :half_dim]
    second_half = values[..., half_dim:]
    return jnp.concatenate([first_half * cosine - second_half * sine_table, second_half * cosine + first_half * sine_table], -1)

def matmul(left_side, right_side):
    return jnp.dot(left_side, right_side, precision=highest)

def layer_forward(segment_row, inputs, query_weight, key_weight, value_weight, output_weight, gate_weight, up_weight, down_weight, attn_gain, ffn_gain):
    length = inputs.shape[0]
    group_size = HEADS // KV_HEADS
    cosine, sine_table = rope_tables(doc_positions(segment_row))
    inv_one = lax.rsqrt(lax.optimization_barrier(jnp.mean(inputs * inputs, -1, keepdims=True)) + epsilon)
    normed_one = low(inputs * inv_one * attn_gain)
    queries = low_back(matmul(normed_one, query_weight)).reshape(length, HEADS, HEAD)
    key_proj = low_back(matmul(normed_one, key_weight)).reshape(length, KV_HEADS, HEAD)
    values = low_back(matmul(normed_one, value_weight)).reshape(length, KV_HEADS, HEAD)
    queries = low(rotate(queries, cosine, sine_table) * HEAD ** (-0.5)).reshape(length, KV_HEADS, group_size, HEAD)
    key_proj = low(rotate(key_proj, cosine, sine_table))
    values = low(values)
    scores = low_back(jnp.einsum('ighd,jgd->ghij', queries, key_proj, precision=highest))
    indices = jnp.arange(length)
    allowed = (segment_row[:, None] == segment_row[None, :]) & (indices[:, None] >= indices[None, :])
    weights = jax.nn.softmax(jnp.where(allowed, scores, masked_value), axis=-1)
    attended = jnp.einsum('ghij,jgd->ighd', low(weights), values, precision=highest).reshape(length, HEADS * HEAD)
    attended = low(low_back(attended))
    residual = inputs + low_back(matmul(attended, output_weight))
    inv_two = lax.rsqrt(lax.optimization_barrier(jnp.mean(residual * residual, -1, keepdims=True)) + epsilon)
    normed_two = low(residual * inv_two * ffn_gain)
    gate_proj = low_back(matmul(normed_two, gate_weight))
    up_value = low_back(matmul(normed_two, up_weight))
    hidden = low(jax.nn.silu(gate_proj) * up_value)
    return residual + low_back(matmul(hidden, down_weight))

def reference(activations, segments, query_weight, key_weight, value_weight, output_weight, gate_weight, up_weight, down_weight, attn_gain, ffn_gain, cotangent):
    weight_list = tuple((weight_arg.astype(jnp.float32) for weight_arg in (query_weight, key_weight, value_weight, output_weight, gate_weight, up_weight, down_weight, attn_gain, ffn_gain)))

    def scan_step(grad_sums, entries):
        inputs, segment_row, grad_rows = entries
        forward_fn = partial(layer_forward, segment_row)
        out_value, pull_back = jax.vjp(forward_fn, inputs.astype(jnp.float32), *weight_list)
        gradients = pull_back(grad_rows.astype(jnp.float32))
        grad_sums = tuple((running + update for running, update in zip(grad_sums, gradients[1:])))
        return (grad_sums, (out_value.astype(jnp.bfloat16), gradients[0]))
    zero_grads = tuple((jnp.zeros_like(weight_arg) for weight_arg in weight_list))
    grad_sums, (block_out, input_grad) = lax.scan(scan_step, zero_grads, (activations, segments, cotangent))
    return (block_out, input_grad, grad_sums[0], grad_sums[1], grad_sums[2], grad_sums[3], grad_sums[4], grad_sums[5], grad_sums[6], grad_sums[7], grad_sums[8])
```

```python
import jax
import jax.numpy as jnp
from jax import lax
from jax.experimental import pallas as pl
from jax.experimental.pallas import tpu as pltpu
from jax.sharding import PartitionSpec as P

HEAD = 64
HALF = HEAD // 2
epsilon = 1e-05
rope_base = 10000.0
masked_value = -1e30
bf16 = jnp.bfloat16
f32 = jnp.float32

SWAP_LOW = [(0, 1), (1, 0), (2, 3), (3, 2)]
SWAP_HIGH = [(0, 2), (2, 0), (1, 3), (3, 1)]
SWAP_TP = [(0, 1), (1, 0)]


def low_swap(value):
    return lax.ppermute(value, "ctx", SWAP_LOW)


def high_swap(value):
    return lax.ppermute(value, "ctx", SWAP_HIGH)


def dot(left, right, left_dim, right_dim):
    return lax.dot_general(
        left, right, (((left_dim,), (right_dim,)), ((), ())), preferred_element_type=f32
    )


def tp_sum(partial_sum):
    mine = partial_sum.astype(bf16)
    return mine.astype(f32) + lax.ppermute(mine, "tp", SWAP_TP).astype(f32)


def ring(shards, step):
    return [(i, (i - step) % shards) for i in range(shards)]


def fetch(weight, ctx, me, shards, direct):
    rows = weight.shape[0] // 4
    mine = lax.dynamic_slice_in_dim(weight, ctx * rows, rows, 0)
    if direct:
        own = [lax.ppermute(mine, "shard", ring(shards, r))[None] for r in range(1, shards)]
        high = [high_swap(piece) for piece in own]
        low = [low_swap(piece) for piece in own]
        both = [low_swap(piece) for piece in high]
        return own, low, high, both
    gathered = lax.all_gather(mine, "shard", axis=0, tiled=False)
    own = jnp.concatenate(
        [
            lax.dynamic_slice_in_dim(gathered, (me + r) % shards, 1, 0)
            for r in range(1, shards)
        ],
        0,
    )
    high = high_swap(own)
    return [own], [low_swap(own)], [high], [low_swap(high)]


def place(weight, pieces, ctx, me, shards, along_rows):
    height, width = weight.shape
    rows = height // 4
    count = len(pieces[0])
    each = pieces[0][0].shape[0]

    def kernel(where, local, *refs):
        parts, out = refs[:-1], refs[-1]
        step = pl.program_id(0)

        def put(slot, value):
            if along_rows:
                out[0, slot] = value
            else:
                out[pl.ds(pl.multiple_of(slot * rows, 16), rows), :] = value

        @pl.when(step == 0)
        def _():
            for slot in range(4):
                put(slot, local[slot])

        for i in range(count):

            @pl.when(step >= 1 if count == 1 else step == i + 1)
            def _():
                for k in range(4):
                    put(jnp.bitwise_xor(where[0], k), parts[k * count + i][0])

    if each == 1:
        piece_spec = pl.BlockSpec((1, rows, width), lambda r, where: (0, 0, 0))
    else:
        piece_spec = pl.BlockSpec(
            (1, rows, width), lambda r, where: (jnp.maximum(r - 1, 0), 0, 0)
        )
    if along_rows:
        out_shape = (shards, 4, rows, width)
        out_spec = pl.BlockSpec(
            (1, 4, rows, width), lambda r, where: (lax.rem(where[1] + r, shards), 0, 0, 0)
        )
    else:
        out_shape = (height, shards * width)
        out_spec = pl.BlockSpec((height, width), lambda r, where: (0, lax.rem(where[1] + r, shards)))
    out = pl.pallas_call(
        kernel,
        out_shape=jax.ShapeDtypeStruct(out_shape, weight.dtype),
        grid_spec=pltpu.PrefetchScalarGridSpec(
            num_scalar_prefetch=1,
            grid=(shards,),
            in_specs=[pl.BlockSpec((4, rows, width), lambda r, where: (0, 0, 0))]
            + [piece_spec] * (4 * count),
            out_specs=out_spec,
        ),
        compiler_params=pltpu.CompilerParams(vmem_limit_bytes=56 * 2**20),
        cost_estimate=pl.CostEstimate(
            flops=0, bytes_accessed=4 * shards * height * width, transcendentals=0
        ),
        name="place",
    )(jnp.stack([ctx, me]), weight.reshape(4, rows, width), *sum(pieces, []))
    return out.reshape(shards * height, width) if along_rows else out


def block_bias(start_row, key_first, diagonal):
    size = start_row.shape[1]
    keys = lax.broadcasted_iota(jnp.int32, (size, size), 0)
    allowed = keys + key_first >= start_row
    if diagonal:
        queries = lax.broadcasted_iota(jnp.int32, (size, size), 1)
        allowed = allowed & (keys <= queries)
    return jnp.where(allowed, 0.0, masked_value).astype(f32)


def turned(block):
    return jnp.transpose(block.astype(f32)).astype(bf16)


def attend_kernel(group, info, q_ref, k_ref, v_ref, start_ref, o_ref, lse_ref, acc, top):
    here, first = info[0], info[1]
    size = q_ref.shape[1]

    def step(block, diagonal):
        keys = turned(k_ref[block])
        values = jnp.concatenate([v_ref[block], jnp.ones((16, size), bf16)], 0)
        bias = block_bias(start_ref[...], block * size, diagonal)
        for h in range(group):
            scores = dot(keys, q_ref[h * HEAD : (h + 1) * HEAD, :], 1, 0) + bias
            block_top = jnp.max(scores, 0, keepdims=True)
            if diagonal:
                weights = jnp.exp(scores - block_top).astype(bf16)
                acc[h] = dot(values, weights, 1, 0)
                top[h] = block_top
            else:
                new_top = jnp.maximum(top[h], block_top)
                weights = jnp.exp(scores - new_top).astype(bf16)
                acc[h] = acc[h] * jnp.exp(top[h] - new_top) + dot(values, weights, 1, 0)
                top[h] = new_top

    step(here, True)

    @pl.loop(first, here)
    def _(block):
        step(block, False)

    for h in range(group):
        total = acc[h, HEAD : HEAD + 1, :]
        o_ref[h * HEAD : (h + 1) * HEAD, :] = (acc[h, :HEAD, :] / total).astype(bf16)
        lse_ref[0, h : h + 1, :] = top[h] + jnp.log(total)


def attend(info, query_t, keyval, start_row, kv_heads, seq):
    blocks, kv_rows, _ = keyval.shape
    size = start_row.shape[1]
    group = query_t.shape[0] // HEAD // kv_heads
    rows = group * HEAD
    return pl.pallas_call(
        lambda *refs: attend_kernel(group, *refs),
        out_shape=(
            jax.ShapeDtypeStruct((query_t.shape[0], size), bf16),
            jax.ShapeDtypeStruct((kv_heads, group, size), f32),
        ),
        grid_spec=pltpu.PrefetchScalarGridSpec(
            num_scalar_prefetch=1,
            grid=(kv_heads,),
            in_specs=[
                pl.BlockSpec((rows, size), lambda g, _: (g, seq)),
                pl.BlockSpec((blocks, HEAD, size), lambda g, _: (0, g, seq)),
                pl.BlockSpec((blocks, HEAD, size), lambda g, _: (0, kv_heads + g, seq)),
                pl.BlockSpec((1, size), lambda g, _: (0, 0)),
            ],
            out_specs=(
                pl.BlockSpec((rows, size), lambda g, _: (g, 0)),
                pl.BlockSpec((1, group, size), lambda g, _: (g, 0, 0)),
            ),
            scratch_shapes=[
                pltpu.VMEM((group, HEAD + 16, size), f32),
                pltpu.VMEM((group, 1, size), f32),
            ],
        ),
        compiler_params=pltpu.CompilerParams(vmem_limit_bytes=48 * 2**20),
        cost_estimate=pl.CostEstimate(
            flops=2 * 2 * query_t.shape[0] * size * size * blocks * 4,
            bytes_accessed=4 * query_t.shape[0] * size,
            transcendentals=0,
        ),
        name="attend",
    )(info, query_t, keyval, keyval, start_row)


def attend_back_kernel(
    group, info, q_ref, k_ref, v_ref, start_ref, d_ref, o_ref, lse_ref, cos_ref, sin_ref,
    dq_ref, dk_ref, dv_ref, acc, inner,
):
    here, first = info[0], info[1]
    size = q_ref.shape[1]
    rows = [slice(h * HEAD, (h + 1) * HEAD) for h in range(group)]
    for h in range(group):
        product = d_ref[rows[h], :].astype(f32) * o_ref[rows[h], :].astype(f32)
        inner[h] = jnp.sum(product, 0, keepdims=True)

    def step(block, diagonal):
        key_block = k_ref[block]
        keys = turned(key_block)
        values = turned(v_ref[block])
        bias = block_bias(start_ref[...], block * size, diagonal)
        key_sum = jnp.zeros((HEAD, size), f32)
        value_sum = jnp.zeros((HEAD, size), f32)
        for h in range(group):
            query, delta = q_ref[rows[h], :], d_ref[rows[h], :]
            scores = dot(keys, query, 1, 0) + bias
            probs = jnp.exp(scores - lse_ref[0, h : h + 1, :])
            probs_delta = dot(values, delta, 1, 0)
            score_delta = (probs * (probs_delta - inner[h])).astype(bf16)
            part = dot(key_block, score_delta, 1, 0)
            if diagonal:
                acc[rows[h], :] = part
            else:
                acc[rows[h], :] += part
            key_sum += dot(query, score_delta, 1, 1)
            value_sum += dot(delta, probs.astype(bf16), 1, 1)
        dk_ref[block] = key_sum.astype(bf16)
        dv_ref[block] = value_sum.astype(bf16)

    step(here, True)

    @pl.loop(first, here)
    def _(block):
        step(block, False)

    def clear(block):
        dk_ref[block] = jnp.zeros((HEAD, size), bf16)
        dv_ref[block] = jnp.zeros((HEAD, size), bf16)

    pl.loop(0, first)(clear)
    pl.loop(here + 1, k_ref.shape[0])(clear)

    cosine, sine = cos_ref[...], sin_ref[...]
    for h in range(group):
        upper = acc[h * HEAD : h * HEAD + HALF, :]
        lower = acc[h * HEAD + HALF : (h + 1) * HEAD, :]
        scale = HEAD ** (-0.5)
        dq_ref[h * HEAD : h * HEAD + HALF, :] = (
            (upper * cosine + lower * sine) * scale
        ).astype(bf16)
        dq_ref[h * HEAD + HALF : (h + 1) * HEAD, :] = (
            (lower * cosine - upper * sine) * scale
        ).astype(bf16)


def attend_back(
    info, query_t, keyval, start_row, delta_t, mixed_t, log_sums, cosine, sine, kv_heads, seq
):
    blocks = keyval.shape[0]
    size = start_row.shape[1]
    group = query_t.shape[0] // HEAD // kv_heads
    rows = group * HEAD
    kv_out = jax.ShapeDtypeStruct((blocks, kv_heads * HEAD, size), bf16)
    kv_spec = pl.BlockSpec((blocks, HEAD, size), lambda g, _: (0, g, 0))
    return pl.pallas_call(
        lambda *refs: attend_back_kernel(group, *refs),
        out_shape=(jax.ShapeDtypeStruct((query_t.shape[0], size), bf16), kv_out, kv_out),
        grid_spec=pltpu.PrefetchScalarGridSpec(
            num_scalar_prefetch=1,
            grid=(kv_heads,),
            in_specs=[
                pl.BlockSpec((rows, size), lambda g, _: (g, seq)),
                pl.BlockSpec((blocks, HEAD, size), lambda g, _: (0, g, seq)),
                pl.BlockSpec((blocks, HEAD, size), lambda g, _: (0, kv_heads + g, seq)),
                pl.BlockSpec((1, size), lambda g, _: (0, 0)),
                pl.BlockSpec((rows, size), lambda g, _: (g, seq)),
                pl.BlockSpec((rows, size), lambda g, _: (g, 0)),
                pl.BlockSpec((1, group, size), lambda g, _: (g, 0, 0)),
                pl.BlockSpec((HALF, size), lambda g, _: (0, seq)),
                pl.BlockSpec((HALF, size), lambda g, _: (0, seq)),
            ],
            out_specs=(pl.BlockSpec((rows, size), lambda g, _: (g, 0)), kv_spec, kv_spec),
            scratch_shapes=[
                pltpu.VMEM((rows, size), f32),
                pltpu.VMEM((group, 1, size), f32),
            ],
        ),
        compiler_params=pltpu.CompilerParams(vmem_limit_bytes=48 * 2**20),
        cost_estimate=pl.CostEstimate(
            flops=5 * 2 * query_t.shape[0] * size * size * blocks * 4,
            bytes_accessed=8 * query_t.shape[0] * size,
            transcendentals=0,
        ),
        name="attend_back",
    )(info, query_t, keyval, keyval, start_row, delta_t, mixed_t, log_sums, cosine, sine)


def rotate_t(values, cosine, sine):
    heads = values.reshape(-1, 2, HALF, values.shape[1])
    first, second = heads[:, 0], heads[:, 1]
    return jnp.stack([first * cosine - second * sine, second * cosine + first * sine], 1).reshape(
        values.shape
    )


def pick(index, when_zero, when_one):
    return jnp.where(index == 0, when_zero, when_one)


def block_products(lefts, rights, came, high, shards, left_rows, right_rows, left_cut):
    cut_side, whole_side = (lefts, rights) if left_cut else (rights, lefts)
    whole_rows = right_rows if left_cut else left_rows
    tokens, model_width = cut_side[0].shape
    part = model_width // shards // 2
    whole = whole_side[0].shape[1 - whole_rows]
    tile = whole // 2 if whole > 1408 else whole
    steps = whole // tile
    cut_spec = pl.BlockSpec((tokens, part), lambda j, s, where: (0, s * 2 + where[0]))
    if whole_rows == 0:
        whole_spec = pl.BlockSpec((tokens, tile), lambda j, s, where: (0, j))
    else:
        whole_spec = pl.BlockSpec((tile, tokens), lambda j, s, where: (j, 0))
    left_spec, right_spec = (cut_spec, whole_spec) if left_cut else (whole_spec, cut_spec)
    if left_cut:
        out_shape = (shards, part, whole)
        out_spec = pl.BlockSpec((1, part, tile), lambda j, s, where: (s, 0, j))
    else:
        out_shape = (shards, whole, part)
        out_spec = pl.BlockSpec((1, tile, part), lambda j, s, where: (s, j, 0))

    def kernel(where, *refs):
        total = dot(refs[0][...], refs[2][...], left_rows, right_rows)
        total += dot(refs[1][...], refs[3][...], left_rows, right_rows)
        if came is not None:
            total += refs[4][0].astype(f32)
        refs[-1][0] = total.astype(bf16)

    extra = [] if came is None else [came]
    return pl.pallas_call(
        kernel,
        out_shape=jax.ShapeDtypeStruct(out_shape, bf16),
        grid_spec=pltpu.PrefetchScalarGridSpec(
            num_scalar_prefetch=1,
            grid=(steps, shards),
            in_specs=[left_spec] * 2 + [right_spec] * 2 + [out_spec] * len(extra),
            out_specs=out_spec,
        ),
        compiler_params=pltpu.CompilerParams(vmem_limit_bytes=56 * 2**20),
        cost_estimate=pl.CostEstimate(
            flops=4 * tokens * shards * part * whole,
            bytes_accessed=4 * tokens * (shards * part + whole) + 2 * shards * part * whole,
            transcendentals=0,
        ),
        name="block_products",
    )(high.reshape(1), *lefts, *rights, *extra)


def column_half(values, which, shards):
    tokens, width = values.shape
    part = width // shards // 2
    return lax.dynamic_slice_in_dim(values.reshape(tokens, shards, 2, part), which, 1, 2)[:, :, 0]


def plain_products(lefts, rights, came, high, shards, left_rows, right_rows, left_cut):
    left = jnp.concatenate(lefts, left_rows)
    right = jnp.concatenate(rights, right_rows)
    if left_cut:
        total = jnp.einsum(
            "tsp,tn->spn" if right_rows == 0 else "tsp,nt->spn",
            column_half(left, high, shards), right, preferred_element_type=f32,
        )
    else:
        total = jnp.einsum(
            "tn,tsp->snp" if left_rows == 0 else "nt,tsp->snp",
            left, column_half(right, high, shards), preferred_element_type=f32,
        )
    return (total if came is None else total + came.astype(f32)).astype(bf16)


def reduced(lefts, rights, high, shards, left_rows, right_rows, left_cut):
    width = (lefts if left_cut else rights)[0].shape[1]
    products = block_products if width // shards // 2 % 128 == 0 else plain_products
    other = products(lefts, rights, None, 1 - high, shards, left_rows, right_rows, left_cut)
    came = high_swap(other)
    total = products(lefts, rights, came, high, shards, left_rows, right_rows, left_cut)
    return lax.psum_scatter(total, "shard", scatter_dimension=0, tiled=True)[0]


def halves(high, own, axis):
    came = high_swap(own)
    return jnp.concatenate([pick(high, own, came), pick(high, came, own)], axis)


def body(
    activations,
    segments,
    query_weight,
    key_weight,
    value_weight,
    output_weight,
    gate_weight,
    up_weight,
    down_weight,
    attn_gain,
    ffn_gain,
    cotangent,
):
    seq_here, block_len, model_width = activations.shape
    seq_len = segments.shape[1]
    tokens = seq_here * block_len
    query_cols = query_weight.shape[1]
    kv_width = key_weight.shape[1]
    kv_heads = kv_width // HEAD
    shards = lax.axis_size("shard")
    ctx = lax.axis_index("ctx")
    low, high = ctx % 2, ctx // 2

    me = lax.axis_index("shard")
    small = shards <= 4

    def whole(weight, along_rows, direct):
        pieces = fetch(weight, ctx, me, shards, direct and small)
        return place(weight, pieces, ctx, me, shards, along_rows)

    qkv_local = jnp.concatenate([query_weight, key_weight, value_weight], 1)
    qkv_weight = whole(qkv_local, True, False)
    gain_one = lax.all_gather(jnp.stack([attn_gain, ffn_gain]), "shard", axis=1, tiled=True)
    gain_one, gain_two = gain_one[0].astype(f32), gain_one[1].astype(f32)
    out_weight = whole(output_weight, False, False)
    down_full = whole(down_weight, False, False)
    gate_full = whole(gate_weight, True, False)
    up_full = whole(up_weight, True, True)

    index = jnp.arange(seq_len, dtype=jnp.int32)[None, :]
    doc_start = jnp.zeros_like(segments)
    for number in range(1, 4):
        before = jnp.sum((segments < number).astype(jnp.int32), 1, keepdims=True)
        doc_start = jnp.where(segments == number, before, doc_start)
    offset = ctx * block_len
    start_here = lax.dynamic_slice_in_dim(doc_start, offset, block_len, 1)
    position = lax.dynamic_slice_in_dim(index, offset, block_len, 1) - start_here
    frequency = jnp.power(rope_base, -jnp.arange(HALF, dtype=f32) / HALF)
    angles = frequency[:, None] * position.reshape(1, tokens).astype(f32)
    cosine, sine = jnp.cos(angles), jnp.sin(angles)
    first_block = start_here[:, 0] // block_len

    inputs = activations.reshape(tokens, model_width).astype(f32)
    grad_out = cotangent.reshape(tokens, model_width)
    inv_one = lax.rsqrt(jnp.mean(inputs * inputs, -1, keepdims=True) + epsilon)
    unit_one = inputs * inv_one
    normed_one = (unit_one * gain_one[None, :]).astype(bf16)

    projected = dot(qkv_weight, normed_one, 0, 1)
    query_t = (rotate_t(projected[:query_cols], cosine, sine) * HEAD ** (-0.5)).astype(bf16)
    key_t = rotate_t(projected[query_cols : query_cols + kv_width], cosine, sine).astype(bf16)
    value_t = projected[query_cols + kv_width :].astype(bf16)
    keyval = lax.all_gather(jnp.concatenate([key_t, value_t], 0), "ctx", axis=0, tiled=False)

    mixed, log_sums, residual, infos = [], [], [], []
    for s in range(seq_here):
        infos.append(jnp.stack([ctx, first_block[s]]).astype(jnp.int32))
        mixed_s, log_s = attend(infos[s], query_t, keyval, start_here[s : s + 1], kv_heads, s)
        mixed.append(mixed_s)
        log_sums.append(log_s)
        residual.append(tp_sum(dot(mixed_s, out_weight, 0, 0)))
    residual = inputs + jnp.concatenate(residual, 0)
    mixed_t = jnp.concatenate(mixed, 1)

    inv_two = lax.rsqrt(jnp.mean(residual * residual, -1, keepdims=True) + epsilon)
    unit_two = residual * inv_two
    normed_two = (unit_two * gain_two[None, :]).astype(bf16)
    gate_proj = dot(normed_two, gate_full, 1, 0)
    up_value = dot(normed_two, up_full, 1, 0)
    sigmoid_gate = jax.nn.sigmoid(gate_proj)
    silu_gate = gate_proj * sigmoid_gate
    hidden = (silu_gate * up_value).astype(bf16)

    hidden_delta = dot(grad_out, down_full, 1, 1)
    gate_delta = (
        hidden_delta * up_value * sigmoid_gate * (1.0 + gate_proj * (1.0 - sigmoid_gate))
    ).astype(bf16)
    up_delta = (hidden_delta * silu_gate).astype(bf16)
    chunk = model_width // 4
    parts = []
    for i in range(4):
        rows = slice(i * chunk, (i + 1) * chunk)
        parts.append(tp_sum(dot(gate_delta, gate_full[rows], 1, 1) + dot(up_delta, up_full[rows], 1, 1)))
    normed_two_delta = jnp.concatenate(parts, 1)
    ffn_branch = tp_sum(dot(hidden, down_full, 1, 0))
    block_out = (residual + ffn_branch).astype(bf16).reshape(activations.shape)

    ffn_gain_term = jnp.sum(normed_two_delta * unit_two, 0)
    scaled_two = normed_two_delta * gain_two[None, :]
    residual_delta = grad_out.astype(f32) + inv_two * (
        scaled_two - unit_two * jnp.mean(scaled_two * unit_two, -1, keepdims=True)
    )
    residual_round = residual_delta.astype(bf16)

    kept = pick(low, gate_delta, up_delta)
    given = pick(low, up_delta, gate_delta)
    normed_pair = (normed_two, low_swap(normed_two))
    gate_up = reduced(normed_pair, (kept, low_swap(given)), high, shards, 0, 0, True)
    gate_up = halves(high, gate_up, 0)
    gate_up_other = low_swap(gate_up)
    gate_grad = pick(low, gate_up, gate_up_other).astype(f32)
    up_grad = pick(low, gate_up_other, gate_up).astype(f32)

    part = hidden.shape[1] // 2
    hidden_kept = lax.dynamic_slice_in_dim(hidden, low * part, part, 1)
    hidden_given = lax.dynamic_slice_in_dim(hidden, (1 - low) * part, part, 1)
    hidden_pair = (hidden_kept, low_swap(hidden_given))
    cotangent_pair = (grad_out, low_swap(grad_out))
    down = reduced(hidden_pair, cotangent_pair, high, shards, 0, 0, False)
    down = halves(high, down, 1)
    down_other = low_swap(down)
    down_grad = jnp.concatenate([pick(low, down, down_other), pick(low, down_other, down)], 0)
    down_grad = down_grad.astype(f32)

    delta_t = dot(out_weight, residual_round, 1, 1).astype(bf16)

    half_rows = query_cols // 2
    mixed_kept = lax.dynamic_slice_in_dim(mixed_t, low * half_rows, half_rows, 0)
    mixed_given = lax.dynamic_slice_in_dim(mixed_t, (1 - low) * half_rows, half_rows, 0)
    mixed_pair = (mixed_kept, low_swap(mixed_given))
    residual_pair = (residual_round, low_swap(residual_round))
    output = reduced(mixed_pair, residual_pair, high, shards, 1, 0, False)
    output = halves(high, output, 1)
    output_other = low_swap(output)
    output_grad = jnp.concatenate(
        [pick(low, output, output_other), pick(low, output_other, output)], 0
    ).astype(f32)

    deltas, normed_one_delta = [], []
    for s in range(seq_here):
        query_delta, key_part, value_part = attend_back(
            infos[s], query_t, keyval, start_here[s : s + 1], delta_t, mixed[s], log_sums[s],
            cosine, sine, kv_heads, s,
        )
        part_sum = jnp.concatenate([key_part, value_part], 1).reshape(2, 2, 2 * kv_width, block_len)
        sent = lax.dynamic_index_in_dim(part_sum, 1 - high, 0, False)
        kept = lax.dynamic_index_in_dim(part_sum, high, 0, False)
        kept = kept.astype(f32) + high_swap(sent).astype(f32)
        sent = lax.dynamic_index_in_dim(kept, 1 - low, 0, False).astype(bf16)
        kept = lax.dynamic_index_in_dim(kept, low, 0, False)
        keyval_delta = kept + low_swap(sent).astype(f32)
        cols = slice(s * block_len, (s + 1) * block_len)
        key_delta = rotate_t(keyval_delta[:kv_width], cosine[:, cols], -sine[:, cols])
        delta = jnp.concatenate(
            [query_delta, key_delta.astype(bf16), keyval_delta[kv_width:].astype(bf16)], 0
        )
        deltas.append(delta)
        normed_one_delta.append(tp_sum(dot(delta, qkv_weight, 0, 1)))
    delta_all = jnp.concatenate(deltas, 1)
    normed_one_delta = jnp.concatenate(normed_one_delta, 0)

    attn_gain_term = jnp.sum(normed_one_delta * unit_one, 0)
    scaled_one = normed_one_delta * gain_one[None, :]
    input_grad = residual_delta + inv_one * (
        scaled_one - unit_one * jnp.mean(scaled_one * unit_one, -1, keepdims=True)
    )

    half_rows = delta_all.shape[0] // 2
    delta_kept = lax.dynamic_slice_in_dim(delta_all, low * half_rows, half_rows, 0)
    delta_given = lax.dynamic_slice_in_dim(delta_all, (1 - low) * half_rows, half_rows, 0)
    delta_pair = (delta_kept.T, low_swap(delta_given).T)
    normed_pair_one = (normed_one, low_swap(normed_one))
    qkv = reduced(normed_pair_one, delta_pair, high, shards, 0, 0, True)
    qkv = halves(high, qkv, 0)
    qkv_other = low_swap(qkv)
    qkv_grad = jnp.concatenate([pick(low, qkv, qkv_other), pick(low, qkv_other, qkv)], 1)
    qkv_grad = qkv_grad.astype(f32)

    gain_terms = jnp.stack([attn_gain_term, ffn_gain_term])
    gain_terms = gain_terms + low_swap(gain_terms)
    gain_terms = gain_terms + high_swap(gain_terms)
    gain_terms = gain_terms.reshape(2, shards, model_width // shards)
    gain_grads = lax.dynamic_index_in_dim(gain_terms, me, 1, False)
    for k in range(1, shards):
        block = lax.dynamic_index_in_dim(gain_terms, (me + k) % shards, 1, False)
        gain_grads = gain_grads + lax.ppermute(
            block, "shard", [(i, (i + k) % shards) for i in range(shards)]
        )

    return (
        block_out,
        input_grad.reshape(activations.shape),
        qkv_grad[:, :query_cols],
        qkv_grad[:, query_cols : query_cols + kv_width],
        qkv_grad[:, query_cols + kv_width :],
        output_grad,
        gate_grad,
        up_grad,
        down_grad,
        gain_grads[0],
        gain_grads[1],
    )


def solution(mesh):
    return jax.shard_map(
        body,
        mesh=mesh,
        in_specs=(
            P("shard", "ctx", None),
            P("shard", None),
            P("shard", "tp"),
            P("shard", "tp"),
            P("shard", "tp"),
            P("tp", "shard"),
            P("shard", "tp"),
            P("shard", "tp"),
            P("tp", "shard"),
            P("shard"),
            P("shard"),
            P("shard", "ctx", None),
        ),
        out_specs=(
            P("shard", "ctx", None),
            P("shard", "ctx", None),
            P("shard", "tp"),
            P("shard", "tp"),
            P("shard", "tp"),
            P("tp", "shard"),
            P("shard", "tp"),
            P("shard", "tp"),
            P("tp", "shard"),
            P("shard"),
            P("shard"),
        ),
        check_vma=False,
    )
```

```python
import jax
import jax.numpy as jnp
from jax import lax
from jax.experimental import pallas as pl
from jax.experimental.pallas import tpu as pltpu
from jax.sharding import PartitionSpec as P

HEAD = 64
HALF = HEAD // 2
epsilon = 1e-05
rope_base = 10000.0
masked_value = -1e30
bf16 = jnp.bfloat16
f32 = jnp.float32

SWAP_LOW = [(0, 1), (1, 0), (2, 3), (3, 2)]
SWAP_HIGH = [(0, 2), (2, 0), (1, 3), (3, 1)]
SWAP_TP = [(0, 1), (1, 0)]


def low_swap(value):
    return lax.ppermute(value, "ctx", SWAP_LOW)


def high_swap(value):
    return lax.ppermute(value, "ctx", SWAP_HIGH)


def dot(left, right, left_dim, right_dim):
    return lax.dot_general(
        left, right, (((left_dim,), (right_dim,)), ((), ())), preferred_element_type=f32
    )


def tp_sum(partial_sum):
    mine = partial_sum.astype(bf16)
    return mine.astype(f32) + lax.ppermute(mine, "tp", SWAP_TP).astype(f32)


UNREAD = pl.BlockSpec(memory_space=pl.ANY)


def taking(microseconds):
    return pl.CostEstimate(flops=int(microseconds * 0.05e9), bytes_accessed=int(microseconds * 0.15e6), transcendentals=0)


def tie(value, *after):
    def kernel(*refs):
        pass

    return pl.pallas_call(
        kernel,
        out_shape=jax.ShapeDtypeStruct(value.shape, value.dtype),
        in_specs=[UNREAD] * (1 + len(after)),
        out_specs=UNREAD,
        input_output_aliases={0: 0},
        name="tie",
    )(value, *after)


def ring(shards, step):
    return [(i, (i - step) % shards) for i in range(shards)]


def quarter(weight, ctx):
    rows = weight.shape[0] // 4
    return lax.dynamic_slice_in_dim(weight, ctx * rows, rows, 0)


def gathered(weight, ctx):
    return lax.all_gather(quarter(weight, ctx), "shard", axis=0, tiled=False)


def spread(own, *after):
    high = [high_swap(piece) for piece in own]
    low = [low_swap(piece) for piece in own]
    if after:
        high = [tie(piece, *after) for piece in high]
    return own, low, high, [low_swap(piece) for piece in high]


def others(everyone, me):
    shards = everyone.shape[0]
    steps = [lax.dynamic_slice_in_dim(everyone, (me + r) % shards, 1, 0) for r in range(1, shards)]
    return jnp.concatenate(steps, 0)


def place(weight, pieces, ctx, me, shards, along_rows, after=()):
    height, width = weight.shape
    rows = height // 4
    count = len(pieces[0])
    each = pieces[0][0].shape[0]

    def kernel(where, local, *refs):
        parts, out = refs[: 4 * count], refs[-1]
        step = pl.program_id(0)

        def put(slot, value):
            if along_rows:
                out[0, slot] = value
            else:
                out[pl.ds(pl.multiple_of(slot * rows, 16), rows), :] = value

        @pl.when(step == 0)
        def _():
            for slot in range(4):
                put(slot, local[slot])

        for i in range(count):

            @pl.when(step >= 1 if count == 1 else step == i + 1)
            def _():
                for k in range(4):
                    put(jnp.bitwise_xor(where[0], k), parts[k * count + i][0])

    if each == 1:
        piece_spec = pl.BlockSpec((1, rows, width), lambda r, where: (0, 0, 0))
    else:
        piece_spec = pl.BlockSpec(
            (1, rows, width), lambda r, where: (jnp.maximum(r - 1, 0), 0, 0)
        )
    if along_rows:
        out_shape = (shards, 4, rows, width)
        out_spec = pl.BlockSpec(
            (1, 4, rows, width), lambda r, where: (lax.rem(where[1] + r, shards), 0, 0, 0)
        )
    else:
        out_shape = (height, shards * width)
        out_spec = pl.BlockSpec((height, width), lambda r, where: (0, lax.rem(where[1] + r, shards)))
    out = pl.pallas_call(
        kernel,
        out_shape=jax.ShapeDtypeStruct(out_shape, weight.dtype),
        grid_spec=pltpu.PrefetchScalarGridSpec(
            num_scalar_prefetch=1,
            grid=(shards,),
            in_specs=[pl.BlockSpec((4, rows, width), lambda r, where: (0, 0, 0))]
            + [piece_spec] * (4 * count)
            + [UNREAD] * len(after),
            out_specs=out_spec,
        ),
        compiler_params=pltpu.CompilerParams(vmem_limit_bytes=56 * 2**20),
        cost_estimate=taking(8),
        name="place",
    )(jnp.stack([ctx, me]), weight.reshape(4, rows, width), *sum(pieces, []), *after)
    return out.reshape(shards * height, width) if along_rows else out


TILE = 256
ROOMY = pltpu.CompilerParams(vmem_limit_bytes=56 * 2**20)


def feed_forward(normed, weights, pieces, ctx, me, shards, after=()):
    tokens, model_width = normed.shape
    height, width = weights[0].shape
    rows = height // 4

    def kernel(where, normed_ref, *refs):
        hidden_ref, gate_ref, up_ref, full_ref = refs[-4:]
        for w in range(2):
            local, parts = refs[5 * w], refs[5 * w + 1 : 5 * w + 5]
            for slot in range(4):
                start = pl.multiple_of(where[1] * height + slot * rows, rows)
                full_ref[w, pl.ds(start, rows), :] = local[slot]
            for r in range(1, shards):
                first = lax.rem(where[1] + r, shards) * height
                for k in range(4):
                    start = first + jnp.bitwise_xor(where[0], k) * rows
                    full_ref[w, pl.ds(pl.multiple_of(start, rows), rows), :] = parts[k][r - 1]
        gate = dot(normed_ref[...], full_ref[0], 1, 0)
        up = dot(normed_ref[...], full_ref[1], 1, 0)
        sigmoid = 1.0 / (1.0 + jnp.exp(-gate))
        silu = gate * sigmoid
        hidden_ref[...] = (silu * up).astype(bf16)
        gate_ref[...] = (up * sigmoid * (1.0 + gate * (1.0 - sigmoid))).astype(bf16)
        up_ref[...] = silu.astype(bf16)

    weight_specs = [pl.BlockSpec((4, rows, TILE), lambda j, _: (0, 0, j))] + [
        pl.BlockSpec((shards - 1, rows, TILE), lambda j, _: (0, 0, j))
    ] * 4
    token_spec = pl.BlockSpec((tokens, TILE), lambda j, _: (0, j))
    token_shape = jax.ShapeDtypeStruct((tokens, width), bf16)
    operands = []
    for weight, parts in zip(weights, pieces):
        operands += [weight.reshape(4, rows, width)] + [part[0] for part in parts]
    return pl.pallas_call(
        kernel,
        out_shape=(
            token_shape,
            token_shape,
            token_shape,
            jax.ShapeDtypeStruct((2, model_width, width), bf16),
        ),
        grid_spec=pltpu.PrefetchScalarGridSpec(
            num_scalar_prefetch=1,
            grid=(width // TILE,),
            in_specs=[pl.BlockSpec((tokens, model_width), lambda j, _: (0, 0))] + weight_specs * 2
            + [UNREAD] * len(after),
            out_specs=(
                token_spec,
                token_spec,
                token_spec,
                pl.BlockSpec((2, model_width, TILE), lambda j, _: (0, 0, j)),
            ),
        ),
        compiler_params=ROOMY,
        cost_estimate=taking(29),
        name="feed_forward",
    )(jnp.stack([ctx, me]), normed, *operands, *after)


def feed_back(grad_out, down_full, gate_factor, up_factor, low, after=()):
    tokens, model_width = grad_out.shape
    width = down_full.shape[0]

    def kernel(where, grad_ref, down_ref, gate_ref, up_ref, *rest):
        kept_ref, given_ref = rest[-2:]
        hidden_delta = dot(grad_ref[...], down_ref[...], 1, 1)
        gate_delta = (hidden_delta * gate_ref[...].astype(f32)).astype(bf16)
        up_delta = (hidden_delta * up_ref[...].astype(f32)).astype(bf16)

        @pl.when(where[0] == 0)
        def _():
            kept_ref[...] = gate_delta
            given_ref[...] = up_delta

        @pl.when(where[0] != 0)
        def _():
            kept_ref[...] = up_delta
            given_ref[...] = gate_delta

    token_spec = pl.BlockSpec((tokens, TILE), lambda j, _: (0, j))
    token_shape = jax.ShapeDtypeStruct((tokens, width), bf16)
    return pl.pallas_call(
        kernel,
        out_shape=(token_shape, token_shape),
        grid_spec=pltpu.PrefetchScalarGridSpec(
            num_scalar_prefetch=1,
            grid=(width // TILE,),
            in_specs=[
                pl.BlockSpec((tokens, model_width), lambda j, _: (0, 0)),
                pl.BlockSpec((TILE, model_width), lambda j, _: (j, 0)),
                token_spec,
                token_spec,
            ]
            + [UNREAD] * len(after),
            out_specs=(token_spec, token_spec),
        ),
        compiler_params=ROOMY,
        cost_estimate=taking(19),
        name="feed_back",
    )(low.reshape(1), grad_out, down_full, gate_factor, up_factor, *after)


def feed_input(kept, given, full, low, part, parts, after=()):
    tokens, width = kept.shape
    model_width = full.shape[1]
    tiles = model_width // parts // TILE

    def kernel(where, kept_ref, given_ref, kept_weight, given_weight, *rest):
        total = dot(kept_ref[...], kept_weight[0], 1, 1)
        total += dot(given_ref[...], given_weight[0], 1, 1)
        rest[-1][...] = total.astype(bf16)

    return pl.pallas_call(
        kernel,
        out_shape=jax.ShapeDtypeStruct((tokens, model_width // parts), bf16),
        grid_spec=pltpu.PrefetchScalarGridSpec(
            num_scalar_prefetch=1,
            grid=(tiles,),
            in_specs=[
                pl.BlockSpec((tokens, width), lambda j, _: (0, 0)),
                pl.BlockSpec((tokens, width), lambda j, _: (0, 0)),
                pl.BlockSpec((1, TILE, width), lambda j, where: (where[0], part * tiles + j, 0)),
                pl.BlockSpec((1, TILE, width), lambda j, where: (1 - where[0], part * tiles + j, 0)),
            ]
            + [UNREAD] * len(after),
            out_specs=pl.BlockSpec((tokens, TILE), lambda j, _: (0, j)),
        ),
        compiler_params=ROOMY,
        cost_estimate=taking(10),
        name="feed_input",
    )(low.reshape(1), kept, given, full, full, *after)


def product(left, right, left_dim, right_dim, tile, after=()):
    rows = left.shape[1 - left_dim]
    width = right.shape[1 - right_dim]
    turn = left_dim == 0 and right_dim == 1

    def kernel(left_ref, right_ref, *rest):
        value = turned(left_ref[...]) if turn else left_ref[...]
        total = dot(value, right_ref[...], 1 if turn else left_dim, right_dim)
        rest[-1][...] = total.astype(bf16)

    if right_dim == 0:
        right_spec = pl.BlockSpec((right.shape[0], tile), lambda j: (0, j))
    else:
        right_spec = pl.BlockSpec((tile, left.shape[left_dim]), lambda j: (j, 0))
    return pl.pallas_call(
        kernel,
        out_shape=jax.ShapeDtypeStruct((rows, width), bf16),
        grid=(width // tile,),
        in_specs=[pl.BlockSpec(left.shape, lambda j: (0, 0)), right_spec] + [UNREAD] * len(after),
        out_specs=pl.BlockSpec((rows, tile), lambda j: (0, j)),
        compiler_params=ROOMY,
        cost_estimate=taking(6),
        name="product",
    )(left, right, *after)


def add_and_norm(activations, mine, came, gain, after=()):
    count = len(mine)
    rows, width = mine[0].shape

    def kernel(act_ref, gain_ref, *refs):
        residual_ref, normed_ref = refs[-2:]
        for i in range(count):

            @pl.when(pl.program_id(0) == i)
            def _():
                total = refs[i][...].astype(f32) + refs[count + i][...].astype(f32)
                residual = act_ref[...].astype(f32) + total
                inverse = lax.rsqrt(jnp.mean(residual * residual, -1, keepdims=True) + epsilon)
                residual_ref[...] = residual
                normed_ref[...] = (residual * inverse * gain_ref[...]).astype(bf16)

    row_spec = pl.BlockSpec((rows, width), lambda i: (i, 0))
    one_spec = pl.BlockSpec((rows, width), lambda i: (0, 0))
    return pl.pallas_call(
        kernel,
        out_shape=(
            jax.ShapeDtypeStruct(activations.shape, f32),
            jax.ShapeDtypeStruct(activations.shape, bf16),
        ),
        grid=(count,),
        in_specs=[row_spec, pl.BlockSpec((1, width), lambda i: (0, 0))]
        + [one_spec] * (2 * count)
        + [UNREAD] * len(after),
        out_specs=(row_spec, row_spec),
        compiler_params=ROOMY,
        cost_estimate=taking(9),
        name="add_and_norm",
    )(activations, gain[None, :], *mine, *came, *after)


def add_three(residual, mine, came, after=()):
    tokens, width = residual.shape
    rows = 128

    def kernel(residual_ref, mine_ref, came_ref, *rest):
        total = mine_ref[...].astype(f32) + came_ref[...].astype(f32)
        rest[-1][...] = (residual_ref[...] + total).astype(bf16)

    row_spec = pl.BlockSpec((rows, width), lambda i: (i, 0))
    return pl.pallas_call(
        kernel,
        out_shape=jax.ShapeDtypeStruct((tokens, width), bf16),
        grid=(tokens // rows,),
        in_specs=[row_spec] * 3 + [UNREAD] * len(after),
        out_specs=row_spec,
        compiler_params=ROOMY,
        cost_estimate=taking(5),
        name="add_three",
    )(residual, mine, came, *after)


def norm_gradient(value, delta, gain, base):
    inverse = lax.rsqrt(jnp.mean(value * value, -1, keepdims=True) + epsilon)
    unit = value * inverse
    scaled = delta * gain
    total = base + inverse * (scaled - unit * jnp.mean(scaled * unit, -1, keepdims=True))
    return total, jnp.sum(delta * unit, 0, keepdims=True)


def add_term(term_ref, term):
    @pl.when(pl.program_id(0) == 0)
    def _():
        term_ref[...] = term

    @pl.when(pl.program_id(0) != 0)
    def _():
        term_ref[...] += term


def norm_back(values, mine, came, gain, base, after=()):
    count = len(mine)
    tokens, width = values.shape
    rows = 128

    def kernel(value_ref, gain_ref, base_ref, *refs):
        delta = jnp.concatenate(
            [refs[i][...].astype(f32) + refs[count + i][...].astype(f32) for i in range(count)], 1
        )
        total, term = norm_gradient(
            value_ref[...], delta, gain_ref[...], base_ref[...].astype(f32)
        )
        refs[-3][...] = total
        refs[-1][...] = total.astype(bf16)
        add_term(refs[-2], term)

    row_spec = pl.BlockSpec((rows, width), lambda i: (i, 0))
    part_spec = pl.BlockSpec((rows, width // count), lambda i: (i, 0))
    line_spec = pl.BlockSpec((1, width), lambda i: (0, 0))
    return pl.pallas_call(
        kernel,
        out_shape=(
            jax.ShapeDtypeStruct((tokens, width), f32),
            jax.ShapeDtypeStruct((1, width), f32),
            jax.ShapeDtypeStruct((tokens, width), bf16),
        ),
        grid=(tokens // rows,),
        in_specs=[row_spec, line_spec, row_spec]
        + [part_spec] * (2 * count)
        + [UNREAD] * len(after),
        out_specs=(row_spec, line_spec, row_spec),
        compiler_params=ROOMY,
        cost_estimate=taking(12),
        name="norm_back",
    )(values, gain[None, :], base, *mine, *came, *after)


def norm_back_rows(values, mine, came, term, gain, base, after=()):
    count = len(mine)
    tokens, width = values.shape
    rows = 128
    steps = mine[0].shape[0] // rows

    def kernel(value_ref, term_ref, gain_ref, base_ref, *refs):
        for i in range(count):

            @pl.when(pl.program_id(0) // steps == i)
            def _():
                delta = refs[i][...].astype(f32) + refs[count + i][...].astype(f32)
                total, gain_term = norm_gradient(
                    value_ref[...].astype(f32),
                    delta + term_ref[...],
                    gain_ref[...],
                    base_ref[...],
                )
                refs[-2][...] = total
                add_term(refs[-1], gain_term)

    row_spec = pl.BlockSpec((rows, width), lambda i: (i, 0))
    line_spec = pl.BlockSpec((1, width), lambda i: (0, 0))

    def part_spec(at):
        return pl.BlockSpec(
            (rows, width), lambda i: (jnp.clip(i - at * steps, 0, steps - 1), 0)
        )

    part_specs = [part_spec(i) for i in range(count)]
    return pl.pallas_call(
        kernel,
        out_shape=(
            jax.ShapeDtypeStruct((tokens, width), f32),
            jax.ShapeDtypeStruct((1, width), f32),
        ),
        grid=(tokens // rows,),
        in_specs=[row_spec, row_spec, line_spec, row_spec]
        + part_specs * 2
        + [UNREAD] * len(after),
        out_specs=(row_spec, line_spec),
        compiler_params=ROOMY,
        cost_estimate=taking(13),
        name="norm_back_rows",
    )(values, term, gain[None, :], base, *mine, *came, *after)


def block_bias(start_row, key_first, diagonal):
    size = start_row.shape[1]
    keys = lax.broadcasted_iota(jnp.int32, (size, size), 0)
    allowed = keys + key_first >= start_row
    if diagonal:
        queries = lax.broadcasted_iota(jnp.int32, (size, size), 1)
        allowed = allowed & (keys <= queries)
    return jnp.where(allowed, 0.0, masked_value).astype(f32)


def turned(block):
    return jnp.transpose(block.astype(f32)).astype(bf16)


def attend_kernel(group, info, q_ref, k_ref, v_ref, start_ref, *rest):
    o_ref, lse_ref, acc, top = rest[-4:]
    here, first = info[0], info[1]
    size = q_ref.shape[1]

    def step(block, diagonal):
        keys = turned(k_ref[block])
        values = jnp.concatenate([v_ref[block], jnp.ones((16, size), bf16)], 0)
        bias = block_bias(start_ref[...], block * size, diagonal)
        for h in range(group):
            scores = dot(keys, q_ref[h * HEAD : (h + 1) * HEAD, :], 1, 0) + bias
            block_top = jnp.max(scores, 0, keepdims=True)
            if diagonal:
                weights = jnp.exp(scores - block_top).astype(bf16)
                acc[h] = dot(values, weights, 1, 0)
                top[h] = block_top
            else:
                new_top = jnp.maximum(top[h], block_top)
                weights = jnp.exp(scores - new_top).astype(bf16)
                acc[h] = acc[h] * jnp.exp(top[h] - new_top) + dot(values, weights, 1, 0)
                top[h] = new_top

    step(here, True)

    @pl.loop(first, here)
    def _(block):
        step(block, False)

    for h in range(group):
        total = acc[h, HEAD : HEAD + 1, :]
        o_ref[h * HEAD : (h + 1) * HEAD, :] = (acc[h, :HEAD, :] / total).astype(bf16)
        lse_ref[0, h : h + 1, :] = top[h] + jnp.log(total)


def attend(info, query_t, keyval, start_row, kv_heads, seq, after=()):
    blocks, kv_rows, _ = keyval.shape
    size = start_row.shape[1]
    group = query_t.shape[0] // HEAD // kv_heads
    rows = group * HEAD
    return pl.pallas_call(
        lambda *refs: attend_kernel(group, *refs),
        out_shape=(
            jax.ShapeDtypeStruct((query_t.shape[0], size), bf16),
            jax.ShapeDtypeStruct((kv_heads, group, size), f32),
        ),
        grid_spec=pltpu.PrefetchScalarGridSpec(
            num_scalar_prefetch=1,
            grid=(kv_heads,),
            in_specs=[
                pl.BlockSpec((rows, size), lambda g, _: (g, seq)),
                pl.BlockSpec((blocks, HEAD, size), lambda g, _: (0, g, seq)),
                pl.BlockSpec((blocks, HEAD, size), lambda g, _: (0, kv_heads + g, seq)),
                pl.BlockSpec((1, size), lambda g, _: (0, 0)),
            ]
            + [UNREAD] * len(after),
            out_specs=(
                pl.BlockSpec((rows, size), lambda g, _: (g, 0)),
                pl.BlockSpec((1, group, size), lambda g, _: (g, 0, 0)),
            ),
            scratch_shapes=[
                pltpu.VMEM((group, HEAD + 16, size), f32),
                pltpu.VMEM((group, 1, size), f32),
            ],
        ),
        compiler_params=pltpu.CompilerParams(vmem_limit_bytes=48 * 2**20),
        cost_estimate=taking(14),
        name="attend",
    )(info, query_t, keyval, keyval, start_row, *after)


def attend_back_kernel(
    group, info, q_ref, k_ref, v_ref, start_ref, d_ref, o_ref, lse_ref, cos_ref, sin_ref, *rest
):
    dq_ref, dk_ref, dv_ref, acc, inner = rest[-5:]
    here, first = info[0], info[1]
    size = q_ref.shape[1]
    rows = [slice(h * HEAD, (h + 1) * HEAD) for h in range(group)]
    for h in range(group):
        product = d_ref[rows[h], :].astype(f32) * o_ref[rows[h], :].astype(f32)
        inner[h] = jnp.sum(product, 0, keepdims=True)

    def step(block, diagonal):
        key_block = k_ref[block]
        keys = turned(key_block)
        values = turned(v_ref[block])
        bias = block_bias(start_ref[...], block * size, diagonal)
        key_sum = jnp.zeros((HEAD, size), f32)
        value_sum = jnp.zeros((HEAD, size), f32)
        for h in range(group):
            query, delta = q_ref[rows[h], :], d_ref[rows[h], :]
            scores = dot(keys, query, 1, 0) + bias
            probs = jnp.exp(scores - lse_ref[0, h : h + 1, :])
            probs_delta = dot(values, delta, 1, 0)
            score_delta = (probs * (probs_delta - inner[h])).astype(bf16)
            part = dot(key_block, score_delta, 1, 0)
            if diagonal:
                acc[rows[h], :] = part
            else:
                acc[rows[h], :] += part
            key_sum += dot(query, score_delta, 1, 1)
            value_sum += dot(delta, probs.astype(bf16), 1, 1)
        dk_ref[block] = key_sum.astype(bf16)
        dv_ref[block] = value_sum.astype(bf16)

    step(here, True)

    @pl.loop(first, here)
    def _(block):
        step(block, False)

    def clear(block):
        dk_ref[block] = jnp.zeros((HEAD, size), bf16)
        dv_ref[block] = jnp.zeros((HEAD, size), bf16)

    pl.loop(0, first)(clear)
    pl.loop(here + 1, k_ref.shape[0])(clear)

    cosine, sine = cos_ref[...], sin_ref[...]
    for h in range(group):
        upper = acc[h * HEAD : h * HEAD + HALF, :]
        lower = acc[h * HEAD + HALF : (h + 1) * HEAD, :]
        scale = HEAD ** (-0.5)
        dq_ref[h * HEAD : h * HEAD + HALF, :] = (
            (upper * cosine + lower * sine) * scale
        ).astype(bf16)
        dq_ref[h * HEAD + HALF : (h + 1) * HEAD, :] = (
            (lower * cosine - upper * sine) * scale
        ).astype(bf16)


def attend_back(
    info, query_t, keyval, start_row, delta_t, mixed_t, log_sums, cosine, sine, kv_heads, seq, after=()
):
    blocks = keyval.shape[0]
    size = start_row.shape[1]
    group = query_t.shape[0] // HEAD // kv_heads
    rows = group * HEAD
    kv_out = jax.ShapeDtypeStruct((blocks, kv_heads * HEAD, size), bf16)
    kv_spec = pl.BlockSpec((blocks, HEAD, size), lambda g, _: (0, g, 0))
    return pl.pallas_call(
        lambda *refs: attend_back_kernel(group, *refs),
        out_shape=(jax.ShapeDtypeStruct((query_t.shape[0], size), bf16), kv_out, kv_out),
        grid_spec=pltpu.PrefetchScalarGridSpec(
            num_scalar_prefetch=1,
            grid=(kv_heads,),
            in_specs=[
                pl.BlockSpec((rows, size), lambda g, _: (g, seq)),
                pl.BlockSpec((blocks, HEAD, size), lambda g, _: (0, g, seq)),
                pl.BlockSpec((blocks, HEAD, size), lambda g, _: (0, kv_heads + g, seq)),
                pl.BlockSpec((1, size), lambda g, _: (0, 0)),
                pl.BlockSpec((rows, size), lambda g, _: (g, seq)),
                pl.BlockSpec((rows, size), lambda g, _: (g, 0)),
                pl.BlockSpec((1, group, size), lambda g, _: (g, 0, 0)),
                pl.BlockSpec((HALF, size), lambda g, _: (0, seq)),
                pl.BlockSpec((HALF, size), lambda g, _: (0, seq)),
            ]
            + [UNREAD] * len(after),
            out_specs=(pl.BlockSpec((rows, size), lambda g, _: (g, 0)), kv_spec, kv_spec),
            scratch_shapes=[
                pltpu.VMEM((rows, size), f32),
                pltpu.VMEM((group, 1, size), f32),
            ],
        ),
        compiler_params=pltpu.CompilerParams(vmem_limit_bytes=48 * 2**20),
        cost_estimate=taking(16),
        name="attend_back",
    )(info, query_t, keyval, keyval, start_row, delta_t, mixed_t, log_sums, cosine, sine, *after)


def rotate_t(values, cosine, sine):
    heads = values.reshape(-1, 2, HALF, values.shape[1])
    first, second = heads[:, 0], heads[:, 1]
    return jnp.stack([first * cosine - second * sine, second * cosine + first * sine], 1).reshape(
        values.shape
    )


def pick(index, when_zero, when_one):
    return jnp.where(index == 0, when_zero, when_one)


def block_products(
    lefts, rights, came, high, shards, left_rows, right_rows, left_cut, half=None, after=()
):
    cut_side, whole_side = (lefts, rights) if left_cut else (rights, lefts)
    whole_rows = right_rows if left_cut else left_rows
    tokens, model_width = cut_side[0].shape
    if high is None:
        part = model_width // shards
        where_high = jnp.zeros((1,), jnp.int32)
        cut_spec = pl.BlockSpec((tokens, part), lambda j, s, where: (0, s))
    else:
        part = model_width // shards // 2
        where_high = high.reshape(1)
        cut_spec = pl.BlockSpec((tokens, part), lambda j, s, where: (0, s * 2 + where[0]))
    whole = whole_side[0].shape[1 - whole_rows]
    first = 0
    if half is not None:
        whole, first = whole // 2, half
    tile = whole // 2 if whole > 1408 else whole
    steps = whole // tile
    if whole_rows == 0:
        whole_spec = pl.BlockSpec((tokens, tile), lambda j, s, where: (0, first + j))
    else:
        whole_spec = pl.BlockSpec((tile, tokens), lambda j, s, where: (first + j, 0))
    left_spec, right_spec = (cut_spec, whole_spec) if left_cut else (whole_spec, cut_spec)
    if left_cut:
        out_shape = (shards, part, whole)
        out_spec = pl.BlockSpec((1, part, tile), lambda j, s, where: (s, 0, j))
    else:
        out_shape = (shards, whole, part)
        out_spec = pl.BlockSpec((1, tile, part), lambda j, s, where: (s, j, 0))

    def kernel(where, *refs):
        total = dot(refs[0][...], refs[2][...], left_rows, right_rows)
        total += dot(refs[1][...], refs[3][...], left_rows, right_rows)
        if came is not None:
            total += refs[4][0].astype(f32)
        refs[-1][0] = total.astype(bf16)

    extra = [] if came is None else [came]
    return pl.pallas_call(
        kernel,
        out_shape=jax.ShapeDtypeStruct(out_shape, bf16),
        grid_spec=pltpu.PrefetchScalarGridSpec(
            num_scalar_prefetch=1,
            grid=(steps, shards),
            in_specs=[left_spec] * 2
            + [right_spec] * 2
            + [out_spec] * len(extra)
            + [UNREAD] * len(after),
            out_specs=out_spec,
        ),
        compiler_params=pltpu.CompilerParams(vmem_limit_bytes=56 * 2**20),
        cost_estimate=taking(9),
        name="block_products",
    )(where_high, *lefts, *rights, *extra, *after)


def column_half(values, which, shards):
    tokens, width = values.shape
    part = width // shards // 2
    return lax.dynamic_slice_in_dim(values.reshape(tokens, shards, 2, part), which, 1, 2)[:, :, 0]


def plain_products(
    lefts, rights, came, high, shards, left_rows, right_rows, left_cut, half=None, after=()
):
    left = jnp.concatenate(lefts, left_rows)
    right = jnp.concatenate(rights, right_rows)
    if half is not None:
        size = right.shape[1] // 2
        right = right[:, half * size : (half + 1) * size]
    if left_cut:
        total = jnp.einsum(
            "tsp,tn->spn" if right_rows == 0 else "tsp,nt->spn",
            column_half(left, high, shards), right, preferred_element_type=f32,
        )
    else:
        total = jnp.einsum(
            "tn,tsp->snp" if left_rows == 0 else "nt,tsp->snp",
            left, column_half(right, high, shards), preferred_element_type=f32,
        )
    return (total if came is None else total + came.astype(f32)).astype(bf16)


def over_shard(total):
    return lax.psum_scatter(total, "shard", scatter_dimension=0, tiled=True)[0]


class Reduced:
    def __init__(self, lefts, rights, high, shards, left_rows, right_rows, left_cut, half=None):
        width = (lefts if left_cut else rights)[0].shape[1]
        self.products = block_products if width // shards // 2 % 128 == 0 else plain_products
        self.sides = lefts, rights
        self.high = high
        self.rest = shards, left_rows, right_rows, left_cut, half

    def send(self, after=(), swap_after=()):
        self.other = self.products(*self.sides, None, 1 - self.high, *self.rest, after)
        self.sent = tie(self.other, *swap_after)
        self.came = high_swap(self.sent)

    def add(self, after=(), sum_after=()):
        self.total = self.products(*self.sides, self.came, self.high, *self.rest, after)
        self.tied = tie(self.total, *sum_after)
        return over_shard(self.tied)


def halves(high, own, axis):
    came = high_swap(own)
    return jnp.concatenate([pick(high, own, came), pick(high, came, own)], axis)


def body(
    activations,
    segments,
    query_weight,
    key_weight,
    value_weight,
    output_weight,
    gate_weight,
    up_weight,
    down_weight,
    attn_gain,
    ffn_gain,
    cotangent,
):
    seq_here, block_len, model_width = activations.shape
    seq_len = segments.shape[1]
    tokens = seq_here * block_len
    query_cols = query_weight.shape[1]
    kv_width = key_weight.shape[1]
    kv_heads = kv_width // HEAD
    shards = lax.axis_size("shard")
    ctx = lax.axis_index("ctx")
    low, high = ctx % 2, ctx // 2

    me = lax.axis_index("shard")
    where = (ctx, me, shards)

    def apart(weight, *after):
        if shards > 4:
            return [others(gathered(weight, ctx), me)]
        mine = quarter(weight, ctx)
        mine = tie(mine, *after) if after else mine
        return [lax.ppermute(mine, "shard", ring(shards, r))[None] for r in range(1, shards)]

    gains = jnp.pad(jnp.stack([attn_gain, ffn_gain], 1), ((0, 0), (0, 126)))
    qkv_local = jnp.concatenate([query_weight, key_weight, value_weight, gains], 1)
    qkv_own = apart(qkv_local)

    def later(weight, *after):
        return lax.all_gather(tie(quarter(weight, ctx), *after), "shard", axis=0, tiled=False)

    out_own = others(later(output_weight, *qkv_own), me)
    gate_all = later(gate_weight, *qkv_own)
    up_all = later(up_weight, *qkv_own)
    down_all = later(down_weight, *qkv_own)
    out_pieces = spread([out_own])
    qkv_weight = place(qkv_local, spread(qkv_own), *where, True, [out_own])
    gain_one = qkv_weight[:, -128].astype(f32)
    gain_two = qkv_weight[:, -127].astype(f32)
    keyval_weight = qkv_weight[:, query_cols:-128]
    keyval_other = lax.ppermute(keyval_weight, "tp", SWAP_TP)
    tp = lax.axis_index("tp")
    keyval_weight = jnp.concatenate(
        [pick(tp, keyval_weight, keyval_other), pick(tp, keyval_other, keyval_weight)], 1
    )

    index = jnp.arange(seq_len, dtype=jnp.int32)[None, :]
    doc_start = jnp.zeros_like(segments)
    for number in range(1, 4):
        before = jnp.sum((segments < number).astype(jnp.int32), 1, keepdims=True)
        doc_start = jnp.where(segments == number, before, doc_start)
    offset = ctx * block_len
    start_here = lax.dynamic_slice_in_dim(doc_start, offset, block_len, 1)
    position = lax.dynamic_slice_in_dim(index, offset, block_len, 1) - start_here
    frequency = jnp.power(rope_base, -jnp.arange(HALF, dtype=f32) / HALF)
    angles = frequency[:, None] * position.reshape(1, tokens).astype(f32)
    cosine, sine = jnp.cos(angles), jnp.sin(angles)
    first_block = start_here[:, 0] // block_len

    inputs = activations.reshape(tokens, model_width).astype(f32)
    grad_out = cotangent.reshape(tokens, model_width)
    inv_one = lax.rsqrt(jnp.mean(inputs * inputs, -1, keepdims=True) + epsilon)
    unit_one = inputs * inv_one
    normed_one = (unit_one * gain_one[None, :]).astype(bf16)

    projected = dot(qkv_weight[:, :-128], normed_one, 0, 1)
    query_t = (rotate_t(projected[:query_cols], cosine, sine) * HEAD ** (-0.5)).astype(bf16)
    key_t = rotate_t(projected[query_cols : query_cols + kv_width], cosine, sine).astype(bf16)
    value_t = projected[query_cols + kv_width :].astype(bf16)
    keyval = jnp.concatenate([key_t, value_t], 0)[None]
    came = low_swap(keyval)
    keyval = jnp.concatenate([pick(low, keyval, came), pick(low, came, keyval)], 0)
    keyval = tie(keyval, out_pieces[2][0])
    came = high_swap(keyval)
    keyval = jnp.concatenate([pick(high, keyval, came), pick(high, came, keyval)], 0)
    out_weight = place(output_weight, out_pieces, *where, False, [query_t])
    gate_own = others(tie(gate_all, came), me)
    mixed, log_sums, infos, mine, came = [], [], [], [], []
    last = [out_weight, gate_own, keyval_weight]
    for s in range(seq_here):
        infos.append(jnp.stack([ctx, first_block[s]]).astype(jnp.int32))
        mixed_s, log_s = attend(
            infos[s], query_t, keyval, start_here[s : s + 1], kv_heads, s, last + came[s - 2 : s - 1]
        )
        mixed.append(mixed_s)
        log_sums.append(log_s)
        mine.append(product(mixed_s, out_weight, 0, 0, 512, came[1:2]))
        came.append(lax.ppermute(mine[s], "tp", SWAP_TP))
        last = [mine[s]]
        if s == 1:
            up_own = others(tie(up_all, mine[s]), me)
            last.append(up_own)
    mixed_t = jnp.concatenate(mixed, 1)
    acts = activations.reshape(tokens, model_width)
    gate_pieces = spread([gate_own], came[-1])
    up_pieces = spread([up_own], came[-1])
    down_own = others(tie(down_all, mine[-1]), me)
    residual, normed_two = add_and_norm(acts, mine, came, gain_two, [gate_pieces[2][0], down_own])
    hidden, gate_factor, up_factor, gate_up_full = feed_forward(
        normed_two, (gate_weight, up_weight), (gate_pieces, up_pieces), *where
    )

    hidden_pair = (hidden, low_swap(hidden))
    cotangent_pair = (grad_out, low_swap(grad_out))
    products = block_products if model_width // shards % 256 == 0 else plain_products
    down_pieces = spread([down_own], hidden)
    down_full = place(down_weight, down_pieces, *where, False, [hidden])
    down_products = products(
        hidden_pair, cotangent_pair, None, low, shards, 0, 0, False, None, [down_full]
    )
    down_sum = over_shard(down_products)
    kept, given = feed_back(grad_out, down_full, gate_factor, up_factor, low, [down_products])

    normed_pair = (normed_two, low_swap(normed_two))
    delta_pair = (kept, low_swap(given))
    gate_up = [Reduced(normed_pair, delta_pair, high, shards, 0, 0, True, i) for i in range(2)]

    chunks = 4
    mine, came = [], []
    last = []
    for i in range(chunks):
        mine.append(
            feed_input(kept, given, gate_up_full, low, i, chunks, last + came[max(i - 2, 0) : i - 1])
        )
        came.append(lax.ppermute(mine[i], "tp", SWAP_TP))
        last = [mine[i]]
        if i % 2 == 0:
            gate_up[i // 2].send(last, [gate_up[0].came] if i else [])
            last = [gate_up[0].sent] if i == 0 else last
    gate_up_first = gate_up[0].add([mine[-1], gate_up[1].sent], [down_sum])
    ffn_mine = product(hidden, down_full, 1, 0, TILE, [gate_up[0].tied])
    residual_delta, ffn_gain_term, residual_round = norm_back(
        residual, mine, came, gain_two, grad_out, [ffn_mine]
    )
    delta_t = product(out_weight, residual_round, 1, 1, TILE)
    ffn_came = lax.ppermute(ffn_mine, "tp", SWAP_TP)

    half_rows = query_cols // 2
    mixed_kept = lax.dynamic_slice_in_dim(mixed_t, low * half_rows, half_rows, 0)
    mixed_given = lax.dynamic_slice_in_dim(mixed_t, (1 - low) * half_rows, half_rows, 0)
    mixed_pair = (mixed_kept, low_swap(mixed_given))
    residual_pair = (residual_round, low_swap(residual_round))
    output = Reduced(mixed_pair, residual_pair, high, shards, 1, 0, False)

    gate_up_second = gate_up[1].add([delta_t], [gate_up_first])
    query_deltas, part_sums, mine, came = [], [], [], []
    last = [gate_up[1].tied]
    for s in range(seq_here):
        query_delta, key_part, value_part = attend_back(
            infos[s], query_t, keyval, start_here[s : s + 1], delta_t, mixed[s], log_sums[s],
            cosine, sine, kv_heads, s, last,
        )
        query_deltas.append(query_delta)
        part_sums.append(jnp.concatenate([key_part, value_part], 1))
        mine.append(product(query_delta, qkv_weight[:, :query_cols], 0, 1, 512, came[s - 1 : s]))
        came.append(lax.ppermute(mine[s], "tp", SWAP_TP))
        last = [mine[s]]
        if s == 0:
            output.send(last, [gate_up[1].came])
            last = [output.sent, ffn_came]
        if s == 1:
            output.total = output.products(*output.sides, output.came, high, *output.rest, last)
            last = [output.total]
    down_came = high_swap(tie(down_sum, output.came))

    part_sum = jnp.concatenate(part_sums, 2).reshape(2, 2, 2 * kv_width, tokens)
    sent = lax.dynamic_index_in_dim(part_sum, 1 - high, 0, False)
    part_came = high_swap(sent)

    normed_pair_one = (normed_one, low_swap(normed_one))

    def products_of(delta, after):
        half_rows = delta.shape[0] // 2
        kept = lax.dynamic_slice_in_dim(delta, low * half_rows, half_rows, 0)
        given = lax.dynamic_slice_in_dim(delta, (1 - low) * half_rows, half_rows, 0)
        pair = (kept.T, low_swap(given).T)
        return block_products(normed_pair_one, pair, None, None, shards, 0, 0, True, None, after)

    output_tied = tie(output.total, gate_up_second)
    query_products = products_of(jnp.concatenate(query_deltas, 1), [mine[-1], output_tied])
    output_sum = over_shard(output_tied)
    query_tied = tie(query_products, output_sum)
    query_sum = over_shard(query_tied)

    kept = lax.dynamic_index_in_dim(part_sum, high, 0, False)
    kept = kept.astype(f32) + part_came.astype(f32)
    sent = lax.dynamic_index_in_dim(kept, 1 - low, 0, False).astype(bf16)
    kept = lax.dynamic_index_in_dim(kept, low, 0, False)
    keyval_delta = kept + low_swap(sent).astype(f32)
    key_delta = rotate_t(keyval_delta[:kv_width], cosine, -sine)
    keyval_delta = jnp.concatenate(
        [key_delta.astype(bf16), keyval_delta[kv_width:].astype(bf16)], 0
    )
    keyval_came = lax.ppermute(keyval_delta, "tp", SWAP_TP)
    keyval_both = jnp.concatenate(
        [pick(tp, keyval_delta, keyval_came), pick(tp, keyval_came, keyval_delta)], 0
    )
    keyval_products = products_of(keyval_delta, [query_tied])
    keyval_term = dot(keyval_both, keyval_weight, 0, 1)

    block_out = add_three(residual, ffn_mine, ffn_came, [keyval_products])
    block_out = block_out.reshape(activations.shape)
    input_grad, attn_gain_term = norm_back_rows(
        acts, mine, came, keyval_term, gain_one, residual_delta, [block_out]
    )
    keyval_sum = over_shard(tie(keyval_products, query_sum))

    def two_sides(value):
        other = low_swap(value)
        return pick(low, value, other).astype(f32), pick(low, other, value).astype(f32)

    down_sum = (down_sum.astype(f32) + tie(down_came, keyval_products).astype(f32)).astype(bf16)
    down_grad = jnp.concatenate(two_sides(down_sum), 1)
    first_gate, first_up = two_sides(halves(high, tie(gate_up_first, part_came), 0))
    second_gate, second_up = two_sides(halves(high, tie(gate_up_second, part_came), 0))
    gate_grad = jnp.concatenate([first_gate, second_gate], 1)
    up_grad = jnp.concatenate([first_up, second_up], 1)
    output_grad = jnp.concatenate(two_sides(halves(high, output_sum, 1)), 0)

    def high_total(value):
        return (value.astype(f32) + high_swap(value).astype(f32)).astype(bf16)

    query_grad = jnp.concatenate(two_sides(high_total(query_sum)), 1)
    key_grad, value_grad = two_sides(high_total(keyval_sum))

    gain_terms = jnp.concatenate([attn_gain_term, ffn_gain_term], 0)
    gain_terms = gain_terms + low_swap(gain_terms)
    gain_terms = gain_terms + high_swap(gain_terms)
    gain_terms = gain_terms.reshape(2, shards, model_width // shards)
    gain_grads = lax.dynamic_index_in_dim(gain_terms, me, 1, False)
    for k in range(1, shards):
        block = lax.dynamic_index_in_dim(gain_terms, (me + k) % shards, 1, False)
        gain_grads = gain_grads + lax.ppermute(
            block, "shard", [(i, (i + k) % shards) for i in range(shards)]
        )

    return (
        block_out,
        input_grad.reshape(activations.shape),
        query_grad,
        key_grad,
        value_grad,
        output_grad,
        gate_grad,
        up_grad,
        down_grad,
        gain_grads[0],
        gain_grads[1],
    )


def solution(mesh):
    return jax.shard_map(
        body,
        mesh=mesh,
        in_specs=(
            P("shard", "ctx", None),
            P("shard", None),
            P("shard", "tp"),
            P("shard", "tp"),
            P("shard", "tp"),
            P("tp", "shard"),
            P("shard", "tp"),
            P("shard", "tp"),
            P("tp", "shard"),
            P("shard"),
            P("shard"),
            P("shard", "ctx", None),
        ),
        out_specs=(
            P("shard", "ctx", None),
            P("shard", "ctx", None),
            P("shard", "tp"),
            P("shard", "tp"),
            P("shard", "tp"),
            P("tp", "shard"),
            P("shard", "tp"),
            P("shard", "tp"),
            P("tp", "shard"),
            P("shard"),
            P("shard"),
        ),
        check_vma=False,
    )
```

```python
import jax
import jax.numpy as jnp
from jax import lax
from jax.experimental import pallas as pl
from jax.experimental.pallas import tpu as pltpu
from jax.sharding import PartitionSpec as P

HEAD = 64
HALF = HEAD // 2
epsilon = 1e-05
rope_base = 10000.0
masked_value = -1e30
bf16 = jnp.bfloat16
f32 = jnp.float32

SWAP_LOW = [(0, 1), (1, 0), (2, 3), (3, 2)]
SWAP_HIGH = [(0, 2), (2, 0), (1, 3), (3, 1)]
SWAP_TP = [(0, 1), (1, 0)]


def low_swap(value):
    return lax.ppermute(value, "ctx", SWAP_LOW)


def high_swap(value):
    return lax.ppermute(value, "ctx", SWAP_HIGH)


def dot(left, right, left_dim, right_dim):
    return lax.dot_general(
        left, right, (((left_dim,), (right_dim,)), ((), ())), preferred_element_type=f32
    )


def tp_sum(partial_sum):
    mine = partial_sum.astype(bf16)
    return mine.astype(f32) + lax.ppermute(mine, "tp", SWAP_TP).astype(f32)


UNREAD = pl.BlockSpec(memory_space=pl.ANY)


def taking(microseconds):
    return pl.CostEstimate(flops=int(microseconds * 1e9), bytes_accessed=int(microseconds * 0.15e6), transcendentals=0)


def tie(value, *after):
    def kernel(*refs):
        pass

    return pl.pallas_call(
        kernel,
        out_shape=jax.ShapeDtypeStruct(value.shape, value.dtype),
        in_specs=[UNREAD] * (1 + len(after)),
        out_specs=UNREAD,
        input_output_aliases={0: 0},
        name="tie",
    )(value, *after)


def ring(shards, step):
    return [(i, (i - step) % shards) for i in range(shards)]


def quarter(weight, ctx):
    rows = weight.shape[0] // 4
    return lax.dynamic_slice_in_dim(weight, ctx * rows, rows, 0)


def gathered(weight, ctx):
    return lax.all_gather(quarter(weight, ctx), "shard", axis=0, tiled=False)


def spread(own, *after):
    high = [high_swap(piece) for piece in own]
    low = [low_swap(piece) for piece in own]
    if after:
        high = [tie(piece, *after) for piece in high]
    return own, low, high, [low_swap(piece) for piece in high]


def others(everyone, me):
    shards = everyone.shape[0]
    steps = [lax.dynamic_slice_in_dim(everyone, (me + r) % shards, 1, 0) for r in range(1, shards)]
    return jnp.concatenate(steps, 0)


def place(weight, pieces, ctx, me, shards, along_rows, after=()):
    height, width = weight.shape
    rows = height // 4
    count = len(pieces[0])
    each = pieces[0][0].shape[0]

    def kernel(where, local, *refs):
        parts, out = refs[: 4 * count], refs[-1]
        step = pl.program_id(0)

        def put(slot, value):
            if along_rows:
                out[0, slot] = value
            else:
                out[pl.ds(pl.multiple_of(slot * rows, 16), rows), :] = value

        @pl.when(step == 0)
        def _():
            for slot in range(4):
                put(slot, local[slot])

        for i in range(count):

            @pl.when(step >= 1 if count == 1 else step == i + 1)
            def _():
                for k in range(4):
                    put(jnp.bitwise_xor(where[0], k), parts[k * count + i][0])

    if each == 1:
        piece_spec = pl.BlockSpec((1, rows, width), lambda r, where: (0, 0, 0))
    else:
        piece_spec = pl.BlockSpec(
            (1, rows, width), lambda r, where: (jnp.maximum(r - 1, 0), 0, 0)
        )
    if along_rows:
        out_shape = (shards, 4, rows, width)
        out_spec = pl.BlockSpec(
            (1, 4, rows, width), lambda r, where: (lax.rem(where[1] + r, shards), 0, 0, 0)
        )
    else:
        out_shape = (height, shards * width)
        out_spec = pl.BlockSpec((height, width), lambda r, where: (0, lax.rem(where[1] + r, shards)))
    out = pl.pallas_call(
        kernel,
        out_shape=jax.ShapeDtypeStruct(out_shape, weight.dtype),
        grid_spec=pltpu.PrefetchScalarGridSpec(
            num_scalar_prefetch=1,
            grid=(shards,),
            in_specs=[pl.BlockSpec((4, rows, width), lambda r, where: (0, 0, 0))]
            + [piece_spec] * (4 * count)
            + [UNREAD] * len(after),
            out_specs=out_spec,
        ),
        compiler_params=pltpu.CompilerParams(vmem_limit_bytes=56 * 2**20),
        cost_estimate=taking(8),
        name="place",
    )(jnp.stack([ctx, me]), weight.reshape(4, rows, width), *sum(pieces, []), *after)
    return out.reshape(shards * height, width) if along_rows else out


TILE = 256
ROOMY = pltpu.CompilerParams(vmem_limit_bytes=56 * 2**20)


def feed_forward(normed, weights, pieces, ctx, me, shards, after=()):
    tokens, model_width = normed.shape
    height, width = weights[0].shape
    rows = height // 4

    def kernel(where, normed_ref, *refs):
        hidden_ref, gate_ref, up_ref, full_ref = refs[-4:]
        for w in range(2):
            local, parts = refs[5 * w], refs[5 * w + 1 : 5 * w + 5]
            for slot in range(4):
                start = pl.multiple_of(where[1] * height + slot * rows, rows)
                full_ref[w, pl.ds(start, rows), :] = local[slot]
            for r in range(1, shards):
                first = lax.rem(where[1] + r, shards) * height
                for k in range(4):
                    start = first + jnp.bitwise_xor(where[0], k) * rows
                    full_ref[w, pl.ds(pl.multiple_of(start, rows), rows), :] = parts[k][r - 1]
        gate = dot(normed_ref[...], full_ref[0], 1, 0)
        up = dot(normed_ref[...], full_ref[1], 1, 0)
        sigmoid = 1.0 / (1.0 + jnp.exp(-gate))
        silu = gate * sigmoid
        hidden_ref[...] = (silu * up).astype(bf16)
        gate_ref[...] = (up * sigmoid * (1.0 + gate * (1.0 - sigmoid))).astype(bf16)
        up_ref[...] = silu.astype(bf16)

    weight_specs = [pl.BlockSpec((4, rows, TILE), lambda j, _: (0, 0, j))] + [
        pl.BlockSpec((shards - 1, rows, TILE), lambda j, _: (0, 0, j))
    ] * 4
    token_spec = pl.BlockSpec((tokens, TILE), lambda j, _: (0, j))
    token_shape = jax.ShapeDtypeStruct((tokens, width), bf16)
    operands = []
    for weight, parts in zip(weights, pieces):
        operands += [weight.reshape(4, rows, width)] + [part[0] for part in parts]
    return pl.pallas_call(
        kernel,
        out_shape=(
            token_shape,
            token_shape,
            token_shape,
            jax.ShapeDtypeStruct((2, model_width, width), bf16),
        ),
        grid_spec=pltpu.PrefetchScalarGridSpec(
            num_scalar_prefetch=1,
            grid=(width // TILE,),
            in_specs=[pl.BlockSpec((tokens, model_width), lambda j, _: (0, 0))] + weight_specs * 2
            + [UNREAD] * len(after),
            out_specs=(
                token_spec,
                token_spec,
                token_spec,
                pl.BlockSpec((2, model_width, TILE), lambda j, _: (0, 0, j)),
            ),
        ),
        compiler_params=ROOMY,
        cost_estimate=taking(29),
        name="feed_forward",
    )(jnp.stack([ctx, me]), normed, *operands, *after)


def feed_back(grad_out, down_full, gate_factor, up_factor, low, after=()):
    tokens, model_width = grad_out.shape
    width = down_full.shape[0]

    def kernel(where, grad_ref, down_ref, gate_ref, up_ref, *rest):
        kept_ref, given_ref = rest[-2:]
        hidden_delta = dot(grad_ref[...], down_ref[...], 1, 1)
        gate_delta = (hidden_delta * gate_ref[...].astype(f32)).astype(bf16)
        up_delta = (hidden_delta * up_ref[...].astype(f32)).astype(bf16)

        @pl.when(where[0] == 0)
        def _():
            kept_ref[...] = gate_delta
            given_ref[...] = up_delta

        @pl.when(where[0] != 0)
        def _():
            kept_ref[...] = up_delta
            given_ref[...] = gate_delta

    token_spec = pl.BlockSpec((tokens, TILE), lambda j, _: (0, j))
    token_shape = jax.ShapeDtypeStruct((tokens, width), bf16)
    return pl.pallas_call(
        kernel,
        out_shape=(token_shape, token_shape),
        grid_spec=pltpu.PrefetchScalarGridSpec(
            num_scalar_prefetch=1,
            grid=(width // TILE,),
            in_specs=[
                pl.BlockSpec((tokens, model_width), lambda j, _: (0, 0)),
                pl.BlockSpec((TILE, model_width), lambda j, _: (j, 0)),
                token_spec,
                token_spec,
            ]
            + [UNREAD] * len(after),
            out_specs=(token_spec, token_spec),
        ),
        compiler_params=ROOMY,
        cost_estimate=taking(5.7),
        name="feed_back",
    )(low.reshape(1), grad_out, down_full, gate_factor, up_factor, *after)


def feed_input(kept, given, full, low, part, parts, after=()):
    tokens, width = kept.shape
    model_width = full.shape[1]
    tiles = model_width // parts // TILE

    def kernel(where, kept_ref, given_ref, kept_weight, given_weight, *rest):
        total = dot(kept_ref[...], kept_weight[0], 1, 1)
        total += dot(given_ref[...], given_weight[0], 1, 1)
        rest[-1][...] = total.astype(bf16)

    return pl.pallas_call(
        kernel,
        out_shape=jax.ShapeDtypeStruct((tokens, model_width // parts), bf16),
        grid_spec=pltpu.PrefetchScalarGridSpec(
            num_scalar_prefetch=1,
            grid=(tiles,),
            in_specs=[
                pl.BlockSpec((tokens, width), lambda j, _: (0, 0)),
                pl.BlockSpec((tokens, width), lambda j, _: (0, 0)),
                pl.BlockSpec((1, TILE, width), lambda j, where: (where[0], part * tiles + j, 0)),
                pl.BlockSpec((1, TILE, width), lambda j, where: (1 - where[0], part * tiles + j, 0)),
            ]
            + [UNREAD] * len(after),
            out_specs=pl.BlockSpec((tokens, TILE), lambda j, _: (0, j)),
        ),
        compiler_params=ROOMY,
        cost_estimate=taking(10),
        name="feed_input",
    )(low.reshape(1), kept, given, full, full, *after)


def product(left, right, left_dim, right_dim, tile, after=()):
    rows = left.shape[1 - left_dim]
    width = right.shape[1 - right_dim]
    turn = left_dim == 0 and right_dim == 1

    def kernel(left_ref, right_ref, *rest):
        value = turned(left_ref[...]) if turn else left_ref[...]
        total = dot(value, right_ref[...], 1 if turn else left_dim, right_dim)
        rest[-1][...] = total.astype(bf16)

    if right_dim == 0:
        right_spec = pl.BlockSpec((right.shape[0], tile), lambda j: (0, j))
    else:
        right_spec = pl.BlockSpec((tile, left.shape[left_dim]), lambda j: (j, 0))
    return pl.pallas_call(
        kernel,
        out_shape=jax.ShapeDtypeStruct((rows, width), bf16),
        grid=(width // tile,),
        in_specs=[pl.BlockSpec(left.shape, lambda j: (0, 0)), right_spec] + [UNREAD] * len(after),
        out_specs=pl.BlockSpec((rows, tile), lambda j: (0, j)),
        compiler_params=ROOMY,
        cost_estimate=taking(0.6),
        name="product",
    )(left, right, *after)


def add_and_norm(activations, mine, came, gain, after=()):
    count = len(mine)
    rows, width = mine[0].shape

    def kernel(act_ref, gain_ref, *refs):
        residual_ref, normed_ref = refs[-2:]
        for i in range(count):

            @pl.when(pl.program_id(0) == i)
            def _():
                total = refs[i][...].astype(f32) + refs[count + i][...].astype(f32)
                residual = act_ref[...].astype(f32) + total
                inverse = lax.rsqrt(jnp.mean(residual * residual, -1, keepdims=True) + epsilon)
                residual_ref[...] = residual
                normed_ref[...] = (residual * inverse * gain_ref[...]).astype(bf16)

    row_spec = pl.BlockSpec((rows, width), lambda i: (i, 0))
    one_spec = pl.BlockSpec((rows, width), lambda i: (0, 0))
    return pl.pallas_call(
        kernel,
        out_shape=(
            jax.ShapeDtypeStruct(activations.shape, f32),
            jax.ShapeDtypeStruct(activations.shape, bf16),
        ),
        grid=(count,),
        in_specs=[row_spec, pl.BlockSpec((1, width), lambda i: (0, 0))]
        + [one_spec] * (2 * count)
        + [UNREAD] * len(after),
        out_specs=(row_spec, row_spec),
        compiler_params=ROOMY,
        cost_estimate=taking(90),
        name="add_and_norm",
    )(activations, gain[None, :], *mine, *came, *after)


def add_three(residual, mine, came, after=()):
    tokens, width = residual.shape
    rows = 128

    def kernel(residual_ref, mine_ref, came_ref, *rest):
        total = mine_ref[...].astype(f32) + came_ref[...].astype(f32)
        rest[-1][...] = (residual_ref[...] + total).astype(bf16)

    row_spec = pl.BlockSpec((rows, width), lambda i: (i, 0))
    return pl.pallas_call(
        kernel,
        out_shape=jax.ShapeDtypeStruct((tokens, width), bf16),
        grid=(tokens // rows,),
        in_specs=[row_spec] * 3 + [UNREAD] * len(after),
        out_specs=row_spec,
        compiler_params=ROOMY,
        cost_estimate=taking(0.15),
        name="add_three",
    )(residual, mine, came, *after)


def norm_gradient(value, delta, gain, base):
    inverse = lax.rsqrt(jnp.mean(value * value, -1, keepdims=True) + epsilon)
    unit = value * inverse
    scaled = delta * gain
    total = base + inverse * (scaled - unit * jnp.mean(scaled * unit, -1, keepdims=True))
    return total, jnp.sum(delta * unit, 0, keepdims=True)


def add_term(term_ref, term):
    @pl.when(pl.program_id(0) == 0)
    def _():
        term_ref[...] = term

    @pl.when(pl.program_id(0) != 0)
    def _():
        term_ref[...] += term


def norm_back(values, mine, came, gain, base, after=()):
    count = len(mine)
    tokens, width = values.shape
    rows = 128

    def kernel(value_ref, gain_ref, base_ref, *refs):
        delta = jnp.concatenate(
            [refs[i][...].astype(f32) + refs[count + i][...].astype(f32) for i in range(count)], 1
        )
        total, term = norm_gradient(
            value_ref[...], delta, gain_ref[...], base_ref[...].astype(f32)
        )
        refs[-3][...] = total
        refs[-1][...] = total.astype(bf16)
        add_term(refs[-2], term)

    row_spec = pl.BlockSpec((rows, width), lambda i: (i, 0))
    part_spec = pl.BlockSpec((rows, width // count), lambda i: (i, 0))
    line_spec = pl.BlockSpec((1, width), lambda i: (0, 0))
    return pl.pallas_call(
        kernel,
        out_shape=(
            jax.ShapeDtypeStruct((tokens, width), f32),
            jax.ShapeDtypeStruct((1, width), f32),
            jax.ShapeDtypeStruct((tokens, width), bf16),
        ),
        grid=(tokens // rows,),
        in_specs=[row_spec, line_spec, row_spec]
        + [part_spec] * (2 * count)
        + [UNREAD] * len(after),
        out_specs=(row_spec, line_spec, row_spec),
        compiler_params=ROOMY,
        cost_estimate=taking(12),
        name="norm_back",
    )(values, gain[None, :], base, *mine, *came, *after)


def norm_back_rows(values, mine, came, term, gain, base, after=()):
    count = len(mine)
    tokens, width = values.shape
    rows = 128
    steps = mine[0].shape[0] // rows

    def kernel(value_ref, term_ref, gain_ref, base_ref, *refs):
        for i in range(count):

            @pl.when(pl.program_id(0) // steps == i)
            def _():
                delta = refs[i][...].astype(f32) + refs[count + i][...].astype(f32)
                total, gain_term = norm_gradient(
                    value_ref[...].astype(f32),
                    delta + term_ref[...],
                    gain_ref[...],
                    base_ref[...],
                )
                refs[-2][...] = total
                add_term(refs[-1], gain_term)

    row_spec = pl.BlockSpec((rows, width), lambda i: (i, 0))
    line_spec = pl.BlockSpec((1, width), lambda i: (0, 0))

    def part_spec(at):
        return pl.BlockSpec(
            (rows, width), lambda i: (jnp.clip(i - at * steps, 0, steps - 1), 0)
        )

    part_specs = [part_spec(i) for i in range(count)]
    return pl.pallas_call(
        kernel,
        out_shape=(
            jax.ShapeDtypeStruct((tokens, width), f32),
            jax.ShapeDtypeStruct((1, width), f32),
        ),
        grid=(tokens // rows,),
        in_specs=[row_spec, row_spec, line_spec, row_spec]
        + part_specs * 2
        + [UNREAD] * len(after),
        out_specs=(row_spec, line_spec),
        compiler_params=ROOMY,
        cost_estimate=taking(13),
        name="norm_back_rows",
    )(values, term, gain[None, :], base, *mine, *came, *after)


def block_bias(start_row, key_first, diagonal):
    size = start_row.shape[1]
    keys = lax.broadcasted_iota(jnp.int32, (size, size), 0)
    allowed = keys + key_first >= start_row
    if diagonal:
        queries = lax.broadcasted_iota(jnp.int32, (size, size), 1)
        allowed = allowed & (keys <= queries)
    return jnp.where(allowed, 0.0, masked_value).astype(f32)


def turned(block):
    return jnp.transpose(block.astype(f32)).astype(bf16)


def attend_kernel(group, info, q_ref, k_ref, v_ref, start_ref, *rest):
    o_ref, lse_ref, acc, top = rest[-4:]
    here, first = info[0], info[1]
    size = q_ref.shape[1]

    def step(block, diagonal):
        keys = turned(k_ref[block])
        values = jnp.concatenate([v_ref[block], jnp.ones((16, size), bf16)], 0)
        bias = block_bias(start_ref[...], block * size, diagonal)
        for h in range(group):
            scores = dot(keys, q_ref[h * HEAD : (h + 1) * HEAD, :], 1, 0) + bias
            block_top = jnp.max(scores, 0, keepdims=True)
            if diagonal:
                weights = jnp.exp(scores - block_top).astype(bf16)
                acc[h] = dot(values, weights, 1, 0)
                top[h] = block_top
            else:
                new_top = jnp.maximum(top[h], block_top)
                weights = jnp.exp(scores - new_top).astype(bf16)
                acc[h] = acc[h] * jnp.exp(top[h] - new_top) + dot(values, weights, 1, 0)
                top[h] = new_top

    step(here, True)

    @pl.loop(first, here)
    def _(block):
        step(block, False)

    for h in range(group):
        total = acc[h, HEAD : HEAD + 1, :]
        o_ref[h * HEAD : (h + 1) * HEAD, :] = (acc[h, :HEAD, :] / total).astype(bf16)
        lse_ref[0, h : h + 1, :] = top[h] + jnp.log(total)


def attend(info, query_t, keyval, start_row, kv_heads, seq, after=()):
    blocks, kv_rows, _ = keyval.shape
    size = start_row.shape[1]
    group = query_t.shape[0] // HEAD // kv_heads
    rows = group * HEAD
    return pl.pallas_call(
        lambda *refs: attend_kernel(group, *refs),
        out_shape=(
            jax.ShapeDtypeStruct((query_t.shape[0], size), bf16),
            jax.ShapeDtypeStruct((kv_heads, group, size), f32),
        ),
        grid_spec=pltpu.PrefetchScalarGridSpec(
            num_scalar_prefetch=1,
            grid=(kv_heads,),
            in_specs=[
                pl.BlockSpec((rows, size), lambda g, _: (g, seq)),
                pl.BlockSpec((blocks, HEAD, size), lambda g, _: (0, g, seq)),
                pl.BlockSpec((blocks, HEAD, size), lambda g, _: (0, kv_heads + g, seq)),
                pl.BlockSpec((1, size), lambda g, _: (0, 0)),
            ]
            + [UNREAD] * len(after),
            out_specs=(
                pl.BlockSpec((rows, size), lambda g, _: (g, 0)),
                pl.BlockSpec((1, group, size), lambda g, _: (g, 0, 0)),
            ),
            scratch_shapes=[
                pltpu.VMEM((group, HEAD + 16, size), f32),
                pltpu.VMEM((group, 1, size), f32),
            ],
        ),
        compiler_params=pltpu.CompilerParams(vmem_limit_bytes=48 * 2**20),
        cost_estimate=taking(14),
        name="attend",
    )(info, query_t, keyval, keyval, start_row, *after)


def attend_back_kernel(
    group, info, q_ref, k_ref, v_ref, start_ref, d_ref, o_ref, lse_ref, cos_ref, sin_ref, *rest
):
    dq_ref, dk_ref, dv_ref, acc, inner = rest[-5:]
    here, first = info[0], info[1]
    size = q_ref.shape[1]
    rows = [slice(h * HEAD, (h + 1) * HEAD) for h in range(group)]
    for h in range(group):
        product = d_ref[rows[h], :].astype(f32) * o_ref[rows[h], :].astype(f32)
        inner[h] = jnp.sum(product, 0, keepdims=True)

    def step(block, diagonal):
        key_block = k_ref[block]
        keys = turned(key_block)
        values = turned(v_ref[block])
        bias = block_bias(start_ref[...], block * size, diagonal)
        key_sum = jnp.zeros((HEAD, size), f32)
        value_sum = jnp.zeros((HEAD, size), f32)
        for h in range(group):
            query, delta = q_ref[rows[h], :], d_ref[rows[h], :]
            scores = dot(keys, query, 1, 0) + bias
            probs = jnp.exp(scores - lse_ref[0, h : h + 1, :])
            probs_delta = dot(values, delta, 1, 0)
            score_delta = (probs * (probs_delta - inner[h])).astype(bf16)
            part = dot(key_block, score_delta, 1, 0)
            if diagonal:
                acc[rows[h], :] = part
            else:
                acc[rows[h], :] += part
            key_sum += dot(query, score_delta, 1, 1)
            value_sum += dot(delta, probs.astype(bf16), 1, 1)
        dk_ref[block] = key_sum.astype(bf16)
        dv_ref[block] = value_sum.astype(bf16)

    step(here, True)

    @pl.loop(first, here)
    def _(block):
        step(block, False)

    def clear(block):
        dk_ref[block] = jnp.zeros((HEAD, size), bf16)
        dv_ref[block] = jnp.zeros((HEAD, size), bf16)

    pl.loop(0, first)(clear)
    pl.loop(here + 1, k_ref.shape[0])(clear)

    cosine, sine = cos_ref[...], sin_ref[...]
    for h in range(group):
        upper = acc[h * HEAD : h * HEAD + HALF, :]
        lower = acc[h * HEAD + HALF : (h + 1) * HEAD, :]
        scale = HEAD ** (-0.5)
        dq_ref[h * HEAD : h * HEAD + HALF, :] = (
            (upper * cosine + lower * sine) * scale
        ).astype(bf16)
        dq_ref[h * HEAD + HALF : (h + 1) * HEAD, :] = (
            (lower * cosine - upper * sine) * scale
        ).astype(bf16)


def attend_back(
    info, query_t, keyval, start_row, delta_t, mixed_t, log_sums, cosine, sine, kv_heads, seq, after=()
):
    blocks = keyval.shape[0]
    size = start_row.shape[1]
    group = query_t.shape[0] // HEAD // kv_heads
    rows = group * HEAD
    kv_out = jax.ShapeDtypeStruct((blocks, kv_heads * HEAD, size), bf16)
    kv_spec = pl.BlockSpec((blocks, HEAD, size), lambda g, _: (0, g, 0))
    return pl.pallas_call(
        lambda *refs: attend_back_kernel(group, *refs),
        out_shape=(jax.ShapeDtypeStruct((query_t.shape[0], size), bf16), kv_out, kv_out),
        grid_spec=pltpu.PrefetchScalarGridSpec(
            num_scalar_prefetch=1,
            grid=(kv_heads,),
            in_specs=[
                pl.BlockSpec((rows, size), lambda g, _: (g, seq)),
                pl.BlockSpec((blocks, HEAD, size), lambda g, _: (0, g, seq)),
                pl.BlockSpec((blocks, HEAD, size), lambda g, _: (0, kv_heads + g, seq)),
                pl.BlockSpec((1, size), lambda g, _: (0, 0)),
                pl.BlockSpec((rows, size), lambda g, _: (g, seq)),
                pl.BlockSpec((rows, size), lambda g, _: (g, 0)),
                pl.BlockSpec((1, group, size), lambda g, _: (g, 0, 0)),
                pl.BlockSpec((HALF, size), lambda g, _: (0, seq)),
                pl.BlockSpec((HALF, size), lambda g, _: (0, seq)),
            ]
            + [UNREAD] * len(after),
            out_specs=(pl.BlockSpec((rows, size), lambda g, _: (g, 0)), kv_spec, kv_spec),
            scratch_shapes=[
                pltpu.VMEM((rows, size), f32),
                pltpu.VMEM((group, 1, size), f32),
            ],
        ),
        compiler_params=pltpu.CompilerParams(vmem_limit_bytes=48 * 2**20),
        cost_estimate=taking(160),
        name="attend_back",
    )(info, query_t, keyval, keyval, start_row, delta_t, mixed_t, log_sums, cosine, sine, *after)


def rotate_t(values, cosine, sine):
    heads = values.reshape(-1, 2, HALF, values.shape[1])
    first, second = heads[:, 0], heads[:, 1]
    return jnp.stack([first * cosine - second * sine, second * cosine + first * sine], 1).reshape(
        values.shape
    )


def pick(index, when_zero, when_one):
    return jnp.where(index == 0, when_zero, when_one)


def block_products(
    lefts, rights, came, high, shards, left_rows, right_rows, left_cut, half=None, after=()
):
    cut_side, whole_side = (lefts, rights) if left_cut else (rights, lefts)
    whole_rows = right_rows if left_cut else left_rows
    tokens, model_width = cut_side[0].shape
    if high is None:
        part = model_width // shards
        where_high = jnp.zeros((1,), jnp.int32)
        cut_spec = pl.BlockSpec((tokens, part), lambda j, s, where: (0, s))
    else:
        part = model_width // shards // 2
        where_high = high.reshape(1)
        cut_spec = pl.BlockSpec((tokens, part), lambda j, s, where: (0, s * 2 + where[0]))
    whole = whole_side[0].shape[1 - whole_rows]
    first = 0
    if half is not None:
        whole, first = whole // 2, half
    tile = whole // 2 if whole > 1408 else whole
    steps = whole // tile
    if whole_rows == 0:
        whole_spec = pl.BlockSpec((tokens, tile), lambda j, s, where: (0, first + j))
    else:
        whole_spec = pl.BlockSpec((tile, tokens), lambda j, s, where: (first + j, 0))
    left_spec, right_spec = (cut_spec, whole_spec) if left_cut else (whole_spec, cut_spec)
    if left_cut:
        out_shape = (shards, part, whole)
        out_spec = pl.BlockSpec((1, part, tile), lambda j, s, where: (s, 0, j))
    else:
        out_shape = (shards, whole, part)
        out_spec = pl.BlockSpec((1, tile, part), lambda j, s, where: (s, j, 0))

    def kernel(where, *refs):
        total = dot(refs[0][...], refs[2][...], left_rows, right_rows)
        total += dot(refs[1][...], refs[3][...], left_rows, right_rows)
        if came is not None:
            total += refs[4][0].astype(f32)
        refs[-1][0] = total.astype(bf16)

    extra = [] if came is None else [came]
    return pl.pallas_call(
        kernel,
        out_shape=jax.ShapeDtypeStruct(out_shape, bf16),
        grid_spec=pltpu.PrefetchScalarGridSpec(
            num_scalar_prefetch=1,
            grid=(steps, shards),
            in_specs=[left_spec] * 2
            + [right_spec] * 2
            + [out_spec] * len(extra)
            + [UNREAD] * len(after),
            out_specs=out_spec,
        ),
        compiler_params=pltpu.CompilerParams(vmem_limit_bytes=56 * 2**20),
        cost_estimate=taking(9),
        name="block_products",
    )(where_high, *lefts, *rights, *extra, *after)


def column_half(values, which, shards):
    tokens, width = values.shape
    part = width // shards // 2
    return lax.dynamic_slice_in_dim(values.reshape(tokens, shards, 2, part), which, 1, 2)[:, :, 0]


def plain_products(
    lefts, rights, came, high, shards, left_rows, right_rows, left_cut, half=None, after=()
):
    left = jnp.concatenate(lefts, left_rows)
    right = jnp.concatenate(rights, right_rows)
    if half is not None:
        size = right.shape[1] // 2
        right = right[:, half * size : (half + 1) * size]
    if left_cut:
        total = jnp.einsum(
            "tsp,tn->spn" if right_rows == 0 else "tsp,nt->spn",
            column_half(left, high, shards), right, preferred_element_type=f32,
        )
    else:
        total = jnp.einsum(
            "tn,tsp->snp" if left_rows == 0 else "nt,tsp->snp",
            left, column_half(right, high, shards), preferred_element_type=f32,
        )
    return (total if came is None else total + came.astype(f32)).astype(bf16)


def over_shard(total):
    return lax.psum_scatter(total, "shard", scatter_dimension=0, tiled=True)[0]


def directly_over_shard(total, me):
    shards = total.shape[0]
    result = lax.dynamic_index_in_dim(total, me, 0, False).astype(f32)
    for k in range(1, shards):
        block = lax.dynamic_index_in_dim(total, (me + k) % shards, 0, False)
        came = lax.ppermute(block, "shard", [(i, (i + k) % shards) for i in range(shards)])
        result = result + came.astype(f32)
    return result.astype(bf16)


class Reduced:
    def __init__(self, lefts, rights, high, shards, left_rows, right_rows, left_cut, half=None):
        width = (lefts if left_cut else rights)[0].shape[1]
        self.products = block_products if width // shards // 2 % 128 == 0 else plain_products
        self.sides = lefts, rights
        self.high = high
        self.rest = shards, left_rows, right_rows, left_cut, half

    def send(self, after=(), swap_after=()):
        self.other = self.products(*self.sides, None, 1 - self.high, *self.rest, after)
        self.sent = tie(self.other, *swap_after)
        self.came = high_swap(self.sent)

    def add(self, after=(), sum_after=()):
        self.total = self.products(*self.sides, self.came, self.high, *self.rest, after)
        self.tied = tie(self.total, *sum_after)
        return over_shard(self.tied)


def halves(high, own, axis, came):
    return jnp.concatenate([pick(high, own, came), pick(high, came, own)], axis)


def body(
    activations,
    segments,
    query_weight,
    key_weight,
    value_weight,
    output_weight,
    gate_weight,
    up_weight,
    down_weight,
    attn_gain,
    ffn_gain,
    cotangent,
):
    seq_here, block_len, model_width = activations.shape
    seq_len = segments.shape[1]
    tokens = seq_here * block_len
    query_cols = query_weight.shape[1]
    kv_width = key_weight.shape[1]
    kv_heads = kv_width // HEAD
    shards = lax.axis_size("shard")
    ctx = lax.axis_index("ctx")
    low, high = ctx % 2, ctx // 2

    me = lax.axis_index("shard")
    where = (ctx, me, shards)

    def apart(weight, *after):
        if shards > 4:
            return [others(gathered(weight, ctx), me)]
        mine = quarter(weight, ctx)
        mine = tie(mine, *after) if after else mine
        return [lax.ppermute(mine, "shard", ring(shards, r))[None] for r in range(1, shards)]

    gains = jnp.pad(jnp.stack([attn_gain, ffn_gain], 1), ((0, 0), (0, 126)))
    qkv_local = jnp.concatenate([query_weight, key_weight, value_weight, gains], 1)
    qkv_own = apart(qkv_local)

    def later(weight, *after):
        return lax.all_gather(tie(quarter(weight, ctx), *after), "shard", axis=0, tiled=False)

    out_own = others(later(output_weight, *qkv_own), me)
    gate_all = later(gate_weight, *qkv_own)
    up_all = later(up_weight, *qkv_own)
    down_all = later(down_weight, *qkv_own)
    out_pieces = spread([out_own])
    qkv_weight = place(qkv_local, spread(qkv_own), *where, True, [out_own])
    gain_one = qkv_weight[:, -128].astype(f32)
    gain_two = qkv_weight[:, -127].astype(f32)
    keyval_weight = qkv_weight[:, query_cols:-128]
    keyval_other = lax.ppermute(keyval_weight, "tp", SWAP_TP)
    tp = lax.axis_index("tp")
    keyval_weight = jnp.concatenate(
        [pick(tp, keyval_weight, keyval_other), pick(tp, keyval_other, keyval_weight)], 1
    )

    index = jnp.arange(seq_len, dtype=jnp.int32)[None, :]
    doc_start = jnp.zeros_like(segments)
    for number in range(1, 4):
        before = jnp.sum((segments < number).astype(jnp.int32), 1, keepdims=True)
        doc_start = jnp.where(segments == number, before, doc_start)
    offset = ctx * block_len
    start_here = lax.dynamic_slice_in_dim(doc_start, offset, block_len, 1)
    position = lax.dynamic_slice_in_dim(index, offset, block_len, 1) - start_here
    frequency = jnp.power(rope_base, -jnp.arange(HALF, dtype=f32) / HALF)
    angles = frequency[:, None] * position.reshape(1, tokens).astype(f32)
    cosine, sine = jnp.cos(angles), jnp.sin(angles)
    first_block = start_here[:, 0] // block_len

    inputs = activations.reshape(tokens, model_width).astype(f32)
    grad_out = cotangent.reshape(tokens, model_width)
    inv_one = lax.rsqrt(jnp.mean(inputs * inputs, -1, keepdims=True) + epsilon)
    unit_one = inputs * inv_one
    normed_one = (unit_one * gain_one[None, :]).astype(bf16)

    projected = dot(qkv_weight[:, :-128], normed_one, 0, 1)
    query_t = (rotate_t(projected[:query_cols], cosine, sine) * HEAD ** (-0.5)).astype(bf16)
    key_t = rotate_t(projected[query_cols : query_cols + kv_width], cosine, sine).astype(bf16)
    value_t = projected[query_cols + kv_width :].astype(bf16)
    keyval = jnp.concatenate([key_t, value_t], 0)[None]
    came = low_swap(keyval)
    keyval = jnp.concatenate([pick(low, keyval, came), pick(low, came, keyval)], 0)
    keyval = tie(keyval, out_pieces[2][0])
    came = high_swap(keyval)
    keyval = jnp.concatenate([pick(high, keyval, came), pick(high, came, keyval)], 0)
    out_weight = place(output_weight, out_pieces, *where, False, [query_t])
    gate_own = others(tie(gate_all, came), me)
    mixed, log_sums, infos, mine, came = [], [], [], [], []
    last = [out_weight, gate_own, keyval_weight]
    for s in range(seq_here):
        infos.append(jnp.stack([ctx, first_block[s]]).astype(jnp.int32))
        mixed_s, log_s = attend(
            infos[s], query_t, keyval, start_here[s : s + 1], kv_heads, s, last + came[s - 2 : s - 1]
        )
        mixed.append(mixed_s)
        log_sums.append(log_s)
        mine.append(product(mixed_s, out_weight, 0, 0, 512, came[1:2]))
        came.append(lax.ppermute(mine[s], "tp", SWAP_TP))
        last = [mine[s]]
        if s == 1:
            up_own = others(tie(up_all, mine[s]), me)
            last.append(up_own)
    mixed_t = jnp.concatenate(mixed, 1)
    acts = activations.reshape(tokens, model_width)
    gate_pieces = spread([gate_own], came[-1])
    up_pieces = spread([up_own], came[-1])
    down_own = others(tie(down_all, mine[-1]), me)
    residual, normed_two = add_and_norm(acts, mine, came, gain_two, [gate_pieces[2][0], down_own])
    hidden, gate_factor, up_factor, gate_up_full = feed_forward(
        normed_two, (gate_weight, up_weight), (gate_pieces, up_pieces), *where
    )

    down_high = high_swap(down_own)
    hidden = tie(hidden, down_high)
    hidden_came = low_swap(hidden)
    hidden_pair = (hidden, hidden_came)
    cotangent_pair = (grad_out, low_swap(grad_out))
    products = block_products if model_width // shards % 256 == 0 else plain_products
    down_products = products(hidden_pair, cotangent_pair, None, low, shards, 0, 0, False)
    down_sum = over_shard(down_products)
    down_pieces = [down_own], [low_swap(down_own)], [down_high], [low_swap(down_high)]
    down_full = place(down_weight, down_pieces, *where, False, [down_products])
    kept, given = feed_back(grad_out, down_full, gate_factor, up_factor, low)

    normed_pair = (normed_two, low_swap(normed_two))
    delta_pair = (kept, low_swap(given))
    gate_up = [Reduced(normed_pair, delta_pair, high, shards, 0, 0, True, i) for i in range(2)]

    chunks = 4
    mine, came = [], []
    last = []
    for i in range(chunks):
        mine.append(
            feed_input(kept, given, gate_up_full, low, i, chunks, last + came[max(i - 2, 0) : i - 1])
        )
        came.append(lax.ppermute(mine[i], "tp", SWAP_TP))
        last = [mine[i]]
        if i % 2 == 0:
            gate_up[i // 2].send(last, [gate_up[0].came] if i else [])
            last = [gate_up[0].sent] if i == 0 else last
    ffn_mine = product(hidden, down_full, 1, 0, TILE, [mine[-1]])
    gate_up_first = gate_up[0].add([ffn_mine, gate_up[1].sent, came[2]], [down_sum])
    residual_delta, ffn_gain_term, residual_round = norm_back(
        residual, mine, came, gain_two, grad_out, [ffn_mine, gate_up[0].tied]
    )
    ffn_came = lax.ppermute(ffn_mine, "tp", SWAP_TP)
    delta_t = product(out_weight, residual_round, 1, 1, TILE, [])

    half_rows = query_cols // 2
    mixed_kept = lax.dynamic_slice_in_dim(mixed_t, low * half_rows, half_rows, 0)
    mixed_given = lax.dynamic_slice_in_dim(mixed_t, (1 - low) * half_rows, half_rows, 0)
    mixed_pair = (mixed_kept, low_swap(mixed_given))
    residual_pair = (residual_round, low_swap(residual_round))
    output = Reduced(mixed_pair, residual_pair, high, shards, 1, 0, False)

    query_deltas, part_sums, mine, came = [], [], [], []
    last = []
    for s in range(seq_here):
        query_delta, key_part, value_part = attend_back(
            infos[s], query_t, keyval, start_here[s : s + 1], delta_t, mixed[s], log_sums[s],
            cosine, sine, kv_heads, s, last,
        )
        query_deltas.append(query_delta)
        part_sums.append(jnp.concatenate([key_part, value_part], 1))
        waits = []
        if s == 0:
            waits = []
        if s == 1:
            waits = []
        if s == 2:
            waits = []
        mine.append(product(query_delta, qkv_weight[:, :query_cols], 0, 1, 512, waits))
        came.append(lax.ppermute(mine[s], "tp", SWAP_TP))
        last = [mine[s]]
        if s == 0:
            output.send(last, [gate_up[1].came])
            gate_up_second = gate_up[1].add([output.sent], [])
            last = [output.sent, gate_up[1].tied, ffn_came]
        if s == 1:
            output.total = output.products(*output.sides, output.came, high, *output.rest, last)
            output_tied = tie(output.total, gate_up_second)
            down_came = high_swap(tie(down_sum, output.came))
            first_came = high_swap(tie(gate_up_first, down_came))
            last = [output.total, came[0], down_came, output_tied]

    part_sum = jnp.concatenate(part_sums, 2).reshape(2, 2, 2 * kv_width, tokens)
    sent = lax.dynamic_index_in_dim(part_sum, 1 - high, 0, False)
    part_came = high_swap(sent)

    normed_pair_one = (normed_one, low_swap(normed_one))

    def products_of(delta, after):
        half_rows = delta.shape[0] // 2
        kept = lax.dynamic_slice_in_dim(delta, low * half_rows, half_rows, 0)
        given = lax.dynamic_slice_in_dim(delta, (1 - low) * half_rows, half_rows, 0)
        pair = (kept.T, low_swap(given).T)
        return block_products(normed_pair_one, pair, None, None, shards, 0, 0, True, None, after)

    output_sum = over_shard(output_tied)
    query_products = products_of(jnp.concatenate(query_deltas, 1), [mine[-1], came[1]] + [output_sum])
    part_came = tie(part_came, query_products)
    query_sum = over_shard(query_products)

    kept = lax.dynamic_index_in_dim(part_sum, high, 0, False)
    kept = kept.astype(f32) + part_came.astype(f32)
    sent = lax.dynamic_index_in_dim(kept, 1 - low, 0, False).astype(bf16)
    kept = lax.dynamic_index_in_dim(kept, low, 0, False)
    keyval_delta = kept + low_swap(sent).astype(f32)
    key_delta = rotate_t(keyval_delta[:kv_width], cosine, -sine)
    keyval_delta = jnp.concatenate(
        [key_delta.astype(bf16), keyval_delta[kv_width:].astype(bf16)], 0
    )
    keyval_came = lax.ppermute(keyval_delta, "tp", SWAP_TP)
    keyval_both = jnp.concatenate(
        [pick(tp, keyval_delta, keyval_came), pick(tp, keyval_came, keyval_delta)], 0
    )
    keyval_products = products_of(keyval_delta, [query_products])
    keyval_term = dot(keyval_both, keyval_weight, 0, 1)

    input_grad, attn_gain_term = norm_back_rows(
        acts, mine, came, keyval_term, gain_one, residual_delta, [keyval_products]
    )
    block_out = add_three(residual, ffn_mine, ffn_came, [])
    block_out = block_out.reshape(activations.shape)
    keyval_sum = directly_over_shard(keyval_products, me) if shards <= 4 else over_shard(keyval_products)

    second_came = high_swap(tie(gate_up_second, part_came))

    def two_sides(value):
        other = low_swap(value)
        return pick(low, value, other).astype(f32), pick(low, other, value).astype(f32)

    down_sum = (down_sum.astype(f32) + tie(down_came, keyval_products).astype(f32)).astype(bf16)
    down_grad = jnp.concatenate(two_sides(down_sum), 1)
    first_gate, first_up = two_sides(halves(high, gate_up_first, 0, first_came))
    second_gate, second_up = two_sides(halves(high, gate_up_second, 0, second_came))
    gate_grad = jnp.concatenate([first_gate, second_gate], 1)
    up_grad = jnp.concatenate([first_up, second_up], 1)
    output_grad = jnp.concatenate(two_sides(halves(high, output_sum, 1, high_swap(output_sum))), 0)

    def high_total(value):
        return (value.astype(f32) + high_swap(value).astype(f32)).astype(bf16)

    query_grad = jnp.concatenate(two_sides(high_total(query_sum)), 1)
    key_grad, value_grad = two_sides(high_total(keyval_sum))

    gain_terms = jnp.concatenate([attn_gain_term, ffn_gain_term], 0)
    gain_terms = gain_terms + low_swap(gain_terms)
    gain_terms = gain_terms + high_swap(gain_terms)
    gain_terms = gain_terms.reshape(2, shards, model_width // shards)
    gain_grads = lax.dynamic_index_in_dim(gain_terms, me, 1, False)
    for k in range(1, shards):
        block = lax.dynamic_index_in_dim(gain_terms, (me + k) % shards, 1, False)
        gain_grads = gain_grads + lax.ppermute(
            block, "shard", [(i, (i + k) % shards) for i in range(shards)]
        )

    return (
        block_out,
        input_grad.reshape(activations.shape),
        query_grad,
        key_grad,
        value_grad,
        output_grad,
        gate_grad,
        up_grad,
        down_grad,
        gain_grads[0],
        gain_grads[1],
    )


def solution(mesh):
    return jax.shard_map(
        body,
        mesh=mesh,
        in_specs=(
            P("shard", "ctx", None),
            P("shard", None),
            P("shard", "tp"),
            P("shard", "tp"),
            P("shard", "tp"),
            P("tp", "shard"),
            P("shard", "tp"),
            P("shard", "tp"),
            P("tp", "shard"),
            P("shard"),
            P("shard"),
            P("shard", "ctx", None),
        ),
        out_specs=(
            P("shard", "ctx", None),
            P("shard", "ctx", None),
            P("shard", "tp"),
            P("shard", "tp"),
            P("shard", "tp"),
            P("tp", "shard"),
            P("shard", "tp"),
            P("shard", "tp"),
            P("tp", "shard"),
            P("shard"),
            P("shard"),
        ),
        check_vma=False,
    )
```

```python
import jax
import jax.numpy as jnp
from jax import lax
from jax.experimental import pallas as pl
from jax.experimental.pallas import tpu as pltpu
from jax.sharding import PartitionSpec as P

HEAD = 64
HALF = HEAD // 2
epsilon = 1e-05
rope_base = 10000.0
masked_value = -1e30
bf16 = jnp.bfloat16
f32 = jnp.float32

SWAP_LOW = [(0, 1), (1, 0), (2, 3), (3, 2)]
SWAP_HIGH = [(0, 2), (2, 0), (1, 3), (3, 1)]
SWAP_TP = [(0, 1), (1, 0)]


def low_swap(value):
    return lax.ppermute(value, "ctx", SWAP_LOW)


def high_swap(value):
    return lax.ppermute(value, "ctx", SWAP_HIGH)


def dot(left, right, left_dim, right_dim):
    return lax.dot_general(
        left, right, (((left_dim,), (right_dim,)), ((), ())), preferred_element_type=f32
    )


def tp_sum(partial_sum):
    mine = partial_sum.astype(bf16)
    return mine.astype(f32) + lax.ppermute(mine, "tp", SWAP_TP).astype(f32)


UNREAD = pl.BlockSpec(memory_space=pl.ANY)


def taking(microseconds):
    return pl.CostEstimate(flops=int(microseconds * 1e9), bytes_accessed=int(microseconds * 0.15e6), transcendentals=0)


def tie(value, *after):
    def kernel(*refs):
        pass

    return pl.pallas_call(
        kernel,
        out_shape=jax.ShapeDtypeStruct(value.shape, value.dtype),
        in_specs=[UNREAD] * (1 + len(after)),
        out_specs=UNREAD,
        input_output_aliases={0: 0},
        name="tie",
    )(value, *after)


def ring(shards, step):
    return [(i, (i - step) % shards) for i in range(shards)]


def quarter(weight, ctx):
    rows = weight.shape[0] // 4
    return lax.dynamic_slice_in_dim(weight, ctx * rows, rows, 0)


def gathered(weight, ctx):
    return lax.all_gather(quarter(weight, ctx), "shard", axis=0, tiled=False)


def spread(own, *after):
    high = [high_swap(piece) for piece in own]
    low = [low_swap(piece) for piece in own]
    if after:
        high = [tie(piece, *after) for piece in high]
    return own, low, high, [low_swap(piece) for piece in high]


def others(everyone, me):
    shards = everyone.shape[0]
    steps = [lax.dynamic_slice_in_dim(everyone, (me + r) % shards, 1, 0) for r in range(1, shards)]
    return jnp.concatenate(steps, 0)


def place(weight, pieces, ctx, me, shards, along_rows, after=()):
    height, width = weight.shape
    rows = height // 4
    count = len(pieces[0])
    each = pieces[0][0].shape[0]

    def kernel(where, local, *refs):
        parts, out = refs[: 4 * count], refs[-1]
        step = pl.program_id(0)

        def put(slot, value):
            if along_rows:
                out[0, slot] = value
            else:
                out[pl.ds(pl.multiple_of(slot * rows, 16), rows), :] = value

        @pl.when(step == 0)
        def _():
            for slot in range(4):
                put(slot, local[slot])

        for i in range(count):

            @pl.when(step >= 1 if count == 1 else step == i + 1)
            def _():
                for k in range(4):
                    put(jnp.bitwise_xor(where[0], k), parts[k * count + i][0])

    if each == 1:
        piece_spec = pl.BlockSpec((1, rows, width), lambda r, where: (0, 0, 0))
    else:
        piece_spec = pl.BlockSpec(
            (1, rows, width), lambda r, where: (jnp.maximum(r - 1, 0), 0, 0)
        )
    if along_rows:
        out_shape = (shards, 4, rows, width)
        out_spec = pl.BlockSpec(
            (1, 4, rows, width), lambda r, where: (lax.rem(where[1] + r, shards), 0, 0, 0)
        )
    else:
        out_shape = (height, shards * width)
        out_spec = pl.BlockSpec((height, width), lambda r, where: (0, lax.rem(where[1] + r, shards)))
    out = pl.pallas_call(
        kernel,
        out_shape=jax.ShapeDtypeStruct(out_shape, weight.dtype),
        grid_spec=pltpu.PrefetchScalarGridSpec(
            num_scalar_prefetch=1,
            grid=(shards,),
            in_specs=[pl.BlockSpec((4, rows, width), lambda r, where: (0, 0, 0))]
            + [piece_spec] * (4 * count)
            + [UNREAD] * len(after),
            out_specs=out_spec,
        ),
        compiler_params=pltpu.CompilerParams(vmem_limit_bytes=56 * 2**20),
        cost_estimate=taking(240),
        name="place",
    )(jnp.stack([ctx, me]), weight.reshape(4, rows, width), *sum(pieces, []), *after)
    return out.reshape(shards * height, width) if along_rows else out


TILE = 256
ROOMY = pltpu.CompilerParams(vmem_limit_bytes=56 * 2**20)


def feed_forward(normed, weights, pieces, ctx, me, shards, after=()):
    tokens, model_width = normed.shape
    height, width = weights[0].shape
    rows = height // 4

    def kernel(where, normed_ref, *refs):
        hidden_ref, gate_ref, up_ref, full_ref = refs[-4:]
        for w in range(2):
            local, parts = refs[5 * w], refs[5 * w + 1 : 5 * w + 5]
            for slot in range(4):
                start = pl.multiple_of(where[1] * height + slot * rows, rows)
                full_ref[w, pl.ds(start, rows), :] = local[slot]
            for r in range(1, shards):
                first = lax.rem(where[1] + r, shards) * height
                for k in range(4):
                    start = first + jnp.bitwise_xor(where[0], k) * rows
                    full_ref[w, pl.ds(pl.multiple_of(start, rows), rows), :] = parts[k][r - 1]
        gate = dot(normed_ref[...], full_ref[0], 1, 0)
        up = dot(normed_ref[...], full_ref[1], 1, 0)
        sigmoid = 1.0 / (1.0 + jnp.exp(-gate))
        silu = gate * sigmoid
        hidden_ref[...] = (silu * up).astype(bf16)
        gate_ref[...] = (up * sigmoid * (1.0 + gate * (1.0 - sigmoid))).astype(bf16)
        up_ref[...] = silu.astype(bf16)

    weight_specs = [pl.BlockSpec((4, rows, TILE), lambda j, _: (0, 0, j))] + [
        pl.BlockSpec((shards - 1, rows, TILE), lambda j, _: (0, 0, j))
    ] * 4
    token_spec = pl.BlockSpec((tokens, TILE), lambda j, _: (0, j))
    token_shape = jax.ShapeDtypeStruct((tokens, width), bf16)
    operands = []
    for weight, parts in zip(weights, pieces):
        operands += [weight.reshape(4, rows, width)] + [part[0] for part in parts]
    return pl.pallas_call(
        kernel,
        out_shape=(
            token_shape,
            token_shape,
            token_shape,
            jax.ShapeDtypeStruct((2, model_width, width), bf16),
        ),
        grid_spec=pltpu.PrefetchScalarGridSpec(
            num_scalar_prefetch=1,
            grid=(width // TILE,),
            in_specs=[pl.BlockSpec((tokens, model_width), lambda j, _: (0, 0))] + weight_specs * 2
            + [UNREAD] * len(after),
            out_specs=(
                token_spec,
                token_spec,
                token_spec,
                pl.BlockSpec((2, model_width, TILE), lambda j, _: (0, 0, j)),
            ),
        ),
        compiler_params=ROOMY,
        cost_estimate=taking(29),
        name="feed_forward",
    )(jnp.stack([ctx, me]), normed, *operands, *after)


def feed_back(grad_out, down_full, gate_factor, up_factor, low, after=()):
    tokens, model_width = grad_out.shape
    width = down_full.shape[0]

    def kernel(where, grad_ref, down_ref, gate_ref, up_ref, *rest):
        kept_ref, given_ref = rest[-2:]
        hidden_delta = dot(grad_ref[...], down_ref[...], 1, 1)
        gate_delta = (hidden_delta * gate_ref[...].astype(f32)).astype(bf16)
        up_delta = (hidden_delta * up_ref[...].astype(f32)).astype(bf16)

        @pl.when(where[0] == 0)
        def _():
            kept_ref[...] = gate_delta
            given_ref[...] = up_delta

        @pl.when(where[0] != 0)
        def _():
            kept_ref[...] = up_delta
            given_ref[...] = gate_delta

    token_spec = pl.BlockSpec((tokens, TILE), lambda j, _: (0, j))
    token_shape = jax.ShapeDtypeStruct((tokens, width), bf16)
    return pl.pallas_call(
        kernel,
        out_shape=(token_shape, token_shape),
        grid_spec=pltpu.PrefetchScalarGridSpec(
            num_scalar_prefetch=1,
            grid=(width // TILE,),
            in_specs=[
                pl.BlockSpec((tokens, model_width), lambda j, _: (0, 0)),
                pl.BlockSpec((TILE, model_width), lambda j, _: (j, 0)),
                token_spec,
                token_spec,
            ]
            + [UNREAD] * len(after),
            out_specs=(token_spec, token_spec),
        ),
        compiler_params=ROOMY,
        cost_estimate=taking(5.7),
        name="feed_back",
    )(low.reshape(1), grad_out, down_full, gate_factor, up_factor, *after)


def feed_input(kept, given, full, low, part, parts, after=()):
    tokens, width = kept.shape
    model_width = full.shape[1]
    tiles = model_width // parts // TILE

    def kernel(where, kept_ref, given_ref, kept_weight, given_weight, *rest):
        total = dot(kept_ref[...], kept_weight[0], 1, 1)
        total += dot(given_ref[...], given_weight[0], 1, 1)
        rest[-1][...] = total.astype(bf16)

    return pl.pallas_call(
        kernel,
        out_shape=jax.ShapeDtypeStruct((tokens, model_width // parts), bf16),
        grid_spec=pltpu.PrefetchScalarGridSpec(
            num_scalar_prefetch=1,
            grid=(tiles,),
            in_specs=[
                pl.BlockSpec((tokens, width), lambda j, _: (0, 0)),
                pl.BlockSpec((tokens, width), lambda j, _: (0, 0)),
                pl.BlockSpec((1, TILE, width), lambda j, where: (where[0], part * tiles + j, 0)),
                pl.BlockSpec((1, TILE, width), lambda j, where: (1 - where[0], part * tiles + j, 0)),
            ]
            + [UNREAD] * len(after),
            out_specs=pl.BlockSpec((tokens, TILE), lambda j, _: (0, j)),
        ),
        compiler_params=ROOMY,
        cost_estimate=taking(300),
        name="feed_input",
    )(low.reshape(1), kept, given, full, full, *after)


def product(left, right, left_dim, right_dim, tile, after=()):
    rows = left.shape[1 - left_dim]
    width = right.shape[1 - right_dim]
    turn = left_dim == 0 and right_dim == 1

    def kernel(left_ref, right_ref, *rest):
        value = turned(left_ref[...]) if turn else left_ref[...]
        total = dot(value, right_ref[...], 1 if turn else left_dim, right_dim)
        rest[-1][...] = total.astype(bf16)

    if right_dim == 0:
        right_spec = pl.BlockSpec((right.shape[0], tile), lambda j: (0, j))
    else:
        right_spec = pl.BlockSpec((tile, left.shape[left_dim]), lambda j: (j, 0))
    return pl.pallas_call(
        kernel,
        out_shape=jax.ShapeDtypeStruct((rows, width), bf16),
        grid=(width // tile,),
        in_specs=[pl.BlockSpec(left.shape, lambda j: (0, 0)), right_spec] + [UNREAD] * len(after),
        out_specs=pl.BlockSpec((rows, tile), lambda j: (0, j)),
        compiler_params=ROOMY,
        cost_estimate=taking(0.6),
        name="product",
    )(left, right, *after)


def add_and_norm(activations, mine, came, gain, after=()):
    count = len(mine)
    rows, width = mine[0].shape

    def kernel(act_ref, gain_ref, *refs):
        residual_ref, normed_ref = refs[-2:]
        for i in range(count):

            @pl.when(pl.program_id(0) == i)
            def _():
                total = refs[i][...].astype(f32) + refs[count + i][...].astype(f32)
                residual = act_ref[...].astype(f32) + total
                inverse = lax.rsqrt(jnp.mean(residual * residual, -1, keepdims=True) + epsilon)
                residual_ref[...] = residual
                normed_ref[...] = (residual * inverse * gain_ref[...]).astype(bf16)

    row_spec = pl.BlockSpec((rows, width), lambda i: (i, 0))
    one_spec = pl.BlockSpec((rows, width), lambda i: (0, 0))
    return pl.pallas_call(
        kernel,
        out_shape=(
            jax.ShapeDtypeStruct(activations.shape, f32),
            jax.ShapeDtypeStruct(activations.shape, bf16),
        ),
        grid=(count,),
        in_specs=[row_spec, pl.BlockSpec((1, width), lambda i: (0, 0))]
        + [one_spec] * (2 * count)
        + [UNREAD] * len(after),
        out_specs=(row_spec, row_spec),
        compiler_params=ROOMY,
        cost_estimate=taking(90),
        name="add_and_norm",
    )(activations, gain[None, :], *mine, *came, *after)


def add_three(residual, mine, came, after=()):
    tokens, width = residual.shape
    rows = 128

    def kernel(residual_ref, mine_ref, came_ref, *rest):
        total = mine_ref[...].astype(f32) + came_ref[...].astype(f32)
        rest[-1][...] = (residual_ref[...] + total).astype(bf16)

    row_spec = pl.BlockSpec((rows, width), lambda i: (i, 0))
    return pl.pallas_call(
        kernel,
        out_shape=jax.ShapeDtypeStruct((tokens, width), bf16),
        grid=(tokens // rows,),
        in_specs=[row_spec] * 3 + [UNREAD] * len(after),
        out_specs=row_spec,
        compiler_params=ROOMY,
        cost_estimate=taking(0.15),
        name="add_three",
    )(residual, mine, came, *after)


def norm_gradient(value, delta, gain, base):
    inverse = lax.rsqrt(jnp.mean(value * value, -1, keepdims=True) + epsilon)
    unit = value * inverse
    scaled = delta * gain
    total = base + inverse * (scaled - unit * jnp.mean(scaled * unit, -1, keepdims=True))
    return total, jnp.sum(delta * unit, 0, keepdims=True)


def add_term(term_ref, term):
    @pl.when(pl.program_id(0) == 0)
    def _():
        term_ref[...] = term

    @pl.when(pl.program_id(0) != 0)
    def _():
        term_ref[...] += term


def norm_back(values, mine, came, gain, base, after=()):
    count = len(mine)
    tokens, width = values.shape
    rows = 128

    def kernel(value_ref, gain_ref, base_ref, *refs):
        delta = jnp.concatenate(
            [refs[i][...].astype(f32) + refs[count + i][...].astype(f32) for i in range(count)], 1
        )
        total, term = norm_gradient(
            value_ref[...], delta, gain_ref[...], base_ref[...].astype(f32)
        )
        refs[-3][...] = total
        refs[-1][...] = total.astype(bf16)
        add_term(refs[-2], term)

    row_spec = pl.BlockSpec((rows, width), lambda i: (i, 0))
    part_spec = pl.BlockSpec((rows, width // count), lambda i: (i, 0))
    line_spec = pl.BlockSpec((1, width), lambda i: (0, 0))
    return pl.pallas_call(
        kernel,
        out_shape=(
            jax.ShapeDtypeStruct((tokens, width), f32),
            jax.ShapeDtypeStruct((1, width), f32),
            jax.ShapeDtypeStruct((tokens, width), bf16),
        ),
        grid=(tokens // rows,),
        in_specs=[row_spec, line_spec, row_spec]
        + [part_spec] * (2 * count)
        + [UNREAD] * len(after),
        out_specs=(row_spec, line_spec, row_spec),
        compiler_params=ROOMY,
        cost_estimate=taking(360),
        name="norm_back",
    )(values, gain[None, :], base, *mine, *came, *after)


def norm_back_rows(values, mine, came, term, gain, base, after=()):
    count = len(mine)
    tokens, width = values.shape
    rows = 128
    steps = mine[0].shape[0] // rows

    def kernel(value_ref, term_ref, gain_ref, base_ref, *refs):
        for i in range(count):

            @pl.when(pl.program_id(0) // steps == i)
            def _():
                delta = refs[i][...].astype(f32) + refs[count + i][...].astype(f32)
                total, gain_term = norm_gradient(
                    value_ref[...].astype(f32),
                    delta + term_ref[...],
                    gain_ref[...],
                    base_ref[...],
                )
                refs[-2][...] = total
                add_term(refs[-1], gain_term)

    row_spec = pl.BlockSpec((rows, width), lambda i: (i, 0))
    line_spec = pl.BlockSpec((1, width), lambda i: (0, 0))

    def part_spec(at):
        return pl.BlockSpec(
            (rows, width), lambda i: (jnp.clip(i - at * steps, 0, steps - 1), 0)
        )

    part_specs = [part_spec(i) for i in range(count)]
    return pl.pallas_call(
        kernel,
        out_shape=(
            jax.ShapeDtypeStruct((tokens, width), f32),
            jax.ShapeDtypeStruct((1, width), f32),
        ),
        grid=(tokens // rows,),
        in_specs=[row_spec, row_spec, line_spec, row_spec]
        + part_specs * 2
        + [UNREAD] * len(after),
        out_specs=(row_spec, line_spec),
        compiler_params=ROOMY,
        cost_estimate=taking(13),
        name="norm_back_rows",
    )(values, term, gain[None, :], base, *mine, *came, *after)


def block_bias(start_row, key_first, diagonal):
    size = start_row.shape[1]
    keys = lax.broadcasted_iota(jnp.int32, (size, size), 0)
    allowed = keys + key_first >= start_row
    if diagonal:
        queries = lax.broadcasted_iota(jnp.int32, (size, size), 1)
        allowed = allowed & (keys <= queries)
    return jnp.where(allowed, 0.0, masked_value).astype(f32)


def turned(block):
    return jnp.transpose(block.astype(f32)).astype(bf16)


def attend_kernel(group, info, q_ref, k_ref, v_ref, start_ref, *rest):
    o_ref, lse_ref, acc, top = rest[-4:]
    here, first = info[0], info[1]
    size = q_ref.shape[1]

    def step(block, diagonal):
        keys = turned(k_ref[block])
        values = jnp.concatenate([v_ref[block], jnp.ones((16, size), bf16)], 0)
        bias = block_bias(start_ref[...], block * size, diagonal)
        for h in range(group):
            scores = dot(keys, q_ref[h * HEAD : (h + 1) * HEAD, :], 1, 0) + bias
            block_top = jnp.max(scores, 0, keepdims=True)
            if diagonal:
                weights = jnp.exp(scores - block_top).astype(bf16)
                acc[h] = dot(values, weights, 1, 0)
                top[h] = block_top
            else:
                new_top = jnp.maximum(top[h], block_top)
                weights = jnp.exp(scores - new_top).astype(bf16)
                acc[h] = acc[h] * jnp.exp(top[h] - new_top) + dot(values, weights, 1, 0)
                top[h] = new_top

    step(here, True)

    @pl.loop(first, here)
    def _(block):
        step(block, False)

    for h in range(group):
        total = acc[h, HEAD : HEAD + 1, :]
        o_ref[h * HEAD : (h + 1) * HEAD, :] = (acc[h, :HEAD, :] / total).astype(bf16)
        lse_ref[0, h : h + 1, :] = top[h] + jnp.log(total)


def attend(info, query_t, keyval, start_row, kv_heads, seq, after=()):
    blocks, kv_rows, _ = keyval.shape
    size = start_row.shape[1]
    group = query_t.shape[0] // HEAD // kv_heads
    rows = group * HEAD
    return pl.pallas_call(
        lambda *refs: attend_kernel(group, *refs),
        out_shape=(
            jax.ShapeDtypeStruct((query_t.shape[0], size), bf16),
            jax.ShapeDtypeStruct((kv_heads, group, size), f32),
        ),
        grid_spec=pltpu.PrefetchScalarGridSpec(
            num_scalar_prefetch=1,
            grid=(kv_heads,),
            in_specs=[
                pl.BlockSpec((rows, size), lambda g, _: (g, seq)),
                pl.BlockSpec((blocks, HEAD, size), lambda g, _: (0, g, seq)),
                pl.BlockSpec((blocks, HEAD, size), lambda g, _: (0, kv_heads + g, seq)),
                pl.BlockSpec((1, size), lambda g, _: (0, 0)),
            ]
            + [UNREAD] * len(after),
            out_specs=(
                pl.BlockSpec((rows, size), lambda g, _: (g, 0)),
                pl.BlockSpec((1, group, size), lambda g, _: (g, 0, 0)),
            ),
            scratch_shapes=[
                pltpu.VMEM((group, HEAD + 16, size), f32),
                pltpu.VMEM((group, 1, size), f32),
            ],
        ),
        compiler_params=pltpu.CompilerParams(vmem_limit_bytes=48 * 2**20),
        cost_estimate=taking(0.42),
        name="attend",
    )(info, query_t, keyval, keyval, start_row, *after)


def attend_back_kernel(
    group, info, q_ref, k_ref, v_ref, start_ref, d_ref, o_ref, lse_ref, cos_ref, sin_ref, *rest
):
    dq_ref, dk_ref, dv_ref, acc, inner = rest[-5:]
    here, first = info[0], info[1]
    size = q_ref.shape[1]
    rows = [slice(h * HEAD, (h + 1) * HEAD) for h in range(group)]
    for h in range(group):
        product = d_ref[rows[h], :].astype(f32) * o_ref[rows[h], :].astype(f32)
        inner[h] = jnp.sum(product, 0, keepdims=True)

    def step(block, diagonal):
        key_block = k_ref[block]
        keys = turned(key_block)
        values = turned(v_ref[block])
        bias = block_bias(start_ref[...], block * size, diagonal)
        key_sum = jnp.zeros((HEAD, size), f32)
        value_sum = jnp.zeros((HEAD, size), f32)
        for h in range(group):
            query, delta = q_ref[rows[h], :], d_ref[rows[h], :]
            scores = dot(keys, query, 1, 0) + bias
            probs = jnp.exp(scores - lse_ref[0, h : h + 1, :])
            probs_delta = dot(values, delta, 1, 0)
            score_delta = (probs * (probs_delta - inner[h])).astype(bf16)
            part = dot(key_block, score_delta, 1, 0)
            if diagonal:
                acc[rows[h], :] = part
            else:
                acc[rows[h], :] += part
            key_sum += dot(query, score_delta, 1, 1)
            value_sum += dot(delta, probs.astype(bf16), 1, 1)
        dk_ref[block] = key_sum.astype(bf16)
        dv_ref[block] = value_sum.astype(bf16)

    step(here, True)

    @pl.loop(first, here)
    def _(block):
        step(block, False)

    def clear(block):
        dk_ref[block] = jnp.zeros((HEAD, size), bf16)
        dv_ref[block] = jnp.zeros((HEAD, size), bf16)

    pl.loop(0, first)(clear)
    pl.loop(here + 1, k_ref.shape[0])(clear)

    cosine, sine = cos_ref[...], sin_ref[...]
    for h in range(group):
        upper = acc[h * HEAD : h * HEAD + HALF, :]
        lower = acc[h * HEAD + HALF : (h + 1) * HEAD, :]
        scale = HEAD ** (-0.5)
        dq_ref[h * HEAD : h * HEAD + HALF, :] = (
            (upper * cosine + lower * sine) * scale
        ).astype(bf16)
        dq_ref[h * HEAD + HALF : (h + 1) * HEAD, :] = (
            (lower * cosine - upper * sine) * scale
        ).astype(bf16)


def attend_back(
    info, query_t, keyval, start_row, delta_t, mixed_t, log_sums, cosine, sine, kv_heads, seq, after=()
):
    blocks = keyval.shape[0]
    size = start_row.shape[1]
    group = query_t.shape[0] // HEAD // kv_heads
    rows = group * HEAD
    kv_out = jax.ShapeDtypeStruct((blocks, kv_heads * HEAD, size), bf16)
    kv_spec = pl.BlockSpec((blocks, HEAD, size), lambda g, _: (0, g, 0))
    return pl.pallas_call(
        lambda *refs: attend_back_kernel(group, *refs),
        out_shape=(jax.ShapeDtypeStruct((query_t.shape[0], size), bf16), kv_out, kv_out),
        grid_spec=pltpu.PrefetchScalarGridSpec(
            num_scalar_prefetch=1,
            grid=(kv_heads,),
            in_specs=[
                pl.BlockSpec((rows, size), lambda g, _: (g, seq)),
                pl.BlockSpec((blocks, HEAD, size), lambda g, _: (0, g, seq)),
                pl.BlockSpec((blocks, HEAD, size), lambda g, _: (0, kv_heads + g, seq)),
                pl.BlockSpec((1, size), lambda g, _: (0, 0)),
                pl.BlockSpec((rows, size), lambda g, _: (g, seq)),
                pl.BlockSpec((rows, size), lambda g, _: (g, 0)),
                pl.BlockSpec((1, group, size), lambda g, _: (g, 0, 0)),
                pl.BlockSpec((HALF, size), lambda g, _: (0, seq)),
                pl.BlockSpec((HALF, size), lambda g, _: (0, seq)),
            ]
            + [UNREAD] * len(after),
            out_specs=(pl.BlockSpec((rows, size), lambda g, _: (g, 0)), kv_spec, kv_spec),
            scratch_shapes=[
                pltpu.VMEM((rows, size), f32),
                pltpu.VMEM((group, 1, size), f32),
            ],
        ),
        compiler_params=pltpu.CompilerParams(vmem_limit_bytes=48 * 2**20),
        cost_estimate=taking(160),
        name="attend_back",
    )(info, query_t, keyval, keyval, start_row, delta_t, mixed_t, log_sums, cosine, sine, *after)


def rotate_t(values, cosine, sine):
    heads = values.reshape(-1, 2, HALF, values.shape[1])
    first, second = heads[:, 0], heads[:, 1]
    return jnp.stack([first * cosine - second * sine, second * cosine + first * sine], 1).reshape(
        values.shape
    )


def pick(index, when_zero, when_one):
    return jnp.where(index == 0, when_zero, when_one)


def block_products(
    lefts, rights, came, high, shards, left_rows, right_rows, left_cut, half=None, after=()
):
    cut_side, whole_side = (lefts, rights) if left_cut else (rights, lefts)
    whole_rows = right_rows if left_cut else left_rows
    tokens, model_width = cut_side[0].shape
    if high is None:
        part = model_width // shards
        where_high = jnp.zeros((1,), jnp.int32)
        cut_spec = pl.BlockSpec((tokens, part), lambda j, s, where: (0, s))
    else:
        part = model_width // shards // 2
        where_high = high.reshape(1)
        cut_spec = pl.BlockSpec((tokens, part), lambda j, s, where: (0, s * 2 + where[0]))
    whole = whole_side[0].shape[1 - whole_rows]
    first = 0
    if half is not None:
        whole, first = whole // 2, half
    tile = whole // 2 if whole > 1408 else whole
    steps = whole // tile
    if whole_rows == 0:
        whole_spec = pl.BlockSpec((tokens, tile), lambda j, s, where: (0, first + j))
    else:
        whole_spec = pl.BlockSpec((tile, tokens), lambda j, s, where: (first + j, 0))
    left_spec, right_spec = (cut_spec, whole_spec) if left_cut else (whole_spec, cut_spec)
    if left_cut:
        out_shape = (shards, part, whole)
        out_spec = pl.BlockSpec((1, part, tile), lambda j, s, where: (s, 0, j))
    else:
        out_shape = (shards, whole, part)
        out_spec = pl.BlockSpec((1, tile, part), lambda j, s, where: (s, j, 0))

    def kernel(where, *refs):
        total = dot(refs[0][...], refs[2][...], left_rows, right_rows)
        total += dot(refs[1][...], refs[3][...], left_rows, right_rows)
        if came is not None:
            total += refs[4][0].astype(f32)
        refs[-1][0] = total.astype(bf16)

    extra = [] if came is None else [came]
    return pl.pallas_call(
        kernel,
        out_shape=jax.ShapeDtypeStruct(out_shape, bf16),
        grid_spec=pltpu.PrefetchScalarGridSpec(
            num_scalar_prefetch=1,
            grid=(steps, shards),
            in_specs=[left_spec] * 2
            + [right_spec] * 2
            + [out_spec] * len(extra)
            + [UNREAD] * len(after),
            out_specs=out_spec,
        ),
        compiler_params=pltpu.CompilerParams(vmem_limit_bytes=56 * 2**20),
        cost_estimate=taking(9),
        name="block_products",
    )(where_high, *lefts, *rights, *extra, *after)


def column_half(values, which, shards):
    tokens, width = values.shape
    part = width // shards // 2
    return lax.dynamic_slice_in_dim(values.reshape(tokens, shards, 2, part), which, 1, 2)[:, :, 0]


def plain_products(
    lefts, rights, came, high, shards, left_rows, right_rows, left_cut, half=None, after=()
):
    left = jnp.concatenate(lefts, left_rows)
    right = jnp.concatenate(rights, right_rows)
    if half is not None:
        size = right.shape[1] // 2
        right = right[:, half * size : (half + 1) * size]
    if left_cut:
        total = jnp.einsum(
            "tsp,tn->spn" if right_rows == 0 else "tsp,nt->spn",
            column_half(left, high, shards), right, preferred_element_type=f32,
        )
    else:
        total = jnp.einsum(
            "tn,tsp->snp" if left_rows == 0 else "nt,tsp->snp",
            left, column_half(right, high, shards), preferred_element_type=f32,
        )
    return (total if came is None else total + came.astype(f32)).astype(bf16)


def over_shard(total):
    return lax.psum_scatter(total, "shard", scatter_dimension=0, tiled=True)[0]


def directly_over_shard(total, me):
    shards = total.shape[0]
    result = lax.dynamic_index_in_dim(total, me, 0, False).astype(f32)
    for k in range(1, shards):
        block = lax.dynamic_index_in_dim(total, (me + k) % shards, 0, False)
        came = lax.ppermute(block, "shard", [(i, (i + k) % shards) for i in range(shards)])
        result = result + came.astype(f32)
    return result.astype(bf16)


class Reduced:
    def __init__(self, lefts, rights, high, shards, left_rows, right_rows, left_cut, half=None):
        width = (lefts if left_cut else rights)[0].shape[1]
        self.products = block_products if width // shards // 2 % 128 == 0 else plain_products
        self.sides = lefts, rights
        self.high = high
        self.rest = shards, left_rows, right_rows, left_cut, half

    def send(self, after=(), swap_after=()):
        self.other = self.products(*self.sides, None, 1 - self.high, *self.rest, after)
        self.sent = tie(self.other, *swap_after)
        self.came = high_swap(self.sent)

    def add(self, after=(), sum_after=()):
        self.total = self.products(*self.sides, self.came, self.high, *self.rest, after)
        self.tied = tie(self.total, *sum_after)
        return over_shard(self.tied)


def halves(high, own, axis, came):
    return jnp.concatenate([pick(high, own, came), pick(high, came, own)], axis)


def body(
    activations,
    segments,
    query_weight,
    key_weight,
    value_weight,
    output_weight,
    gate_weight,
    up_weight,
    down_weight,
    attn_gain,
    ffn_gain,
    cotangent,
):
    seq_here, block_len, model_width = activations.shape
    seq_len = segments.shape[1]
    tokens = seq_here * block_len
    query_cols = query_weight.shape[1]
    kv_width = key_weight.shape[1]
    kv_heads = kv_width // HEAD
    shards = lax.axis_size("shard")
    ctx = lax.axis_index("ctx")
    low, high = ctx % 2, ctx // 2

    me = lax.axis_index("shard")
    where = (ctx, me, shards)

    def apart(weight, *after):
        if shards > 4:
            return [others(gathered(weight, ctx), me)]
        mine = quarter(weight, ctx)
        mine = tie(mine, *after) if after else mine
        return [lax.ppermute(mine, "shard", ring(shards, r))[None] for r in range(1, shards)]

    gains = jnp.pad(jnp.stack([attn_gain, ffn_gain], 1), ((0, 0), (0, 126)))
    qkv_local = jnp.concatenate([query_weight, key_weight, value_weight, gains], 1)
    qkv_own = apart(qkv_local)

    def later(weight, *after):
        return lax.all_gather(tie(quarter(weight, ctx), *after), "shard", axis=0, tiled=False)

    out_own = others(later(output_weight, *qkv_own), me)
    gate_all = later(gate_weight, *qkv_own)
    up_all = later(up_weight, *qkv_own)
    down_all = later(down_weight, *qkv_own)
    out_pieces = spread([out_own])
    qkv_weight = place(qkv_local, spread(qkv_own), *where, True, [out_own])
    gain_one = qkv_weight[:, -128].astype(f32)
    gain_two = qkv_weight[:, -127].astype(f32)
    keyval_weight = qkv_weight[:, query_cols:-128]
    keyval_other = lax.ppermute(keyval_weight, "tp", SWAP_TP)
    tp = lax.axis_index("tp")
    keyval_weight = jnp.concatenate(
        [pick(tp, keyval_weight, keyval_other), pick(tp, keyval_other, keyval_weight)], 1
    )

    index = jnp.arange(seq_len, dtype=jnp.int32)[None, :]
    doc_start = jnp.zeros_like(segments)
    for number in range(1, 4):
        before = jnp.sum((segments < number).astype(jnp.int32), 1, keepdims=True)
        doc_start = jnp.where(segments == number, before, doc_start)
    offset = ctx * block_len
    start_here = lax.dynamic_slice_in_dim(doc_start, offset, block_len, 1)
    position = lax.dynamic_slice_in_dim(index, offset, block_len, 1) - start_here
    frequency = jnp.power(rope_base, -jnp.arange(HALF, dtype=f32) / HALF)
    angles = frequency[:, None] * position.reshape(1, tokens).astype(f32)
    cosine, sine = jnp.cos(angles), jnp.sin(angles)
    first_block = start_here[:, 0] // block_len

    inputs = activations.reshape(tokens, model_width).astype(f32)
    grad_out = cotangent.reshape(tokens, model_width)
    inv_one = lax.rsqrt(jnp.mean(inputs * inputs, -1, keepdims=True) + epsilon)
    unit_one = inputs * inv_one
    normed_one = (unit_one * gain_one[None, :]).astype(bf16)

    projected = dot(qkv_weight[:, :-128], normed_one, 0, 1)
    query_t = (rotate_t(projected[:query_cols], cosine, sine) * HEAD ** (-0.5)).astype(bf16)
    key_t = rotate_t(projected[query_cols : query_cols + kv_width], cosine, sine).astype(bf16)
    value_t = projected[query_cols + kv_width :].astype(bf16)
    keyval = jnp.concatenate([key_t, value_t], 0)[None]
    came = low_swap(keyval)
    keyval = jnp.concatenate([pick(low, keyval, came), pick(low, came, keyval)], 0)
    keyval = tie(keyval, out_pieces[2][0])
    came = high_swap(keyval)
    keyval = jnp.concatenate([pick(high, keyval, came), pick(high, came, keyval)], 0)
    out_weight = place(output_weight, out_pieces, *where, False, [query_t])
    gate_own = others(tie(gate_all, came), me)
    mixed, log_sums, infos, mine, came = [], [], [], [], []
    last = [gate_own, keyval_weight]
    for s in range(seq_here):
        infos.append(jnp.stack([ctx, first_block[s]]).astype(jnp.int32))
        mixed_s, log_s = attend(
            infos[s], query_t, keyval, start_here[s : s + 1], kv_heads, s, last + came[s - 2 : s - 1]
        )
        mixed.append(mixed_s)
        log_sums.append(log_s)
        mine.append(product(mixed_s, out_weight, 0, 0, 512, came[1:2]))
        came.append(lax.ppermute(mine[s], "tp", SWAP_TP))
        last = [mine[s]]
        if s == 1:
            up_own = others(tie(up_all, mine[s]), me)
            last.append(up_own)
    mixed_t = jnp.concatenate(mixed, 1)
    acts = activations.reshape(tokens, model_width)
    gate_pieces = spread([gate_own], came[-1])
    up_pieces = spread([up_own], came[-1])
    down_own = others(tie(down_all, mine[-1]), me)
    residual, normed_two = add_and_norm(acts, mine, came, gain_two, [gate_pieces[2][0], down_own])
    hidden, gate_factor, up_factor, gate_up_full = feed_forward(
        normed_two, (gate_weight, up_weight), (gate_pieces, up_pieces), *where
    )

    down_high = high_swap(down_own)
    hidden = tie(hidden, down_high)
    hidden_came = low_swap(hidden)
    hidden_pair = (hidden, hidden_came)
    cotangent_pair = (grad_out, low_swap(grad_out))
    products = block_products if model_width // shards % 256 == 0 else plain_products
    down_products = products(hidden_pair, cotangent_pair, None, low, shards, 0, 0, False)
    down_sum = over_shard(down_products)
    down_pieces = [down_own], [low_swap(down_own)], [down_high], [low_swap(down_high)]
    down_full = place(down_weight, down_pieces, *where, False, [down_products])
    kept, given = feed_back(grad_out, down_full, gate_factor, up_factor, low)

    normed_pair = (normed_two, low_swap(normed_two))
    delta_pair = (kept, low_swap(given))
    gate_up = [Reduced(normed_pair, delta_pair, high, shards, 0, 0, True, i) for i in range(2)]

    chunks = 4
    mine, came = [], []
    last = []
    for i in range(chunks):
        mine.append(
            feed_input(kept, given, gate_up_full, low, i, chunks, last + came[max(i - 2, 0) : i - 1])
        )
        came.append(lax.ppermute(mine[i], "tp", SWAP_TP))
        last = [mine[i]]
        if i % 2 == 0:
            gate_up[i // 2].send(last, [gate_up[0].came] if i else [])
            last = [gate_up[0].sent] if i == 0 else last
    ffn_mine = product(hidden, down_full, 1, 0, TILE, [mine[-1]])
    gate_up_first = gate_up[0].add([ffn_mine, gate_up[1].sent, came[2]], [down_sum])
    residual_delta, ffn_gain_term, residual_round = norm_back(
        residual, mine, came, gain_two, grad_out, [ffn_mine, gate_up[0].tied]
    )
    ffn_came = lax.ppermute(ffn_mine, "tp", SWAP_TP)
    delta_t = product(out_weight, residual_round, 1, 1, TILE, [])

    half_rows = query_cols // 2
    mixed_kept = lax.dynamic_slice_in_dim(mixed_t, low * half_rows, half_rows, 0)
    mixed_given = lax.dynamic_slice_in_dim(mixed_t, (1 - low) * half_rows, half_rows, 0)
    mixed_pair = (mixed_kept, low_swap(mixed_given))
    residual_pair = (residual_round, low_swap(residual_round))
    output = Reduced(mixed_pair, residual_pair, high, shards, 1, 0, False)

    query_deltas, part_sums, mine, came = [], [], [], []
    last = []
    for s in range(seq_here):
        query_delta, key_part, value_part = attend_back(
            infos[s], query_t, keyval, start_here[s : s + 1], delta_t, mixed[s], log_sums[s],
            cosine, sine, kv_heads, s, last,
        )
        query_deltas.append(query_delta)
        part_sums.append(jnp.concatenate([key_part, value_part], 1))
        waits = []
        if s == 0:
            waits = []
        if s == 1:
            waits = [came[0], ffn_came]
        if s == 2:
            waits = []
        mine.append(product(query_delta, qkv_weight[:, :query_cols], 0, 1, 512, waits))
        came.append(lax.ppermute(mine[s], "tp", SWAP_TP))
        last = [mine[s]]
        if s == 0:
            output.send(last, [gate_up[1].came])
            gate_up_second = gate_up[1].add([output.sent], [])
            last = [output.sent, gate_up[1].tied, ffn_came]
        if s == 1:
            output.total = output.products(*output.sides, output.came, high, *output.rest, last)
            output_tied = tie(output.total, gate_up_second)
            down_came = high_swap(tie(down_sum, output.came))
            first_came = high_swap(tie(gate_up_first, down_came))
            last = [output.total, came[0], came[1], down_came] + [output_tied]

    part_sum = jnp.concatenate(part_sums, 2).reshape(2, 2, 2 * kv_width, tokens)
    sent = lax.dynamic_index_in_dim(part_sum, 1 - high, 0, False)
    part_came = high_swap(sent)

    normed_pair_one = (normed_one, low_swap(normed_one))

    def products_of(delta, after):
        half_rows = delta.shape[0] // 2
        kept = lax.dynamic_slice_in_dim(delta, low * half_rows, half_rows, 0)
        given = lax.dynamic_slice_in_dim(delta, (1 - low) * half_rows, half_rows, 0)
        pair = (kept.T, low_swap(given).T)
        return block_products(normed_pair_one, pair, None, None, shards, 0, 0, True, None, after)

    output_sum = over_shard(output_tied)
    query_products = products_of(jnp.concatenate(query_deltas, 1), [mine[-1], came[1]] + [output_sum])
    part_came = tie(part_came, query_products)
    query_sum = over_shard(query_products)

    kept = lax.dynamic_index_in_dim(part_sum, high, 0, False)
    kept = kept.astype(f32) + part_came.astype(f32)
    sent = lax.dynamic_index_in_dim(kept, 1 - low, 0, False).astype(bf16)
    kept = lax.dynamic_index_in_dim(kept, low, 0, False)
    keyval_delta = kept + low_swap(sent).astype(f32)
    key_delta = rotate_t(keyval_delta[:kv_width], cosine, -sine)
    keyval_delta = jnp.concatenate(
        [key_delta.astype(bf16), keyval_delta[kv_width:].astype(bf16)], 0
    )
    keyval_came = lax.ppermute(keyval_delta, "tp", SWAP_TP)
    keyval_both = jnp.concatenate(
        [pick(tp, keyval_delta, keyval_came), pick(tp, keyval_came, keyval_delta)], 0
    )
    keyval_products = products_of(keyval_delta, [query_products])
    keyval_term = dot(keyval_both, keyval_weight, 0, 1)

    input_grad, attn_gain_term = norm_back_rows(
        acts, mine, came, keyval_term, gain_one, residual_delta, [keyval_products, query_sum]
    )
    block_out = add_three(residual, ffn_mine, ffn_came, [])
    block_out = block_out.reshape(activations.shape)
    keyval_sum = directly_over_shard(keyval_products, me) if shards <= 4 else over_shard(keyval_products)

    second_came = high_swap(tie(gate_up_second, part_came))

    def two_sides(value):
        other = low_swap(value)
        return pick(low, value, other).astype(f32), pick(low, other, value).astype(f32)

    down_sum = (down_sum.astype(f32) + tie(down_came, keyval_products).astype(f32)).astype(bf16)
    down_grad = jnp.concatenate(two_sides(down_sum), 1)
    first_gate, first_up = two_sides(halves(high, gate_up_first, 0, first_came))
    second_gate, second_up = two_sides(halves(high, gate_up_second, 0, second_came))
    gate_grad = jnp.concatenate([first_gate, second_gate], 1)
    up_grad = jnp.concatenate([first_up, second_up], 1)
    output_grad = jnp.concatenate(two_sides(halves(high, output_sum, 1, high_swap(output_sum))), 0)

    def high_total(value):
        return (value.astype(f32) + high_swap(value).astype(f32)).astype(bf16)

    query_grad = jnp.concatenate(two_sides(high_total(query_sum)), 1)
    key_grad, value_grad = two_sides(high_total(keyval_sum))

    gain_terms = jnp.concatenate([attn_gain_term, ffn_gain_term], 0)
    gain_terms = gain_terms + low_swap(gain_terms)
    gain_terms = gain_terms + high_swap(gain_terms)
    gain_terms = gain_terms.reshape(2, shards, model_width // shards)
    gain_grads = lax.dynamic_index_in_dim(gain_terms, me, 1, False)
    for k in range(1, shards):
        block = lax.dynamic_index_in_dim(gain_terms, (me + k) % shards, 1, False)
        gain_grads = gain_grads + lax.ppermute(
            block, "shard", [(i, (i + k) % shards) for i in range(shards)]
        )

    return (
        block_out,
        input_grad.reshape(activations.shape),
        query_grad,
        key_grad,
        value_grad,
        output_grad,
        gate_grad,
        up_grad,
        down_grad,
        gain_grads[0],
        gain_grads[1],
    )


def solution(mesh):
    return jax.shard_map(
        body,
        mesh=mesh,
        in_specs=(
            P("shard", "ctx", None),
            P("shard", None),
            P("shard", "tp"),
            P("shard", "tp"),
            P("shard", "tp"),
            P("tp", "shard"),
            P("shard", "tp"),
            P("shard", "tp"),
            P("tp", "shard"),
            P("shard"),
            P("shard"),
            P("shard", "ctx", None),
        ),
        out_specs=(
            P("shard", "ctx", None),
            P("shard", "ctx", None),
            P("shard", "tp"),
            P("shard", "tp"),
            P("shard", "tp"),
            P("tp", "shard"),
            P("shard", "tp"),
            P("shard", "tp"),
            P("tp", "shard"),
            P("shard"),
            P("shard"),
        ),
        check_vma=False,
    )
```

```python
import jax
import jax.numpy as jnp
from jax import lax
from jax.experimental import pallas as pl
from jax.experimental.pallas import tpu as pltpu
from jax.sharding import PartitionSpec as P

HEAD = 64
HALF = HEAD // 2
epsilon = 1e-05
rope_base = 10000.0
masked_value = -1e30
bf16 = jnp.bfloat16
f32 = jnp.float32

SWAP_LOW = [(0, 1), (1, 0), (2, 3), (3, 2)]
SWAP_HIGH = [(0, 2), (2, 0), (1, 3), (3, 1)]
SWAP_TP = [(0, 1), (1, 0)]


def low_swap(value):
    return lax.ppermute(value, "ctx", SWAP_LOW)


def high_swap(value):
    return lax.ppermute(value, "ctx", SWAP_HIGH)


def dot(left, right, left_dim, right_dim):
    return lax.dot_general(
        left, right, (((left_dim,), (right_dim,)), ((), ())), preferred_element_type=f32
    )


def tp_sum(partial_sum):
    mine = partial_sum.astype(bf16)
    return mine.astype(f32) + lax.ppermute(mine, "tp", SWAP_TP).astype(f32)


UNREAD = pl.BlockSpec(memory_space=pl.ANY)


def taking(microseconds):
    return pl.CostEstimate(flops=int(microseconds * 1e9), bytes_accessed=int(microseconds * 0.15e6), transcendentals=0)


def tie(value, *after):
    def kernel(*refs):
        pass

    return pl.pallas_call(
        kernel,
        out_shape=jax.ShapeDtypeStruct(value.shape, value.dtype),
        in_specs=[UNREAD] * (1 + len(after)),
        out_specs=UNREAD,
        input_output_aliases={0: 0},
        name="tie",
    )(value, *after)


def ring(shards, step):
    return [(i, (i - step) % shards) for i in range(shards)]


def quarter(weight, ctx):
    rows = weight.shape[0] // 4
    return lax.dynamic_slice_in_dim(weight, ctx * rows, rows, 0)


def gathered(weight, ctx):
    return lax.all_gather(quarter(weight, ctx), "shard", axis=0, tiled=False)


def spread(own, *after):
    high = [high_swap(piece) for piece in own]
    low = [low_swap(piece) for piece in own]
    if after:
        high = [tie(piece, *after) for piece in high]
    return own, low, high, [low_swap(piece) for piece in high]


def others(everyone, me):
    shards = everyone.shape[0]
    steps = [lax.dynamic_slice_in_dim(everyone, (me + r) % shards, 1, 0) for r in range(1, shards)]
    return jnp.concatenate(steps, 0)


def place(weight, pieces, ctx, me, shards, along_rows, after=()):
    height, width = weight.shape
    rows = height // 4
    count = len(pieces[0])
    each = pieces[0][0].shape[0]

    def kernel(where, local, *refs):
        parts, out = refs[: 4 * count], refs[-1]
        step = pl.program_id(0)

        def put(slot, value):
            if along_rows:
                out[0, slot] = value
            else:
                out[pl.ds(pl.multiple_of(slot * rows, 16), rows), :] = value

        @pl.when(step == 0)
        def _():
            for slot in range(4):
                put(slot, local[slot])

        for i in range(count):

            @pl.when(step >= 1 if count == 1 else step == i + 1)
            def _():
                for k in range(4):
                    put(jnp.bitwise_xor(where[0], k), parts[k * count + i][0])

    if each == 1:
        piece_spec = pl.BlockSpec((1, rows, width), lambda r, where: (0, 0, 0))
    else:
        piece_spec = pl.BlockSpec(
            (1, rows, width), lambda r, where: (jnp.maximum(r - 1, 0), 0, 0)
        )
    if along_rows:
        out_shape = (shards, 4, rows, width)
        out_spec = pl.BlockSpec(
            (1, 4, rows, width), lambda r, where: (lax.rem(where[1] + r, shards), 0, 0, 0)
        )
    else:
        out_shape = (height, shards * width)
        out_spec = pl.BlockSpec((height, width), lambda r, where: (0, lax.rem(where[1] + r, shards)))
    out = pl.pallas_call(
        kernel,
        out_shape=jax.ShapeDtypeStruct(out_shape, weight.dtype),
        grid_spec=pltpu.PrefetchScalarGridSpec(
            num_scalar_prefetch=1,
            grid=(shards,),
            in_specs=[pl.BlockSpec((4, rows, width), lambda r, where: (0, 0, 0))]
            + [piece_spec] * (4 * count)
            + [UNREAD] * len(after),
            out_specs=out_spec,
        ),
        compiler_params=pltpu.CompilerParams(vmem_limit_bytes=56 * 2**20),
        cost_estimate=taking(240),
        name="place",
    )(jnp.stack([ctx, me]), weight.reshape(4, rows, width), *sum(pieces, []), *after)
    return out.reshape(shards * height, width) if along_rows else out


TILE = 256
ROOMY = pltpu.CompilerParams(vmem_limit_bytes=56 * 2**20)


def feed_forward(normed, weights, pieces, ctx, me, shards, after=()):
    tokens, model_width = normed.shape
    height, width = weights[0].shape
    rows = height // 4

    def kernel(where, normed_ref, *refs):
        hidden_ref, gate_ref, up_ref, full_ref = refs[-4:]
        for w in range(2):
            local, parts = refs[5 * w], refs[5 * w + 1 : 5 * w + 5]
            for slot in range(4):
                start = pl.multiple_of(where[1] * height + slot * rows, rows)
                full_ref[w, pl.ds(start, rows), :] = local[slot]
            for r in range(1, shards):
                first = lax.rem(where[1] + r, shards) * height
                for k in range(4):
                    start = first + jnp.bitwise_xor(where[0], k) * rows
                    full_ref[w, pl.ds(pl.multiple_of(start, rows), rows), :] = parts[k][r - 1]
        gate = dot(normed_ref[...], full_ref[0], 1, 0)
        up = dot(normed_ref[...], full_ref[1], 1, 0)
        sigmoid = 1.0 / (1.0 + jnp.exp(-gate))
        silu = gate * sigmoid
        hidden_ref[...] = (silu * up).astype(bf16)
        gate_ref[...] = (up * sigmoid * (1.0 + gate * (1.0 - sigmoid))).astype(bf16)
        up_ref[...] = silu.astype(bf16)

    weight_specs = [pl.BlockSpec((4, rows, TILE), lambda j, _: (0, 0, j))] + [
        pl.BlockSpec((shards - 1, rows, TILE), lambda j, _: (0, 0, j))
    ] * 4
    token_spec = pl.BlockSpec((tokens, TILE), lambda j, _: (0, j))
    token_shape = jax.ShapeDtypeStruct((tokens, width), bf16)
    operands = []
    for weight, parts in zip(weights, pieces):
        operands += [weight.reshape(4, rows, width)] + [part[0] for part in parts]
    return pl.pallas_call(
        kernel,
        out_shape=(
            token_shape,
            token_shape,
            token_shape,
            jax.ShapeDtypeStruct((2, model_width, width), bf16),
        ),
        grid_spec=pltpu.PrefetchScalarGridSpec(
            num_scalar_prefetch=1,
            grid=(width // TILE,),
            in_specs=[pl.BlockSpec((tokens, model_width), lambda j, _: (0, 0))] + weight_specs * 2
            + [UNREAD] * len(after),
            out_specs=(
                token_spec,
                token_spec,
                token_spec,
                pl.BlockSpec((2, model_width, TILE), lambda j, _: (0, 0, j)),
            ),
        ),
        compiler_params=ROOMY,
        cost_estimate=taking(29),
        name="feed_forward",
    )(jnp.stack([ctx, me]), normed, *operands, *after)


def feed_back(grad_out, down_full, gate_factor, up_factor, low, after=()):
    tokens, model_width = grad_out.shape
    width = down_full.shape[0]

    def kernel(where, grad_ref, down_ref, gate_ref, up_ref, *rest):
        kept_ref, given_ref = rest[-2:]
        hidden_delta = dot(grad_ref[...], down_ref[...], 1, 1)
        gate_delta = (hidden_delta * gate_ref[...].astype(f32)).astype(bf16)
        up_delta = (hidden_delta * up_ref[...].astype(f32)).astype(bf16)

        @pl.when(where[0] == 0)
        def _():
            kept_ref[...] = gate_delta
            given_ref[...] = up_delta

        @pl.when(where[0] != 0)
        def _():
            kept_ref[...] = up_delta
            given_ref[...] = gate_delta

    token_spec = pl.BlockSpec((tokens, TILE), lambda j, _: (0, j))
    token_shape = jax.ShapeDtypeStruct((tokens, width), bf16)
    return pl.pallas_call(
        kernel,
        out_shape=(token_shape, token_shape),
        grid_spec=pltpu.PrefetchScalarGridSpec(
            num_scalar_prefetch=1,
            grid=(width // TILE,),
            in_specs=[
                pl.BlockSpec((tokens, model_width), lambda j, _: (0, 0)),
                pl.BlockSpec((TILE, model_width), lambda j, _: (j, 0)),
                token_spec,
                token_spec,
            ]
            + [UNREAD] * len(after),
            out_specs=(token_spec, token_spec),
        ),
        compiler_params=ROOMY,
        cost_estimate=taking(5.7),
        name="feed_back",
    )(low.reshape(1), grad_out, down_full, gate_factor, up_factor, *after)


def feed_input(kept, given, full, low, part, parts, after=()):
    tokens, width = kept.shape
    model_width = full.shape[1]
    tiles = model_width // parts // TILE

    def kernel(where, kept_ref, given_ref, kept_weight, given_weight, *rest):
        total = dot(kept_ref[...], kept_weight[0], 1, 1)
        total += dot(given_ref[...], given_weight[0], 1, 1)
        rest[-1][...] = total.astype(bf16)

    return pl.pallas_call(
        kernel,
        out_shape=jax.ShapeDtypeStruct((tokens, model_width // parts), bf16),
        grid_spec=pltpu.PrefetchScalarGridSpec(
            num_scalar_prefetch=1,
            grid=(tiles,),
            in_specs=[
                pl.BlockSpec((tokens, width), lambda j, _: (0, 0)),
                pl.BlockSpec((tokens, width), lambda j, _: (0, 0)),
                pl.BlockSpec((1, TILE, width), lambda j, where: (where[0], part * tiles + j, 0)),
                pl.BlockSpec((1, TILE, width), lambda j, where: (1 - where[0], part * tiles + j, 0)),
            ]
            + [UNREAD] * len(after),
            out_specs=pl.BlockSpec((tokens, TILE), lambda j, _: (0, j)),
        ),
        compiler_params=ROOMY,
        cost_estimate=taking(300),
        name="feed_input",
    )(low.reshape(1), kept, given, full, full, *after)


def product(left, right, left_dim, right_dim, tile, after=()):
    rows = left.shape[1 - left_dim]
    width = right.shape[1 - right_dim]
    turn = left_dim == 0 and right_dim == 1

    def kernel(left_ref, right_ref, *rest):
        value = turned(left_ref[...]) if turn else left_ref[...]
        total = dot(value, right_ref[...], 1 if turn else left_dim, right_dim)
        rest[-1][...] = total.astype(bf16)

    if right_dim == 0:
        right_spec = pl.BlockSpec((right.shape[0], tile), lambda j: (0, j))
    else:
        right_spec = pl.BlockSpec((tile, left.shape[left_dim]), lambda j: (j, 0))
    return pl.pallas_call(
        kernel,
        out_shape=jax.ShapeDtypeStruct((rows, width), bf16),
        grid=(width // tile,),
        in_specs=[pl.BlockSpec(left.shape, lambda j: (0, 0)), right_spec] + [UNREAD] * len(after),
        out_specs=pl.BlockSpec((rows, tile), lambda j: (0, j)),
        compiler_params=ROOMY,
        cost_estimate=taking(0.6),
        name="product",
    )(left, right, *after)


def add_and_norm(activations, mine, came, gain, after=()):
    count = len(mine)
    rows, width = mine[0].shape

    def kernel(act_ref, gain_ref, *refs):
        residual_ref, normed_ref = refs[-2:]
        for i in range(count):

            @pl.when(pl.program_id(0) == i)
            def _():
                total = refs[i][...].astype(f32) + refs[count + i][...].astype(f32)
                residual = act_ref[...].astype(f32) + total
                inverse = lax.rsqrt(jnp.mean(residual * residual, -1, keepdims=True) + epsilon)
                residual_ref[...] = residual
                normed_ref[...] = (residual * inverse * gain_ref[...]).astype(bf16)

    row_spec = pl.BlockSpec((rows, width), lambda i: (i, 0))
    one_spec = pl.BlockSpec((rows, width), lambda i: (0, 0))
    return pl.pallas_call(
        kernel,
        out_shape=(
            jax.ShapeDtypeStruct(activations.shape, f32),
            jax.ShapeDtypeStruct(activations.shape, bf16),
        ),
        grid=(count,),
        in_specs=[row_spec, pl.BlockSpec((1, width), lambda i: (0, 0))]
        + [one_spec] * (2 * count)
        + [UNREAD] * len(after),
        out_specs=(row_spec, row_spec),
        compiler_params=ROOMY,
        cost_estimate=taking(90),
        name="add_and_norm",
    )(activations, gain[None, :], *mine, *came, *after)


def add_three(residual, mine, came, after=()):
    tokens, width = residual.shape
    rows = 128

    def kernel(residual_ref, mine_ref, came_ref, *rest):
        total = mine_ref[...].astype(f32) + came_ref[...].astype(f32)
        rest[-1][...] = (residual_ref[...] + total).astype(bf16)

    row_spec = pl.BlockSpec((rows, width), lambda i: (i, 0))
    return pl.pallas_call(
        kernel,
        out_shape=jax.ShapeDtypeStruct((tokens, width), bf16),
        grid=(tokens // rows,),
        in_specs=[row_spec] * 3 + [UNREAD] * len(after),
        out_specs=row_spec,
        compiler_params=ROOMY,
        cost_estimate=taking(0.15),
        name="add_three",
    )(residual, mine, came, *after)


def norm_gradient(value, delta, gain, base):
    inverse = lax.rsqrt(jnp.mean(value * value, -1, keepdims=True) + epsilon)
    unit = value * inverse
    scaled = delta * gain
    total = base + inverse * (scaled - unit * jnp.mean(scaled * unit, -1, keepdims=True))
    return total, jnp.sum(delta * unit, 0, keepdims=True)


def add_term(term_ref, term):
    @pl.when(pl.program_id(0) == 0)
    def _():
        term_ref[...] = term

    @pl.when(pl.program_id(0) != 0)
    def _():
        term_ref[...] += term


def norm_back(values, mine, came, gain, base, after=()):
    count = len(mine)
    tokens, width = values.shape
    rows = 128

    def kernel(value_ref, gain_ref, base_ref, *refs):
        delta = jnp.concatenate(
            [refs[i][...].astype(f32) + refs[count + i][...].astype(f32) for i in range(count)], 1
        )
        total, term = norm_gradient(
            value_ref[...], delta, gain_ref[...], base_ref[...].astype(f32)
        )
        refs[-3][...] = total
        refs[-1][...] = total.astype(bf16)
        add_term(refs[-2], term)

    row_spec = pl.BlockSpec((rows, width), lambda i: (i, 0))
    part_spec = pl.BlockSpec((rows, width // count), lambda i: (i, 0))
    line_spec = pl.BlockSpec((1, width), lambda i: (0, 0))
    return pl.pallas_call(
        kernel,
        out_shape=(
            jax.ShapeDtypeStruct((tokens, width), f32),
            jax.ShapeDtypeStruct((1, width), f32),
            jax.ShapeDtypeStruct((tokens, width), bf16),
        ),
        grid=(tokens // rows,),
        in_specs=[row_spec, line_spec, row_spec]
        + [part_spec] * (2 * count)
        + [UNREAD] * len(after),
        out_specs=(row_spec, line_spec, row_spec),
        compiler_params=ROOMY,
        cost_estimate=taking(360),
        name="norm_back",
    )(values, gain[None, :], base, *mine, *came, *after)


def norm_back_rows(values, mine, came, term, gain, base, after=()):
    count = len(mine)
    tokens, width = values.shape
    rows = 128
    steps = mine[0].shape[0] // rows

    def kernel(value_ref, term_ref, gain_ref, base_ref, *refs):
        for i in range(count):

            @pl.when(pl.program_id(0) // steps == i)
            def _():
                delta = refs[i][...].astype(f32) + refs[count + i][...].astype(f32)
                total, gain_term = norm_gradient(
                    value_ref[...].astype(f32),
                    delta + term_ref[...],
                    gain_ref[...],
                    base_ref[...],
                )
                refs[-2][...] = total
                add_term(refs[-1], gain_term)

    row_spec = pl.BlockSpec((rows, width), lambda i: (i, 0))
    line_spec = pl.BlockSpec((1, width), lambda i: (0, 0))

    def part_spec(at):
        return pl.BlockSpec(
            (rows, width), lambda i: (jnp.clip(i - at * steps, 0, steps - 1), 0)
        )

    part_specs = [part_spec(i) for i in range(count)]
    return pl.pallas_call(
        kernel,
        out_shape=(
            jax.ShapeDtypeStruct((tokens, width), f32),
            jax.ShapeDtypeStruct((1, width), f32),
        ),
        grid=(tokens // rows,),
        in_specs=[row_spec, row_spec, line_spec, row_spec]
        + part_specs * 2
        + [UNREAD] * len(after),
        out_specs=(row_spec, line_spec),
        compiler_params=ROOMY,
        cost_estimate=taking(13),
        name="norm_back_rows",
    )(values, term, gain[None, :], base, *mine, *came, *after)


def block_bias(start_row, key_first, diagonal):
    size = start_row.shape[1]
    keys = lax.broadcasted_iota(jnp.int32, (size, size), 0)
    allowed = keys + key_first >= start_row
    if diagonal:
        queries = lax.broadcasted_iota(jnp.int32, (size, size), 1)
        allowed = allowed & (keys <= queries)
    return jnp.where(allowed, 0.0, masked_value).astype(f32)


def turned(block):
    return jnp.transpose(block.astype(f32)).astype(bf16)


def attend_kernel(group, info, q_ref, k_ref, v_ref, start_ref, *rest):
    o_ref, lse_ref, acc, top = rest[-4:]
    here, first = info[0], info[1]
    size = q_ref.shape[1]

    def step(block, diagonal):
        keys = turned(k_ref[block])
        values = jnp.concatenate([v_ref[block], jnp.ones((16, size), bf16)], 0)
        bias = block_bias(start_ref[...], block * size, diagonal)
        for h in range(group):
            scores = dot(keys, q_ref[h * HEAD : (h + 1) * HEAD, :], 1, 0) + bias
            block_top = jnp.max(scores, 0, keepdims=True)
            if diagonal:
                weights = jnp.exp(scores - block_top).astype(bf16)
                acc[h] = dot(values, weights, 1, 0)
                top[h] = block_top
            else:
                new_top = jnp.maximum(top[h], block_top)
                weights = jnp.exp(scores - new_top).astype(bf16)
                acc[h] = acc[h] * jnp.exp(top[h] - new_top) + dot(values, weights, 1, 0)
                top[h] = new_top

    step(here, True)

    @pl.loop(first, here)
    def _(block):
        step(block, False)

    for h in range(group):
        total = acc[h, HEAD : HEAD + 1, :]
        o_ref[h * HEAD : (h + 1) * HEAD, :] = (acc[h, :HEAD, :] / total).astype(bf16)
        lse_ref[0, h : h + 1, :] = top[h] + jnp.log(total)


def attend(info, query_t, keyval, start_row, kv_heads, seq, after=()):
    blocks, kv_rows, _ = keyval.shape
    size = start_row.shape[1]
    group = query_t.shape[0] // HEAD // kv_heads
    rows = group * HEAD
    return pl.pallas_call(
        lambda *refs: attend_kernel(group, *refs),
        out_shape=(
            jax.ShapeDtypeStruct((query_t.shape[0], size), bf16),
            jax.ShapeDtypeStruct((kv_heads, group, size), f32),
        ),
        grid_spec=pltpu.PrefetchScalarGridSpec(
            num_scalar_prefetch=1,
            grid=(kv_heads,),
            in_specs=[
                pl.BlockSpec((rows, size), lambda g, _: (g, seq)),
                pl.BlockSpec((blocks, HEAD, size), lambda g, _: (0, g, seq)),
                pl.BlockSpec((blocks, HEAD, size), lambda g, _: (0, kv_heads + g, seq)),
                pl.BlockSpec((1, size), lambda g, _: (0, 0)),
            ]
            + [UNREAD] * len(after),
            out_specs=(
                pl.BlockSpec((rows, size), lambda g, _: (g, 0)),
                pl.BlockSpec((1, group, size), lambda g, _: (g, 0, 0)),
            ),
            scratch_shapes=[
                pltpu.VMEM((group, HEAD + 16, size), f32),
                pltpu.VMEM((group, 1, size), f32),
            ],
        ),
        compiler_params=pltpu.CompilerParams(vmem_limit_bytes=48 * 2**20),
        cost_estimate=taking(0.42),
        name="attend",
    )(info, query_t, keyval, keyval, start_row, *after)


def attend_back_kernel(
    group, info, q_ref, k_ref, v_ref, start_ref, d_ref, o_ref, lse_ref, cos_ref, sin_ref, *rest
):
    dq_ref, dk_ref, dv_ref, acc, inner = rest[-5:]
    here, first = info[0], info[1]
    size = q_ref.shape[1]
    rows = [slice(h * HEAD, (h + 1) * HEAD) for h in range(group)]
    for h in range(group):
        product = d_ref[rows[h], :].astype(f32) * o_ref[rows[h], :].astype(f32)
        inner[h] = jnp.sum(product, 0, keepdims=True)

    def step(block, diagonal):
        key_block = k_ref[block]
        keys = turned(key_block)
        values = turned(v_ref[block])
        bias = block_bias(start_ref[...], block * size, diagonal)
        key_sum = jnp.zeros((HEAD, size), f32)
        value_sum = jnp.zeros((HEAD, size), f32)
        for h in range(group):
            query, delta = q_ref[rows[h], :], d_ref[rows[h], :]
            scores = dot(keys, query, 1, 0) + bias
            probs = jnp.exp(scores - lse_ref[0, h : h + 1, :])
            probs_delta = dot(values, delta, 1, 0)
            score_delta = (probs * (probs_delta - inner[h])).astype(bf16)
            part = dot(key_block, score_delta, 1, 0)
            if diagonal:
                acc[rows[h], :] = part
            else:
                acc[rows[h], :] += part
            key_sum += dot(query, score_delta, 1, 1)
            value_sum += dot(delta, probs.astype(bf16), 1, 1)
        dk_ref[block] = key_sum.astype(bf16)
        dv_ref[block] = value_sum.astype(bf16)

    step(here, True)

    @pl.loop(first, here)
    def _(block):
        step(block, False)

    def clear(block):
        dk_ref[block] = jnp.zeros((HEAD, size), bf16)
        dv_ref[block] = jnp.zeros((HEAD, size), bf16)

    pl.loop(0, first)(clear)
    pl.loop(here + 1, k_ref.shape[0])(clear)

    cosine, sine = cos_ref[...], sin_ref[...]
    for h in range(group):
        upper = acc[h * HEAD : h * HEAD + HALF, :]
        lower = acc[h * HEAD + HALF : (h + 1) * HEAD, :]
        scale = HEAD ** (-0.5)
        dq_ref[h * HEAD : h * HEAD + HALF, :] = (
            (upper * cosine + lower * sine) * scale
        ).astype(bf16)
        dq_ref[h * HEAD + HALF : (h + 1) * HEAD, :] = (
            (lower * cosine - upper * sine) * scale
        ).astype(bf16)


def attend_back(
    info, query_t, keyval, start_row, delta_t, mixed_t, log_sums, cosine, sine, kv_heads, seq, after=()
):
    blocks = keyval.shape[0]
    size = start_row.shape[1]
    group = query_t.shape[0] // HEAD // kv_heads
    rows = group * HEAD
    kv_out = jax.ShapeDtypeStruct((blocks, kv_heads * HEAD, size), bf16)
    kv_spec = pl.BlockSpec((blocks, HEAD, size), lambda g, _: (0, g, 0))
    return pl.pallas_call(
        lambda *refs: attend_back_kernel(group, *refs),
        out_shape=(jax.ShapeDtypeStruct((query_t.shape[0], size), bf16), kv_out, kv_out),
        grid_spec=pltpu.PrefetchScalarGridSpec(
            num_scalar_prefetch=1,
            grid=(kv_heads,),
            in_specs=[
                pl.BlockSpec((rows, size), lambda g, _: (g, seq)),
                pl.BlockSpec((blocks, HEAD, size), lambda g, _: (0, g, seq)),
                pl.BlockSpec((blocks, HEAD, size), lambda g, _: (0, kv_heads + g, seq)),
                pl.BlockSpec((1, size), lambda g, _: (0, 0)),
                pl.BlockSpec((rows, size), lambda g, _: (g, seq)),
                pl.BlockSpec((rows, size), lambda g, _: (g, 0)),
                pl.BlockSpec((1, group, size), lambda g, _: (g, 0, 0)),
                pl.BlockSpec((HALF, size), lambda g, _: (0, seq)),
                pl.BlockSpec((HALF, size), lambda g, _: (0, seq)),
            ]
            + [UNREAD] * len(after),
            out_specs=(pl.BlockSpec((rows, size), lambda g, _: (g, 0)), kv_spec, kv_spec),
            scratch_shapes=[
                pltpu.VMEM((rows, size), f32),
                pltpu.VMEM((group, 1, size), f32),
            ],
        ),
        compiler_params=pltpu.CompilerParams(vmem_limit_bytes=48 * 2**20),
        cost_estimate=taking(160),
        name="attend_back",
    )(info, query_t, keyval, keyval, start_row, delta_t, mixed_t, log_sums, cosine, sine, *after)


def rotate_t(values, cosine, sine):
    heads = values.reshape(-1, 2, HALF, values.shape[1])
    first, second = heads[:, 0], heads[:, 1]
    return jnp.stack([first * cosine - second * sine, second * cosine + first * sine], 1).reshape(
        values.shape
    )


def pick(index, when_zero, when_one):
    return jnp.where(index == 0, when_zero, when_one)


def block_products(
    lefts, rights, came, high, shards, left_rows, right_rows, left_cut, half=None, after=()
):
    cut_side, whole_side = (lefts, rights) if left_cut else (rights, lefts)
    whole_rows = right_rows if left_cut else left_rows
    tokens, model_width = cut_side[0].shape
    if high is None:
        part = model_width // shards
        where_high = jnp.zeros((1,), jnp.int32)
        cut_spec = pl.BlockSpec((tokens, part), lambda j, s, where: (0, s))
    else:
        part = model_width // shards // 2
        where_high = high.reshape(1)
        cut_spec = pl.BlockSpec((tokens, part), lambda j, s, where: (0, s * 2 + where[0]))
    whole = whole_side[0].shape[1 - whole_rows]
    first = 0
    if half is not None:
        whole, first = whole // 2, half
    tile = whole // 2 if whole > 1408 else whole
    steps = whole // tile
    if whole_rows == 0:
        whole_spec = pl.BlockSpec((tokens, tile), lambda j, s, where: (0, first + j))
    else:
        whole_spec = pl.BlockSpec((tile, tokens), lambda j, s, where: (first + j, 0))
    left_spec, right_spec = (cut_spec, whole_spec) if left_cut else (whole_spec, cut_spec)
    if left_cut:
        out_shape = (shards, part, whole)
        out_spec = pl.BlockSpec((1, part, tile), lambda j, s, where: (s, 0, j))
    else:
        out_shape = (shards, whole, part)
        out_spec = pl.BlockSpec((1, tile, part), lambda j, s, where: (s, j, 0))

    def kernel(where, *refs):
        total = dot(refs[0][...], refs[2][...], left_rows, right_rows)
        total += dot(refs[1][...], refs[3][...], left_rows, right_rows)
        if came is not None:
            total += refs[4][0].astype(f32)
        refs[-1][0] = total.astype(bf16)

    extra = [] if came is None else [came]
    return pl.pallas_call(
        kernel,
        out_shape=jax.ShapeDtypeStruct(out_shape, bf16),
        grid_spec=pltpu.PrefetchScalarGridSpec(
            num_scalar_prefetch=1,
            grid=(steps, shards),
            in_specs=[left_spec] * 2
            + [right_spec] * 2
            + [out_spec] * len(extra)
            + [UNREAD] * len(after),
            out_specs=out_spec,
        ),
        compiler_params=pltpu.CompilerParams(vmem_limit_bytes=56 * 2**20),
        cost_estimate=taking(9),
        name="block_products",
    )(where_high, *lefts, *rights, *extra, *after)


def column_half(values, which, shards):
    tokens, width = values.shape
    part = width // shards // 2
    return lax.dynamic_slice_in_dim(values.reshape(tokens, shards, 2, part), which, 1, 2)[:, :, 0]


def plain_products(
    lefts, rights, came, high, shards, left_rows, right_rows, left_cut, half=None, after=()
):
    left = jnp.concatenate(lefts, left_rows)
    right = jnp.concatenate(rights, right_rows)
    if half is not None:
        size = right.shape[1] // 2
        right = right[:, half * size : (half + 1) * size]
    if left_cut:
        total = jnp.einsum(
            "tsp,tn->spn" if right_rows == 0 else "tsp,nt->spn",
            column_half(left, high, shards), right, preferred_element_type=f32,
        )
    else:
        total = jnp.einsum(
            "tn,tsp->snp" if left_rows == 0 else "nt,tsp->snp",
            left, column_half(right, high, shards), preferred_element_type=f32,
        )
    return (total if came is None else total + came.astype(f32)).astype(bf16)


def over_shard(total):
    return lax.psum_scatter(total, "shard", scatter_dimension=0, tiled=True)[0]


def directly_over_shard(total, me, after):
    shards = total.shape[0]
    result = lax.dynamic_index_in_dim(total, me, 0, False).astype(f32)
    for k in range(1, shards):
        block = lax.dynamic_index_in_dim(total, (me + k) % shards, 0, False)
        came = lax.ppermute(block, "shard", [(i, (i + k) % shards) for i in range(shards)])
        result = result + tie(came, after).astype(f32)
    return result.astype(bf16)


class Reduced:
    def __init__(self, lefts, rights, high, shards, left_rows, right_rows, left_cut, half=None):
        width = (lefts if left_cut else rights)[0].shape[1]
        self.products = block_products if width // shards // 2 % 128 == 0 else plain_products
        self.sides = lefts, rights
        self.high = high
        self.rest = shards, left_rows, right_rows, left_cut, half

    def send(self, after=(), swap_after=()):
        self.other = self.products(*self.sides, None, 1 - self.high, *self.rest, after)
        self.sent = tie(self.other, *swap_after)
        self.came = high_swap(self.sent)

    def add(self, after=(), sum_after=()):
        self.total = self.products(*self.sides, self.came, self.high, *self.rest, after)
        self.tied = tie(self.total, *sum_after)
        return over_shard(self.tied)


def halves(high, own, axis, came):
    return jnp.concatenate([pick(high, own, came), pick(high, came, own)], axis)


def body(
    activations,
    segments,
    query_weight,
    key_weight,
    value_weight,
    output_weight,
    gate_weight,
    up_weight,
    down_weight,
    attn_gain,
    ffn_gain,
    cotangent,
):
    seq_here, block_len, model_width = activations.shape
    seq_len = segments.shape[1]
    tokens = seq_here * block_len
    query_cols = query_weight.shape[1]
    kv_width = key_weight.shape[1]
    kv_heads = kv_width // HEAD
    shards = lax.axis_size("shard")
    ctx = lax.axis_index("ctx")
    low, high = ctx % 2, ctx // 2

    me = lax.axis_index("shard")
    where = (ctx, me, shards)

    def apart(weight, *after):
        if shards > 4:
            return [others(gathered(weight, ctx), me)]
        mine = quarter(weight, ctx)
        mine = tie(mine, *after) if after else mine
        return [lax.ppermute(mine, "shard", ring(shards, r))[None] for r in range(1, shards)]

    gains = jnp.pad(jnp.stack([attn_gain, ffn_gain], 1), ((0, 0), (0, 126)))
    qkv_local = jnp.concatenate([query_weight, key_weight, value_weight, gains], 1)
    qkv_own = apart(qkv_local)

    def later(weight, *after):
        return lax.all_gather(tie(quarter(weight, ctx), *after), "shard", axis=0, tiled=False)

    out_own = others(later(output_weight, *qkv_own), me)
    gate_all = later(gate_weight, *qkv_own)
    up_all = later(up_weight, *qkv_own)
    down_all = later(down_weight, *qkv_own)
    out_pieces = spread([out_own])
    qkv_weight = place(qkv_local, spread(qkv_own), *where, True, [out_own])
    gain_one = qkv_weight[:, -128].astype(f32)
    gain_two = qkv_weight[:, -127].astype(f32)
    keyval_weight = qkv_weight[:, query_cols:-128]
    keyval_other = lax.ppermute(keyval_weight, "tp", SWAP_TP)
    tp = lax.axis_index("tp")
    keyval_weight = jnp.concatenate(
        [pick(tp, keyval_weight, keyval_other), pick(tp, keyval_other, keyval_weight)], 1
    )

    index = jnp.arange(seq_len, dtype=jnp.int32)[None, :]
    doc_start = jnp.zeros_like(segments)
    for number in range(1, 4):
        before = jnp.sum((segments < number).astype(jnp.int32), 1, keepdims=True)
        doc_start = jnp.where(segments == number, before, doc_start)
    offset = ctx * block_len
    start_here = lax.dynamic_slice_in_dim(doc_start, offset, block_len, 1)
    position = lax.dynamic_slice_in_dim(index, offset, block_len, 1) - start_here
    frequency = jnp.power(rope_base, -jnp.arange(HALF, dtype=f32) / HALF)
    angles = frequency[:, None] * position.reshape(1, tokens).astype(f32)
    cosine, sine = jnp.cos(angles), jnp.sin(angles)
    first_block = start_here[:, 0] // block_len

    inputs = activations.reshape(tokens, model_width).astype(f32)
    grad_out = cotangent.reshape(tokens, model_width)
    inv_one = lax.rsqrt(jnp.mean(inputs * inputs, -1, keepdims=True) + epsilon)
    unit_one = inputs * inv_one
    normed_one = (unit_one * gain_one[None, :]).astype(bf16)

    projected = dot(qkv_weight[:, :-128], normed_one, 0, 1)
    query_t = (rotate_t(projected[:query_cols], cosine, sine) * HEAD ** (-0.5)).astype(bf16)
    key_t = rotate_t(projected[query_cols : query_cols + kv_width], cosine, sine).astype(bf16)
    value_t = projected[query_cols + kv_width :].astype(bf16)
    keyval = jnp.concatenate([key_t, value_t], 0)[None]
    came = low_swap(keyval)
    keyval = jnp.concatenate([pick(low, keyval, came), pick(low, came, keyval)], 0)
    keyval = tie(keyval, out_pieces[2][0])
    came = high_swap(keyval)
    keyval = jnp.concatenate([pick(high, keyval, came), pick(high, came, keyval)], 0)
    out_weight = place(output_weight, out_pieces, *where, False, [query_t])
    gate_own = others(tie(gate_all, came), me)
    mixed, log_sums, infos, mine, came = [], [], [], [], []
    last = [gate_own, keyval_weight]
    for s in range(seq_here):
        infos.append(jnp.stack([ctx, first_block[s]]).astype(jnp.int32))
        mixed_s, log_s = attend(
            infos[s], query_t, keyval, start_here[s : s + 1], kv_heads, s, last + came[s - 2 : s - 1]
        )
        mixed.append(mixed_s)
        log_sums.append(log_s)
        mine.append(product(mixed_s, out_weight, 0, 0, 512, came[1:2]))
        came.append(lax.ppermute(mine[s], "tp", SWAP_TP))
        last = [mine[s]]
        if s == 1:
            up_own = others(tie(up_all, mine[s]), me)
            last.append(up_own)
    mixed_t = jnp.concatenate(mixed, 1)
    acts = activations.reshape(tokens, model_width)
    gate_pieces = spread([gate_own], came[-1])
    up_pieces = spread([up_own], came[-1])
    down_own = others(tie(down_all, mine[-1]), me)
    residual, normed_two = add_and_norm(acts, mine, came, gain_two, [gate_pieces[2][0], down_own])
    hidden, gate_factor, up_factor, gate_up_full = feed_forward(
        normed_two, (gate_weight, up_weight), (gate_pieces, up_pieces), *where
    )

    down_high = high_swap(down_own)
    hidden = tie(hidden, down_high)
    hidden_came = low_swap(hidden)
    hidden_pair = (hidden, hidden_came)
    cotangent_pair = (grad_out, low_swap(grad_out))
    products = block_products if model_width // shards % 256 == 0 else plain_products
    down_products = products(hidden_pair, cotangent_pair, None, low, shards, 0, 0, False)
    down_sum = over_shard(down_products)
    down_pieces = [down_own], [low_swap(down_own)], [down_high], [low_swap(down_high)]
    down_full = place(down_weight, down_pieces, *where, False, [down_products])
    kept, given = feed_back(grad_out, down_full, gate_factor, up_factor, low)

    normed_pair = (normed_two, low_swap(normed_two))
    delta_pair = (kept, low_swap(given))
    gate_up = [Reduced(normed_pair, delta_pair, high, shards, 0, 0, True, i) for i in range(2)]

    chunks = 4
    mine, came = [], []
    last = []
    for i in range(chunks):
        mine.append(
            feed_input(kept, given, gate_up_full, low, i, chunks, last + came[max(i - 2, 0) : i - 1])
        )
        came.append(lax.ppermute(mine[i], "tp", SWAP_TP))
        last = [mine[i]]
        if i % 2 == 0:
            gate_up[i // 2].send(last, [gate_up[0].came] if i else [])
            last = [gate_up[0].sent] if i == 0 else last
    ffn_mine = product(hidden, down_full, 1, 0, TILE, [mine[-1]])
    gate_up_first = gate_up[0].add([ffn_mine, gate_up[1].sent, came[2]], [down_sum])
    residual_delta, ffn_gain_term, residual_round = norm_back(
        residual, mine, came, gain_two, grad_out, [ffn_mine, gate_up[0].tied]
    )
    ffn_came = lax.ppermute(ffn_mine, "tp", SWAP_TP)
    delta_t = product(out_weight, residual_round, 1, 1, TILE, [])

    half_rows = query_cols // 2
    mixed_kept = lax.dynamic_slice_in_dim(mixed_t, low * half_rows, half_rows, 0)
    mixed_given = lax.dynamic_slice_in_dim(mixed_t, (1 - low) * half_rows, half_rows, 0)
    mixed_pair = (mixed_kept, low_swap(mixed_given))
    residual_pair = (residual_round, low_swap(residual_round))
    output = Reduced(mixed_pair, residual_pair, high, shards, 1, 0, False)

    query_deltas, part_sums, mine, came = [], [], [], []
    last = []
    for s in range(seq_here):
        query_delta, key_part, value_part = attend_back(
            infos[s], query_t, keyval, start_here[s : s + 1], delta_t, mixed[s], log_sums[s],
            cosine, sine, kv_heads, s, last,
        )
        query_deltas.append(query_delta)
        part_sums.append(jnp.concatenate([key_part, value_part], 1))
        waits = []
        if s == 0:
            waits = []
        if s == 1:
            waits = [came[0], ffn_came]
        if s == 2:
            waits = []
        mine.append(product(query_delta, qkv_weight[:, :query_cols], 0, 1, 512, waits))
        came.append(lax.ppermute(mine[s], "tp", SWAP_TP))
        last = [mine[s]]
        if s == 0:
            output.send(last, [gate_up[1].came])
            gate_up_second = gate_up[1].add([output.sent], [])
            last = [output.sent, gate_up[1].tied, ffn_came]
        if s == 1:
            output.total = output.products(*output.sides, output.came, high, *output.rest, last)
            output_tied = tie(output.total, gate_up_second)
            down_came = high_swap(tie(down_sum, output.came))
            first_came = high_swap(tie(gate_up_first, down_came))
            last = [output.total, came[0], came[1], down_came]

    part_sum = jnp.concatenate(part_sums, 2).reshape(2, 2, 2 * kv_width, tokens)
    sent = lax.dynamic_index_in_dim(part_sum, 1 - high, 0, False)
    part_came = high_swap(sent)

    normed_pair_one = (normed_one, low_swap(normed_one))

    def products_of(delta, after):
        half_rows = delta.shape[0] // 2
        kept = lax.dynamic_slice_in_dim(delta, low * half_rows, half_rows, 0)
        given = lax.dynamic_slice_in_dim(delta, (1 - low) * half_rows, half_rows, 0)
        pair = (kept.T, low_swap(given).T)
        return block_products(normed_pair_one, pair, None, None, shards, 0, 0, True, None, after)

    output_sum = over_shard(output_tied)
    query_products = products_of(jnp.concatenate(query_deltas, 1), [mine[-1], came[1]] + [output_sum])
    part_came = tie(part_came, query_products)
    query_sum = over_shard(query_products)

    kept = lax.dynamic_index_in_dim(part_sum, high, 0, False)
    kept = kept.astype(f32) + part_came.astype(f32)
    sent = lax.dynamic_index_in_dim(kept, 1 - low, 0, False).astype(bf16)
    kept = lax.dynamic_index_in_dim(kept, low, 0, False)
    keyval_delta = kept + low_swap(sent).astype(f32)
    key_delta = rotate_t(keyval_delta[:kv_width], cosine, -sine)
    keyval_delta = jnp.concatenate(
        [key_delta.astype(bf16), keyval_delta[kv_width:].astype(bf16)], 0
    )
    keyval_came = lax.ppermute(keyval_delta, "tp", SWAP_TP)
    keyval_both = jnp.concatenate(
        [pick(tp, keyval_delta, keyval_came), pick(tp, keyval_came, keyval_delta)], 0
    )
    keyval_products = products_of(keyval_delta, [query_products])
    keyval_term = dot(keyval_both, keyval_weight, 0, 1)

    input_grad, attn_gain_term = norm_back_rows(
        acts, mine, came, keyval_term, gain_one, residual_delta, [keyval_products]
    )
    block_out = add_three(residual, ffn_mine, ffn_came, [])
    block_out = block_out.reshape(activations.shape)
    keyval_sum = (
        directly_over_shard(keyval_products, me, input_grad)
        if shards <= 4
        else over_shard(keyval_products)
    )

    second_came = high_swap(tie(gate_up_second, part_came))

    def two_sides(value):
        other = low_swap(value)
        return pick(low, value, other).astype(f32), pick(low, other, value).astype(f32)

    down_sum = (down_sum.astype(f32) + tie(down_came, input_grad).astype(f32)).astype(bf16)
    down_grad = jnp.concatenate(two_sides(down_sum), 1)
    first_gate, first_up = two_sides(halves(high, gate_up_first, 0, first_came))
    second_gate, second_up = two_sides(halves(high, gate_up_second, 0, second_came))
    gate_grad = jnp.concatenate([first_gate, second_gate], 1)
    up_grad = jnp.concatenate([first_up, second_up], 1)
    output_grad = jnp.concatenate(two_sides(halves(high, output_sum, 1, high_swap(output_sum))), 0)

    def high_total(value):
        return (value.astype(f32) + high_swap(value).astype(f32)).astype(bf16)

    query_grad = jnp.concatenate(two_sides(high_total(tie(query_sum, input_grad))), 1)
    key_grad, value_grad = two_sides(high_total(keyval_sum))

    gain_terms = jnp.concatenate([attn_gain_term, ffn_gain_term], 0)
    gain_terms = gain_terms + low_swap(gain_terms)
    gain_terms = gain_terms + high_swap(gain_terms)
    gain_terms = gain_terms.reshape(2, shards, model_width // shards)
    gain_grads = lax.dynamic_index_in_dim(gain_terms, me, 1, False)
    for k in range(1, shards):
        block = lax.dynamic_index_in_dim(gain_terms, (me + k) % shards, 1, False)
        gain_grads = gain_grads + lax.ppermute(
            block, "shard", [(i, (i + k) % shards) for i in range(shards)]
        )

    return (
        block_out,
        input_grad.reshape(activations.shape),
        query_grad,
        key_grad,
        value_grad,
        output_grad,
        gate_grad,
        up_grad,
        down_grad,
        gain_grads[0],
        gain_grads[1],
    )


def solution(mesh):
    return jax.shard_map(
        body,
        mesh=mesh,
        in_specs=(
            P("shard", "ctx", None),
            P("shard", None),
            P("shard", "tp"),
            P("shard", "tp"),
            P("shard", "tp"),
            P("tp", "shard"),
            P("shard", "tp"),
            P("shard", "tp"),
            P("tp", "shard"),
            P("shard"),
            P("shard"),
            P("shard", "ctx", None),
        ),
        out_specs=(
            P("shard", "ctx", None),
            P("shard", "ctx", None),
            P("shard", "tp"),
            P("shard", "tp"),
            P("shard", "tp"),
            P("tp", "shard"),
            P("shard", "tp"),
            P("shard", "tp"),
            P("tp", "shard"),
            P("shard"),
            P("shard"),
        ),
        check_vma=False,
    )
```
